32 devices in a mesh: groups: 2 (over y), slab: 4 (over z), sub: 2 (over x), comp: 2 (over core).
Axes of the slice: x: 2, y: 2, z: 4, core: 2. Of those that a mesh axis runs over, the one named last changes fastest.
Arguments:
- electric: float32 [3, 256, 64, 256], P(None, ('groups', 'slab'), 'sub', 'comp'), parts along dimension 1, may hold values from -6 to 6
- magnetic: float32 [3, 256, 64, 256], P(None, ('groups', 'slab'), 'sub', 'comp'), parts along dimension 1, may hold values from -6 to 6
- conduct: float32 [256, 64, 256], P(('groups', 'slab'), 'sub', 'comp'), parts along dimension 0, may hold values from 0.1 to 1
- temp_old: float32 [128, 32, 256], P(('groups', 'slab'), 'sub', 'comp'), parts along dimension 0, may hold values from 0.5 to 1.5
- capacity: float32 [128, 32, 256], P(('groups', 'slab'), 'sub', 'comp'), parts along dimension 0, may hold values from 1 to 4
- offsets: int32 [256, 64, 2], P(('groups', 'slab'), 'sub', 'comp'), parts along dimension 0, may hold values from -1 to 1, as said below
- targets: int32 [256, 64, 2], P(('groups', 'slab'), 'sub', 'comp'), parts along dimension 0, may hold values from 0 to 255
Outputs:
- electric_out: float32 [3, 256, 64, 256], P(None, ('groups', 'slab'), 'sub', 'comp'), parts along dimension 1
- magnetic_out: float32 [3, 256, 64, 256], P(None, ('groups', 'slab'), 'sub', 'comp'), parts along dimension 1
- temp_new: float32 [128, 32, 256], P(('groups', 'slab'), 'sub', 'comp'), parts along dimension 0
- conduct_new: float32 [256, 64, 256], P(('groups', 'slab'), 'sub', 'comp'), parts along dimension 0
The draws below stay inside these ranges and needn't reach their ends.
There are 2 independent parts, one for each index of `groups`. The reference program is written for one: setup_inputs(seed, part) draws one part's arguments, and reference() takes and returns one part's arrays. A program takes and returns all parts, laid end to end along the dimension named above; each array names one. Nothing has to cross between parts.
Inputs may be any that keep to these rules, and one draw needn't show every extreme that they name: `offsets`: -1, 0 or 1; -1 never on the first slab and 1 never on the last; of the field blocks of one device at most 256 have -1 and at most 256 have 1, and each bound is reached by some device.
All inputs are finite; a program needn't handle non-finite values.
Results may differ from the reference program's by a relative error of at most 0.0001.
Values sent between devices are 32-bit elements; how exact they have to be, the bound alone decides.
No kernel may reach another device: no remote copies, remote signals or barrier semaphores. Data moves between devices by JAX's collectives and lax.ppermute only.
A program may use at most 64 MiB of HBM per device.

```python
import math
import jax
import jax.numpy as jnp
from jax import lax

S_DEV = 32
Y_DEV = 32
BLK = 128
TS = 16
TY = 16
STEPS = 4
SWEEPS = 3
TB = 256
NS = 128
NY = 64
NX = 256
NTS = 64
NTY = 32
N_SLAB = 4
N_SUB = 2
N_COMP = 2


def draw_offsets(key, part):
    key = jax.random.fold_in(key, 11)
    keys = jax.random.split(key, 5)
    blocks = S_DEV * Y_DEV
    limit = blocks // 4
    devices = N_SLAB * N_SUB * N_COMP
    shape = (N_SLAB, N_SUB, N_COMP)
    rising = jax.random.randint(keys[0], shape, limit // 4, limit + 1)
    falling = jax.random.randint(keys[1], shape, limit // 4, limit + 1)
    others = (N_SLAB - 1) * N_SUB * N_COMP
    pick_rising = jax.random.randint(keys[2], (), 0, others)
    pick_falling = jax.random.randint(keys[3], (), 0, others) + N_SUB * N_COMP
    flat = jnp.arange(devices, dtype=jnp.int32).reshape(shape)
    rising = jnp.where(flat == pick_rising, limit, rising)
    falling = jnp.where(flat == pick_falling, limit, falling)
    slab_place = jnp.arange(N_SLAB, dtype=jnp.int32)[:, None, None]
    rising = jnp.where(slab_place < N_SLAB - 1, rising, 0)
    falling = jnp.where(slab_place > 0, falling, 0)
    position = jnp.arange(blocks, dtype=jnp.int32)
    labels = jnp.where(position < falling[..., None], -1, jnp.where(position < (falling + rising)[..., None], 1, 0))
    perm_keys = jax.random.split(keys[4], devices)
    orders = jax.vmap(lambda one_key: jax.random.permutation(one_key, blocks))(perm_keys)
    orders = orders.reshape(N_SLAB, N_SUB, N_COMP, blocks)
    labels = jnp.take_along_axis(labels, orders, axis=-1)
    labels = labels.reshape(N_SLAB, N_SUB, N_COMP, S_DEV, Y_DEV)
    labels = jnp.transpose(labels, (0, 3, 1, 4, 2))
    return labels.reshape(N_SLAB * S_DEV, N_SUB * Y_DEV, N_COMP).astype(jnp.int32)


def set_ends(entries, rng, least, high):
    longest = entries.shape.index(max(entries.shape))
    spots = []
    for shift in (0, 1):
        where = [jax.random.randint(jax.random.fold_in(rng, axis), (), 0, length) for axis, length in enumerate(entries.shape)]
        where[longest] = (where[longest] + shift) % entries.shape[longest]
        spots.append(tuple(where))
    return entries.at[spots[0]].set(least).at[spots[1]].set(high)


def shard_levels(rng, dims, cuts, low, high):
    factor_of = 1.0
    for dim, blocks in cuts:
        steps = jax.random.uniform(jax.random.fold_in(jax.random.fold_in(rng, 6), dim), (blocks,), jnp.float32, low / len(cuts), high / len(cuts))
        factor_of = factor_of * jnp.repeat(jnp.exp(steps), dims[dim] // blocks).reshape((-1,) + (1,) * (len(dims) - 1 - dim))
    return factor_of


def centred(own_key, dims, deviation, most, pieces=(), held_as=jnp.bfloat16):
    values = deviation * jax.random.normal(own_key, dims, jnp.float32)
    if pieces:
        values = values * shard_levels(own_key, dims, pieces, -0.22, 0.18)
    return jnp.clip(values, -most, most).astype(held_as)


def setup_inputs(seed: int = 0, part: int = 0) -> dict:
    arg_keys = jax.random.split(jax.random.key(seed), 8)
    part_splits = jax.random.split(jax.random.fold_in(arg_keys[7], part), 8)
    electric = centred(part_splits[0], (3, NS, NY, NX), 1.0, 6.0, ((1, 4), (2, 2), (3, 2)), jnp.float32)
    magnetic = centred(part_splits[1], (3, NS, NY, NX), 1.0, 6.0, ((1, 4), (2, 2), (3, 2)), jnp.float32)
    conduct = jnp.clip(jnp.exp(math.log(1.0) - 2.3025851 * jax.random.uniform(part_splits[2], (NS, NY, NX), jnp.float32) ** shard_levels(part_splits[2], (NS, NY, NX), ((0, 4), (1, 2), (2, 2)), -0.2, 0.2)), 0.1, 1.0)
    temp_old = jnp.clip(0.5 + 1.0 * jax.random.uniform(part_splits[3], (NTS, NTY, NX), jnp.float32) ** shard_levels(part_splits[3], (NTS, NTY, NX), ((0, 4), (1, 2), (2, 2)), -0.2, 0.2), 0.5, 1.5)
    capacity = jnp.clip(1.0 + 3.0 * jax.random.uniform(part_splits[4], (NTS, NTY, NX), jnp.float32) ** shard_levels(part_splits[4], (NTS, NTY, NX), ((0, 4), (1, 2), (2, 2)), -0.2, 0.2), 1.0, 4.0)
    offsets = draw_offsets(jax.random.fold_in(jax.random.fold_in(arg_keys[7], part), 71), part)
    targets = set_ends(jax.random.randint(part_splits[6], (NS, NY, N_COMP), 0, TB), jax.random.fold_in(part_splits[6], 1), 0, TB - 1).astype(jnp.int32)
    return {"electric": electric, "magnetic": magnetic, "conduct": conduct, "temp_old": temp_old, "capacity": capacity, "offsets": offsets, "targets": targets}


time_step = 0.5
conduction = 2.0
heating = 0.25
softening = 0.25


def chebyshev_constants(sweep_count):
    lowest = 1.0
    highest = 4.0 + 12.0 * conduction
    center = 0.5 * (highest + lowest)
    spread = 0.5 * (highest - lowest)
    ratio = center / spread
    rhos = [1.0 / ratio]
    for sweep in range(sweep_count - 1):
        rhos.append(1.0 / (2.0 * ratio - rhos[-1]))
    return center, spread, rhos


def forward_diff(values, along):
    length = values.shape[along]
    beyond = jnp.zeros_like(lax.slice_in_dim(values, 0, 1, axis=along))
    shifted = jnp.concatenate([lax.slice_in_dim(values, 1, length, axis=along), beyond], along)
    return shifted - values


def backward_diff(values, along):
    length = values.shape[along]
    before = jnp.zeros_like(lax.slice_in_dim(values, 0, 1, axis=along))
    shifted = jnp.concatenate([before, lax.slice_in_dim(values, 0, length - 1, axis=along)], along)
    return values - shifted


def curl_forward(electric):
    return jnp.stack([
        forward_diff(electric[2], 1) - forward_diff(electric[1], 2),
        forward_diff(electric[0], 2) - forward_diff(electric[2], 0),
        forward_diff(electric[1], 0) - forward_diff(electric[0], 1)])


def curl_backward(magnetic):
    return jnp.stack([
        backward_diff(magnetic[2], 1) - backward_diff(magnetic[1], 2),
        backward_diff(magnetic[0], 2) - backward_diff(magnetic[2], 0),
        backward_diff(magnetic[1], 0) - backward_diff(magnetic[0], 1)])


def maxwell_step(electric, magnetic, conduct, heat):
    magnetic = magnetic - time_step * curl_forward(electric)
    damping = 0.5 * time_step * conduct
    electric_next = (electric * (1.0 - damping) + time_step * curl_backward(magnetic)) / (1.0 + damping)
    average = 0.5 * (electric + electric_next)
    heat = heat + time_step * conduct * jnp.sum(average * average, axis=0)
    return electric_next, magnetic, heat


def heat_stencil(padded, values, capacity):
    beside_all = padded[2:, 1:-1, 1:-1] + padded[:-2, 1:-1, 1:-1]
    beside_all = beside_all + padded[1:-1, 2:, 1:-1] + padded[1:-1, :-2, 1:-1]
    beside_all = beside_all + padded[1:-1, 1:-1, 2:] + padded[1:-1, 1:-1, :-2]
    return capacity * values + conduction * (6.0 * values - beside_all)


def chebyshev(start, source, apply_heat, inside):
    center, spread, rhos = chebyshev_constants(SWEEPS)
    resid = (source - apply_heat(start)) * inside
    update = resid / center
    result = start + update
    for sweep in range(1, SWEEPS):
        resid = resid - apply_heat(update) * inside
        update = (rhos[sweep] * rhos[sweep - 1]) * update + (2.0 * rhos[sweep] / spread) * resid
        result = result + update
    return result


def reference(electric, magnetic, conduct, temp_old, capacity, offsets, targets):
    heat = jnp.zeros(conduct.shape, jnp.float32)
    for turn_index in range(STEPS):
        electric, magnetic, heat = maxwell_step(electric, magnetic, conduct, heat)
    slab_rows = jnp.arange(N_SLAB * S_DEV, dtype=jnp.int32)[:, None, None] // S_DEV
    sub_rows = jnp.arange(N_SUB * Y_DEV, dtype=jnp.int32)[None, :, None] // Y_DEV
    comp_rows = jnp.broadcast_to(jnp.arange(N_COMP, dtype=jnp.int32)[None, None, :], offsets.shape)
    first_rows = (slab_rows + offsets) * TS + targets // TY
    second_rows = sub_rows * TY + targets % TY
    heat_blocks = heat.reshape(N_SLAB * S_DEV, N_SUB * Y_DEV, N_COMP, BLK)
    deposit = jnp.zeros((N_SLAB * TS, N_SUB * TY, N_COMP, BLK), jnp.float32)
    deposit = deposit.at[first_rows, second_rows, comp_rows].add(heat_blocks)
    deposit = deposit.reshape(temp_old.shape)
    source = capacity * temp_old + heating * deposit

    def apply_heat(values):
        return heat_stencil(jnp.pad(values, 1), values, capacity)

    temp_new = chebyshev(temp_old, source, apply_heat, 1.0)
    looked = temp_new.reshape(N_SLAB * TS, N_SUB * TY, N_COMP, BLK)[first_rows, second_rows, comp_rows]
    looked = looked.reshape(conduct.shape)
    conduct_new = conduct / (1.0 + softening * looked * looked)
    return electric, magnetic, temp_new, conduct_new
```

```python
import functools

import jax
import jax.numpy as jnp
from jax import lax
from jax.experimental import pallas as pl
from jax.experimental.pallas import tpu as pltpu
from jax.sharding import PartitionSpec as P

STEPS = 4
SWEEPS = 3
W = STEPS

time_step = 0.5
conduction = 2.0
heating = 0.25
softening = 0.25

F32 = jnp.float32
BF16 = jnp.bfloat16
VMEM_LIMIT = 56 * 1024 * 1024


def chebyshev_constants(sweep_count):
    lowest = 1.0
    highest = 4.0 + 12.0 * conduction
    center = 0.5 * (highest + lowest)
    spread = 0.5 * (highest - lowest)
    ratio = center / spread
    rhos = [1.0 / ratio]
    for sweep in range(sweep_count - 1):
        rhos.append(1.0 / (2.0 * ratio - rhos[-1]))
    return (center, spread, rhos)


def passed_along(array, axis, by):
    devices = lax.axis_size(axis)
    pairs = [(i, i + by) for i in range(devices) if 0 <= i + by < devices]
    return lax.ppermute(array, axis, pairs)


def swapped(array, axis):
    return lax.ppermute(array, axis, [(0, 1), (1, 0)])


def plane_list(s_dev):
    up, dn = [], []
    for f in range(7):
        up_rows = W if f in (0, 1, 2, 4, 5) else W - 1
        dn_rows = W if f in (1, 2) else W - 1
        for r in range(s_dev - up_rows, s_dev):
            up.append((f, r))
        for r in range(dn_rows):
            dn.append((f, r))
    return up, dn


def slab_messages(electric, magnetic, conduct, temp_old, capacity):
    s_dev = conduct.shape[0]

    def rows(f, a, b):
        if f < 3:
            return electric[f, a:b]
        if f < 6:
            return magnetic[f - 3, a:b]
        return conduct[a:b]

    def ends(i):
        return jnp.concatenate([temp_old[i], capacity[i]], 0)[None]

    up, dn = [], []
    for f in range(7):
        up_rows = W if f in (0, 1, 2, 4, 5) else W - 1
        dn_rows = W if f in (1, 2) else W - 1
        up.append(rows(f, s_dev - up_rows, s_dev))
        dn.append(rows(f, 0, dn_rows))
    up.append(ends(temp_old.shape[0] - 1))
    dn.append(ends(0))
    return jnp.concatenate(up, 0), jnp.concatenate(dn, 0)


def row_source(f, i, s_dev, own, lo, hi, up_index, dn_index):
    r = i - W
    if 0 <= r < s_dev:
        e_ref, h_ref, c_ref = own
        if f < 3:
            return e_ref, (f, r)
        if f < 6:
            return h_ref, (f - 3, r)
        return c_ref, (r,)
    if r < 0:
        key = (f, s_dev + r)
        return (lo, (up_index[key],)) if key in up_index else None
    key = (f, r - s_dev)
    return (hi, (dn_index[key],)) if key in dn_index else None


def indices_of(s_dev):
    up, dn = plane_list(s_dev)
    return (
        {key: n for n, key in enumerate(up)},
        {key: n for n, key in enumerate(dn)},
    )


def sub_pack_kernel(edges, e_ref, h_ref, c_ref, t_ref, cap_ref, lo_ref, hi_ref, *out_refs):
    s_dev, y_dev = c_ref.shape[0], c_ref.shape[1]
    ty = t_ref.shape[1]
    up_index, dn_index = indices_of(s_dev)
    own = (e_ref, h_ref, c_ref)
    for edge, out in zip(edges, out_refs):
        if edge == "high":
            y0, t0 = y_dev - W, ty - 1
        elif edge == "low":
            y0, t0 = 0, 0
        else:
            upper = lax.axis_index("sub") == 0
            y0 = jnp.where(upper, y_dev - W, 0)
            t0 = jnp.where(upper, ty - 1, 0)
        zero = jnp.zeros((W, 128), F32)
        for c in range(4):
            for i in range(s_dev + 2 * W):
                for half in range(2):
                    if c == 3 and half == 1:
                        continue
                    f = 6 if c == 3 else c + 3 * half
                    source = row_source(f, i, s_dev, own, lo_ref, hi_ref, up_index, dn_index)
                    if source is None:
                        value = zero
                    else:
                        ref, at = source
                        value = ref[at + (pl.ds(y0, W), slice(None))]
                    out[c, i, pl.ds(half * W, W), :] = value
        out[3, :, pl.ds(W, W), :] = jnp.zeros((s_dev + 2 * W, W, 128), F32)
        for i in range(t_ref.shape[0]):
            out[3, i, pl.ds(W, 1), :] = t_ref[i, pl.ds(t0, 1), :]
            out[3, i, pl.ds(W + 1, 1), :] = cap_ref[i, pl.ds(t0, 1), :]


def sub_exchange(electric, magnetic, conduct, temp_old, capacity, lo, hi):
    count = lax.axis_size("sub")
    edges = ("either",) if count == 2 else ("high", "low")
    s_ext = conduct.shape[0] + 2 * W
    shape = jax.ShapeDtypeStruct((4, s_ext, 2 * W, conduct.shape[2]), F32)
    messages = pl.pallas_call(
        functools.partial(sub_pack_kernel, edges),
        out_shape=[shape] * len(edges),
        compiler_params=pltpu.CompilerParams(vmem_limit_bytes=VMEM_LIMIT),
        name="sub_pack",
    )(electric, magnetic, conduct, temp_old, capacity, lo, hi)
    if count == 2:
        received = swapped(messages[0], "sub")
        return received, received
    return passed_along(messages[0], "sub", 1), passed_along(messages[1], "sub", -1)


def inside_flags(axis, count):
    index = lax.axis_index(axis)
    return (index > 0), (index < count - 1)


def comp_pack_kernel(
    n_sub, e_ref, h_ref, c_ref, t_ref, cap_ref, lo_ref, hi_ref, ml_ref, mh_ref, out_ref, a_ref, b_ref
):
    s_dev, y_dev, lanes = c_ref.shape
    y_ext = y_dev + 2 * W
    up_index, dn_index = indices_of(s_dev)
    own = (e_ref, h_ref, c_ref)
    has_lo, has_hi = inside_flags("sub", n_sub)
    first = jnp.where(lax.axis_index("comp") == 0, lanes - W, 0)
    lane = lax.broadcasted_iota(jnp.int32, (8, lanes), 1) // W
    a_ref[...] = jnp.zeros_like(a_ref)
    b_ref[...] = jnp.zeros_like(b_ref)
    blocks = (s_dev + 2 * W) // 8
    for b in range(blocks):
        acc_a = jnp.zeros((y_dev, lanes), F32)
        acc_b = jnp.zeros((y_dev, lanes), F32)
        acc_lo = jnp.zeros((8, lanes), F32)
        acc_hi = jnp.zeros((8, lanes), F32)
        for c in range(4):
            for j in range(8):
                i = b * 8 + j
                group = c * 8 + j
                shift = lax.rem(group * W - first + 2 * lanes, lanes)
                here = lane == group
                here_own = jnp.concatenate([here] * (y_dev // 8), 0)
                for which in range(2):
                    if c == 3 and which == 1:
                        continue
                    f = 6 if c == 3 else c + 3 * which
                    source = row_source(f, i, s_dev, own, lo_ref, hi_ref, up_index, dn_index)
                    if source is None:
                        continue
                    ref, at = source
                    moved = pltpu.roll(ref[at], shift, 1)
                    if which == 0:
                        acc_a = jnp.where(here_own, moved, acc_a)
                    else:
                        acc_b = jnp.where(here_own, moved, acc_b)
                acc_lo = jnp.where(here, pltpu.roll(ml_ref[c, i], shift, 1), acc_lo)
                acc_hi = jnp.where(here, pltpu.roll(mh_ref[c, i], shift, 1), acc_hi)
        acc_lo = jnp.where(has_lo, acc_lo, 0.0)
        acc_hi = jnp.where(has_hi, acc_hi, 0.0)
        a_ref[pl.ds(0, W), :] = acc_lo[:W]
        a_ref[pl.ds(W, y_dev), :] = acc_a
        a_ref[pl.ds(W + y_dev, W), :] = acc_hi[:W]
        b_ref[pl.ds(0, W), :] = acc_lo[W:]
        b_ref[pl.ds(W, y_dev), :] = acc_b
        b_ref[pl.ds(W + y_dev, W), :] = acc_hi[W:]
        out_ref[2 * b] = a_ref[...].T
        out_ref[2 * b + 1] = b_ref[...].T
    rows = t_ref.shape[0] * t_ref.shape[1] // lanes
    for n in range(rows):
        per = lanes // t_ref.shape[1]
        out_ref[2 * blocks + n] = t_ref[pl.ds(n * per, per)].reshape(lanes, lanes)
        out_ref[2 * blocks + rows + n] = cap_ref[pl.ds(n * per, per)].reshape(lanes, lanes)


def comp_pack(electric, magnetic, conduct, temp_old, capacity, lo, hi, m_lo, m_hi):
    s_dev, y_dev, lanes = conduct.shape
    count = 2 * ((s_dev + 2 * W) // 8) + 2 * (temp_old.shape[0] * temp_old.shape[1] // lanes)
    return pl.pallas_call(
        functools.partial(comp_pack_kernel, lax.axis_size("sub")),
        out_shape=jax.ShapeDtypeStruct((count, lanes, lanes), F32),
        scratch_shapes=[pltpu.VMEM((lanes, lanes), F32)] * 2,
        compiler_params=pltpu.CompilerParams(vmem_limit_bytes=VMEM_LIMIT),
        name="comp_pack",
    )(electric, magnetic, conduct, temp_old, capacity, lo, hi, m_lo, m_hi)


TOP = 8


def coefficients(conduct, inside):
    damping = 0.5 * time_step * conduct
    inverse = inside / (1.0 + damping)
    return (1.0 - damping) * inverse, time_step * inverse


def split_two(values):
    high = values.astype(BF16)
    low = (values - high.astype(F32)).astype(BF16)
    return jnp.concatenate([high, low], 1)


def main_kernel(
    n_slab, n_sub,
    e_ref, h_ref, c_ref, t_ref, ids_ref, lo_ref, hi_ref, ml_ref, mh_ref, own_ref, other_ref,
    e_out, h_out, d_out,
    es, hs, ce, ch, heat, sde, sdh, sce, sch, bt, bp,
):
    s_dev, y_dev, lanes = c_ref.shape
    s_ext, y_ext = s_dev + 2 * W, y_dev + 2 * W
    up_index, dn_index = indices_of(s_dev)
    own = (e_ref, h_ref, c_ref)
    slab_lo, slab_hi = inside_flags("slab", n_slab)
    sub_lo, sub_hi = inside_flags("sub", n_sub)
    comp = lax.axis_index("comp")

    def place(ref, at, f, i, half, c):
        source = row_source(f, i, s_dev, own, lo_ref, hi_ref, up_index, dn_index)
        if source is None:
            ref[at + (pl.ds(TOP + W, y_dev), slice(None))] = jnp.zeros((y_dev, lanes), F32)
        else:
            s, sat = source
            ref[at + (pl.ds(TOP + W, y_dev), slice(None))] = s[sat]
        low = ml_ref[c, i, pl.ds(half * W, W), :]
        high = mh_ref[c, i, pl.ds(half * W, W), :]
        ref[at + (pl.ds(TOP, W), slice(None))] = jnp.where(sub_lo, low, 0.0)
        ref[at + (pl.ds(TOP + W + y_dev, W), slice(None))] = jnp.where(sub_hi, high, 0.0)
        ref[at + (pl.ds(0, TOP), slice(None))] = jnp.zeros((TOP, lanes), F32)
        ref[at + (pl.ds(TOP + y_ext, 8), slice(None))] = jnp.zeros((8, lanes), F32)

    place_y = lax.broadcasted_iota(jnp.int32, (y_ext, lanes), 0)
    in_y = ((place_y >= W) | sub_lo) & ((place_y < W + y_dev) | sub_hi)
    in_y = jnp.where(in_y, 1.0, 0.0)
    lane = lax.broadcasted_iota(jnp.int32, (y_ext, lanes), 1)
    is_last = lane == lanes - 1
    is_first = lane == 0

    def slab_inside(i):
        good = ((i >= W) | slab_lo) & ((i < W + s_dev) | slab_hi)
        return jnp.where(good, 1.0, 0.0)

    for i in range(s_ext):
        for c in range(3):
            place(es, (c, i), c, i, 0, c)
            place(hs, (c, i), c + 3, i, 1, c)
        place(ce, (i,), 6, i, 0, 3)

    def coefs(i, carry):
        keep, gain = coefficients(ce[i, pl.ds(TOP, y_ext), :], in_y * slab_inside(i))
        ce[i, pl.ds(TOP, y_ext), :] = keep
        ch[i] = gain
        return carry

    lax.fori_loop(0, s_ext, coefs, 0)

    first = comp == 0
    blocks = s_ext // 8
    lane8 = lax.broadcasted_iota(jnp.int32, (8, lanes), 1)
    in_y8 = ((lane8 >= W) | sub_lo) & ((lane8 < W + y_dev) | sub_hi)
    in_y8 = jnp.where(in_y8, 1.0, 0.0)
    for b in range(blocks):
        for c in range(4):
            for j in range(8):
                i = b * 8 + j
                for which in range(2):
                    if c == 3 and which == 1:
                        continue
                    at = pl.ds((c * 8 + j) * W, W)
                    mine = own_ref[2 * b + which, at, :]
                    theirs = other_ref[2 * b + which, at, :]
                    target = (sdh if which else sde).at[c, i] if c < 3 else sce.at[i]
                    target[pl.ds(0, W), :] = jnp.where(first, mine, theirs)
                    target[pl.ds(W, W), :] = jnp.where(first, theirs, mine)

    def side_coefs(i, carry):
        sce[i], sch[i] = coefficients(sce[i], in_y8 * slab_inside(i))
        return carry

    lax.fori_loop(0, s_ext, side_coefs, 0)

    e_on = jnp.where(comp == 0, 1.0, 0.0)
    h_on = jnp.where(comp == 0, 0.0, 1.0)

    def up_y(v):
        return pltpu.roll(v, lanes - 1, 1)

    def down_y(v):
        return pltpu.roll(v, 1, 1)

    def up_x(v):
        return pltpu.roll(v, 7, 0)

    def down_x(v):
        return pltpu.roll(v, 1, 0)

    bt[...] = jnp.zeros_like(bt)

    def side_h(step, i):
        e0, e1, e2 = sde[0, i], sde[1, i], sde[2, i]
        bt[pl.ds(i * 16 + 2 * step, 1), :] = e0[W : W + 1] * e_on
        bt[pl.ds(i * 16 + 2 * step + 1, 1), :] = e1[W : W + 1] * e_on
        scale = (time_step * slab_inside(i)) * in_y8
        h0 = sdh[0, i] - scale * ((up_y(e2) - e2) - (up_x(e1) - e1))
        h1 = sdh[1, i] - scale * ((up_x(e0) - e0) - (sde[2, i + 1] - e2))
        h2 = sdh[2, i] - scale * ((sde[1, i + 1] - e1) - (up_y(e0) - e0))
        sdh[0, i], sdh[1, i], sdh[2, i] = h0, h1, h2
        bt[pl.ds(i * 16 + 8 + 2 * step, 1), :] = h0[W - 1 : W] * h_on
        bt[pl.ds(i * 16 + 8 + 2 * step + 1, 1), :] = h1[W - 1 : W] * h_on
        return h0, h1, h2

    def side_e(i, h0, h1, h2):
        keep, gain = sce[i], sch[i]
        sde[0, i] = keep * sde[0, i] + gain * ((h2 - down_y(h2)) - (h1 - down_x(h1)))
        sde[1, i] = keep * sde[1, i] + gain * ((h0 - down_x(h0)) - (h2 - sdh[2, i - 1]))
        sde[2, i] = keep * sde[2, i] + gain * ((h1 - sdh[1, i - 1]) - (h0 - down_y(h0)))

    for step in range(STEPS):
        side_h(step, step)

        def side_row(i, carry, step=step):
            side_e(i, *side_h(step, i))
            return carry

        lax.fori_loop(step + 1, s_ext - 1 - step, side_row, 0)

    for b in range(blocks):
        bp[b] = bt[pl.ds(b * lanes, lanes), :].T[:y_ext]

    centre = pl.ds(TOP, y_ext)
    above = pl.ds(TOP + 1, y_ext)
    below = pl.ds(TOP - 1, y_ext)

    def border(i, q, to):
        block, place = i // 8, i % 8
        return pltpu.roll(bp[block], lax.rem(2 * lanes + to - place * 16 - q, lanes), 1)

    def main_h(step, i):
        e0, e1, e2 = es[0, i, centre, :], es[1, i, centre, :], es[2, i, centre, :]
        e0x = jnp.where(is_last, border(i, 2 * step, lanes - 1), pltpu.roll(e0, lanes - 1, 1))
        e1x = jnp.where(is_last, border(i, 2 * step + 1, lanes - 1), pltpu.roll(e1, lanes - 1, 1))
        scale = (time_step * slab_inside(i)) * in_y
        h0 = hs[0, i, centre, :] - scale * ((es[2, i, above, :] - e2) - (e1x - e1))
        h1 = hs[1, i, centre, :] - scale * ((e0x - e0) - (es[2, i + 1, centre, :] - e2))
        h2 = hs[2, i, centre, :] - scale * ((es[1, i + 1, centre, :] - e1) - (es[0, i, above, :] - e0))
        hs[0, i, centre, :] = h0
        hs[1, i, centre, :] = h1
        hs[2, i, centre, :] = h2

    def main_e(step, i):
        h0, h1, h2 = hs[0, i, centre, :], hs[1, i, centre, :], hs[2, i, centre, :]
        h0x = jnp.where(is_first, border(i, 8 + 2 * step, 0), pltpu.roll(h0, 1, 1))
        h1x = jnp.where(is_first, border(i, 8 + 2 * step + 1, 0), pltpu.roll(h1, 1, 1))
        keep, gain = ce[i, centre, :], ch[i]
        e0, e1, e2 = es[0, i, centre, :], es[1, i, centre, :], es[2, i, centre, :]
        n0 = keep * e0 + gain * ((h2 - hs[2, i, below, :]) - (h1 - h1x))
        n1 = keep * e1 + gain * ((h0 - h0x) - (h2 - hs[2, i - 1, centre, :]))
        n2 = keep * e2 + gain * ((h1 - hs[1, i - 1, centre, :]) - (h0 - hs[0, i, below, :]))
        es[0, i, centre, :] = n0
        es[1, i, centre, :] = n1
        es[2, i, centre, :] = n2
        s0, s1, s2 = e0 + n0, e1 + n1, e2 + n2
        total = s0 * s0 + s1 * s1 + s2 * s2
        if step == 0:
            heat[i] = total
        else:
            heat[i] = heat[i] + total

    for step in range(STEPS):
        main_h(step, step)

        def main_row(i, carry, step=step):
            main_h(step, i)
            main_e(step, i)
            return carry

        lax.fori_loop(step + 1, s_ext - 1 - step, main_row, 0)

    ys = pl.ds(TOP + W, y_dev)
    for c in range(3):
        e_out[c] = es[c, pl.ds(W, s_dev), ys, :]
        h_out[c] = hs[c, pl.ds(W, s_dev), ys, :]

    loss = heat[pl.ds(W, s_dev), pl.ds(W, y_dev), :] * c_ref[...] * (0.25 * time_step * heating)
    parts = split_two(loss.reshape(s_dev * y_dev, lanes))
    thermal = t_ref.shape[0] * t_ref.shape[1]
    ids = ids_ref[...]
    for n in range(3):
        kinds = lax.broadcasted_iota(jnp.int32, (thermal, s_dev * y_dev), 0) + n * thermal
        chosen = jnp.where(kinds == ids, 1.0, 0.0).astype(BF16)
        sums = jnp.dot(chosen, parts, preferred_element_type=F32)
        d_out[n] = (sums[:, :lanes] + sums[:, lanes:]).reshape(t_ref.shape)

    ts, ty = t_ref.shape[0], t_ref.shape[1]
    per = lanes // ty
    row_t = lax.broadcasted_iota(jnp.int32, (ty, lanes), 0)
    lane_t = lax.broadcasted_iota(jnp.int32, (ty, lanes), 1)
    lo_plane, hi_plane = len(up_index), len(dn_index)
    for i in range(ts):
        x = t_ref[i]
        before = t_ref[i - 1] if i > 0 else lo_ref[lo_plane, pl.ds(0, ty), :]
        after = t_ref[i + 1] if i < ts - 1 else hi_ref[hi_plane, pl.ds(0, ty), :]
        edge_lo = jnp.where(sub_lo, ml_ref[3, i, pl.ds(W, 1), :], 0.0)
        edge_hi = jnp.where(sub_hi, mh_ref[3, i, pl.ds(W, 1), :], 0.0)
        left_y = jnp.where(row_t == 0, edge_lo, pltpu.roll(x, 1, 0))
        right_y = jnp.where(row_t == ty - 1, edge_hi, pltpu.roll(x, ty - 1, 0))
        beyond = other_ref[2 * blocks + i // per, pl.ds((i % per) * ty, ty), :]
        from_low = pltpu.roll(beyond, 1, 1) * h_on
        from_high = pltpu.roll(beyond, lanes - 1, 1) * e_on
        left_x = jnp.where(lane_t == 0, from_low, pltpu.roll(x, 1, 1))
        right_x = jnp.where(lane_t == lanes - 1, from_high, pltpu.roll(x, lanes - 1, 1))
        beside = before + after + left_y + right_y + left_x + right_x
        d_out[1, i] = d_out[1, i] - conduction * (6.0 * x - beside)


def main_call(electric, magnetic, conduct, temp_old, ids, lo, hi, m_lo, m_hi, own, other):
    s_dev, y_dev, lanes = conduct.shape
    s_ext, y_ext = s_dev + 2 * W, y_dev + 2 * W
    tall = TOP + y_ext + 8
    return pl.pallas_call(
        functools.partial(main_kernel, lax.axis_size("slab"), lax.axis_size("sub")),
        out_shape=[
            jax.ShapeDtypeStruct(electric.shape, F32),
            jax.ShapeDtypeStruct(magnetic.shape, F32),
            jax.ShapeDtypeStruct((3,) + temp_old.shape, F32),
        ],
        scratch_shapes=[
            pltpu.VMEM((3, s_ext, tall, lanes), F32),
            pltpu.VMEM((3, s_ext, tall, lanes), F32),
            pltpu.VMEM((s_ext, tall, lanes), F32),
            pltpu.VMEM((s_ext, y_ext, lanes), F32),
            pltpu.VMEM((s_ext, y_ext, lanes), F32),
            pltpu.VMEM((3, s_ext, 8, lanes), F32),
            pltpu.VMEM((3, s_ext, 8, lanes), F32),
            pltpu.VMEM((s_ext, 8, lanes), F32),
            pltpu.VMEM((s_ext, 8, lanes), F32),
            pltpu.VMEM((s_ext * 16, lanes), F32),
            pltpu.VMEM((s_ext // 8, y_ext, lanes), F32),
        ],
        compiler_params=pltpu.CompilerParams(vmem_limit_bytes=VMEM_LIMIT),
        name="leapfrog",
    )(electric, magnetic, conduct, temp_old, ids, lo, hi, m_lo, m_hi, own, other)


R = SWEEPS - 1
TTOP = 8


def thermal_kernel(
    n_slab, n_sub, z_ref, zo_ref, t_ref, cap_ref, lo_ref, hi_ref, ml_ref, mh_ref, other_ref,
    out_ref, d0, d1, r0, cs,
):
    ts, ty, lanes = t_ref.shape
    center, spread, rhos = chebyshev_constants(SWEEPS)
    slab_lo, slab_hi = inside_flags("slab", n_slab)
    sub_lo, sub_hi = inside_flags("sub", n_sub)
    comp = lax.axis_index("comp")
    y_ext = 24
    shift = 4
    chunk = pl.ds(TTOP, y_ext)
    above = pl.ds(TTOP + 1, y_ext)
    below = pl.ds(TTOP - 1, y_ext)
    for ref in (d0, d1, r0, cs):
        ref[...] = jnp.zeros_like(ref)
    per = lanes // ty
    caps = other_ref.shape[0] - ts // per
    for half, z in enumerate((z_ref, zo_ref)):
        r0[half, :, pl.ds(TTOP + shift - R, ty + 2 * R), :] = z[...]
    for i in range(ts):
        cs[0, i + 1, pl.ds(TTOP + shift, ty), :] = cap_ref[i]
        cs[0, i + 1, pl.ds(TTOP + shift - 1, 1), :] = ml_ref[3, i, pl.ds(W + 1, 1), :]
        cs[0, i + 1, pl.ds(TTOP + shift + ty, 1), :] = mh_ref[3, i, pl.ds(W + 1, 1), :]
        cs[1, i + 1, pl.ds(TTOP + shift, ty), :] = other_ref[caps + i // per, pl.ds((i % per) * ty, ty), :]
    cs[0, 0, pl.ds(TTOP + shift, ty), :] = lo_ref[lo_ref.shape[0] - 1, pl.ds(ty, ty), :]
    cs[0, ts + 1, pl.ds(TTOP + shift, ty), :] = hi_ref[hi_ref.shape[0] - 1, pl.ds(ty, ty), :]
    d0[...] = r0[...] * (1.0 / center)

    row = lax.broadcasted_iota(jnp.int32, (y_ext, lanes), 0)
    lane = lax.broadcasted_iota(jnp.int32, (y_ext, lanes), 1)
    in_y = ((row >= shift) | sub_lo) & ((row < shift + ty) | sub_hi)
    in_y = jnp.where(in_y, 1.0, 0.0)
    low_half = comp == 0

    def applied(ref, half, i, cap):
        v = ref[half, i, chunk, :]
        w = ref[1 - half, i, chunk, :]
        other_high = low_half if half == 0 else jnp.logical_not(low_half)
        from_low = jnp.where(other_high, 0.0, pltpu.roll(w, 1, 1))
        from_high = jnp.where(other_high, pltpu.roll(w, lanes - 1, 1), 0.0)
        left = jnp.where(lane == 0, from_low, pltpu.roll(v, 1, 1))
        right = jnp.where(lane == lanes - 1, from_high, pltpu.roll(v, lanes - 1, 1))
        beside = ref[half, i - 1, chunk, :] + ref[half, i + 1, chunk, :]
        beside = beside + ref[half, i, above, :] + ref[half, i, below, :] + left + right
        return v, cap * v + conduction * (6.0 * v - beside)

    for i in range(R - 1, ts + R + 1):
        inside = in_y
        if i < R:
            inside = inside * jnp.where(slab_lo, 1.0, 0.0)
        if i >= ts + R:
            inside = inside * jnp.where(slab_hi, 1.0, 0.0)
        for half in range(2):
            if half == 1 and not R <= i < ts + R:
                continue
            v, av = applied(d0, half, i, cs[half, i - 1, chunk, :])
            resid = (r0[half, i, chunk, :] - av) * inside
            r0[half, i, chunk, :] = resid
            d1[half, i, chunk, :] = (rhos[1] * rhos[0]) * v + (2.0 * rhos[1] / spread) * resid
    mine = pl.ds(TTOP + shift, ty)
    for i in range(R, ts + R):
        v, av = applied(d1, 0, i, cs[0, i - 1, chunk, :])
        resid = r0[0, i, chunk, :] - av
        last = (rhos[2] * rhos[1]) * v + (2.0 * rhos[2] / spread) * resid
        r0[0, i, chunk, :] = d0[0, i, chunk, :] + v + last
        out_ref[i - R] = t_ref[i - R] + r0[0, i, mine, :]


def thermal_call(z, z_other, temp_old, capacity, lo, hi, m_lo, m_hi, other):
    ts, ty, lanes = temp_old.shape
    wide = pltpu.VMEM((2, ts + 2 * R, TTOP + 24 + 8, lanes), F32)
    return pl.pallas_call(
        functools.partial(thermal_kernel, lax.axis_size("slab"), lax.axis_size("sub")),
        out_shape=jax.ShapeDtypeStruct(temp_old.shape, F32),
        scratch_shapes=[wide, wide, wide, pltpu.VMEM((2, ts + 2, TTOP + 24 + 8, lanes), F32)],
        compiler_params=pltpu.CompilerParams(vmem_limit_bytes=VMEM_LIMIT),
        name="conduction",
    )(z, z_other, temp_old, capacity, lo, hi, m_lo, m_hi, other)


def lookup_kernel(ids_ref, t_ref, lo_ref, hi_ref, c_ref, out_ref):
    ts, ty, lanes = t_ref.shape
    thermal = ts * ty
    s_dev, y_dev, _ = c_ref.shape
    rows = s_dev * y_dev // lanes
    columns = ids_ref[...].T
    tables = [split_two(r[...].reshape(thermal, lanes)) for r in (lo_ref, t_ref, hi_ref)]
    per = lanes // y_dev
    for a in range(rows):
        column = columns[:, a : a + 1]
        total = jnp.zeros((lanes, 2 * lanes), F32)
        for n in range(3):
            kinds = lax.broadcasted_iota(jnp.int32, (lanes, thermal), 1) + n * thermal
            chosen = jnp.where(kinds == column, 1.0, 0.0).astype(BF16)
            total = total + jnp.dot(chosen, tables[n], preferred_element_type=F32)
        looked = (total[:, :lanes] + total[:, lanes:]).reshape(per, y_dev, lanes)
        at = pl.ds(a * per, per)
        out_ref[at] = c_ref[at] / (1.0 + softening * looked * looked)


def lookup_call(ids, temp_new, lo, hi, conduct):
    return pl.pallas_call(
        lookup_kernel,
        out_shape=jax.ShapeDtypeStruct(conduct.shape, F32),
        compiler_params=pltpu.CompilerParams(vmem_limit_bytes=VMEM_LIMIT),
        name="lookup",
    )(ids, temp_new, lo, hi, conduct)


def sub_edges(values, depth):
    count = lax.axis_size("sub")
    index = lax.axis_index("sub")
    length = values.shape[1]
    if count == 2:
        start = jnp.where(index == 0, length - depth, 0)
        received = swapped(lax.dynamic_slice_in_dim(values, start, depth, axis=1), "sub")
        zero = jnp.zeros_like(received)
        return jnp.where(index == 0, zero, received), jnp.where(index == 0, received, zero)
    return (
        passed_along(values[:, length - depth :], "sub", 1),
        passed_along(values[:, :depth], "sub", -1),
    )


def on_device(electric, magnetic, conduct, temp_old, capacity, offsets, targets):
    lanes = conduct.shape[2]
    thermal = temp_old.shape[0] * temp_old.shape[1]
    ids = (offsets + 1) * thermal + targets
    ids_row = ids.reshape(1, -1)
    ids_square = ids.reshape(-1, lanes)

    up, dn = slab_messages(electric, magnetic, conduct, temp_old, capacity)
    lo, hi = passed_along(up, "slab", 1), passed_along(dn, "slab", -1)
    m_lo, m_hi = sub_exchange(electric, magnetic, conduct, temp_old, capacity, lo, hi)
    own = comp_pack(electric, magnetic, conduct, temp_old, capacity, lo, hi, m_lo, m_hi)
    other = swapped(own, "comp")
    electric, magnetic, sums = main_call(
        electric, magnetic, conduct, temp_old, ids_row, lo, hi, m_lo, m_hi, own, other
    )
    r0 = sums[1] + passed_along(sums[2], "slab", 1) + passed_along(sums[0], "slab", -1)
    y_lo, y_hi = sub_edges(r0, R)
    r_y = jnp.concatenate([y_lo, r0, y_hi], 1)
    s_lo = passed_along(r_y[-R:], "slab", 1)
    s_hi = passed_along(r_y[:R], "slab", -1)
    z = jnp.concatenate([s_lo, r_y, s_hi], 0)
    z_other = swapped(z, "comp")
    temp_new = thermal_call(z, z_other, temp_old, capacity, lo, hi, m_lo, m_hi, other)
    t_lo = passed_along(temp_new, "slab", 1)
    t_hi = passed_along(temp_new, "slab", -1)
    conduct_new = lookup_call(ids_square, temp_new, t_lo, t_hi, conduct)
    return (electric, magnetic, temp_new, conduct_new)


def solution(mesh):
    placed = (
        P(None, ("groups", "slab"), "sub", "comp"),
        P(None, ("groups", "slab"), "sub", "comp"),
        P(("groups", "slab"), "sub", "comp"),
        P(("groups", "slab"), "sub", "comp"),
        P(("groups", "slab"), "sub", "comp"),
        P(("groups", "slab"), "sub", "comp"),
        P(("groups", "slab"), "sub", "comp"),
    )
    return jax.shard_map(
        on_device,
        mesh=mesh,
        in_specs=placed,
        out_specs=(
            P(None, ("groups", "slab"), "sub", "comp"),
            P(None, ("groups", "slab"), "sub", "comp"),
            P(("groups", "slab"), "sub", "comp"),
            P(("groups", "slab"), "sub", "comp"),
        ),
        check_vma=False,
    )
```

```python
import functools

import jax
import jax.numpy as jnp
from jax import lax
from jax.experimental import pallas as pl
from jax.experimental.pallas import tpu as pltpu
from jax.sharding import PartitionSpec as P

STEPS = 4
SWEEPS = 3
W = STEPS

time_step = 0.5
conduction = 2.0
heating = 0.25
softening = 0.25

F32 = jnp.float32
BF16 = jnp.bfloat16
VMEM_LIMIT = 26 * 1024 * 1024
SMALL_LIMIT = 12 * 1024 * 1024


def chebyshev_constants(sweep_count):
    lowest = 1.0
    highest = 4.0 + 12.0 * conduction
    center = 0.5 * (highest + lowest)
    spread = 0.5 * (highest - lowest)
    ratio = center / spread
    rhos = [1.0 / ratio]
    for sweep in range(sweep_count - 1):
        rhos.append(1.0 / (2.0 * ratio - rhos[-1]))
    return (center, spread, rhos)


def passed_along(array, axis, by):
    devices = lax.axis_size(axis)
    pairs = [(i, i + by) for i in range(devices) if 0 <= i + by < devices]
    return lax.ppermute(array, axis, pairs)


def swapped(array, axis):
    return lax.ppermute(array, axis, [(0, 1), (1, 0)])


def plane_list(s_dev):
    up, dn = [], []
    for f in range(7):
        up_rows = W if f in (0, 1, 2, 4, 5) else W - 1
        dn_rows = W if f in (1, 2) else W - 1
        for r in range(s_dev - up_rows, s_dev):
            up.append((f, r))
        for r in range(dn_rows):
            dn.append((f, r))
    return up, dn


def row_source(f, i, s_dev, own, lo, hi, up_index, dn_index):
    r = i - W
    if 0 <= r < s_dev:
        e_ref, h_ref, c_ref = own
        if f < 3:
            return e_ref, (f, r)
        if f < 6:
            return h_ref, (f - 3, r)
        return c_ref, (r,)
    if r < 0:
        key = (f, s_dev + r)
        return (lo, (up_index[key],)) if key in up_index else None
    key = (f, r - s_dev)
    return (hi, (dn_index[key],)) if key in dn_index else None


def indices_of(s_dev):
    up, dn = plane_list(s_dev)
    return (
        {key: n for n, key in enumerate(up)},
        {key: n for n, key in enumerate(dn)},
    )


def edge_rows(edge, y_dev, ty):
    if edge == "high":
        return y_dev - W, ty - 1
    if edge == "low":
        return 0, 0
    upper = lax.axis_index("sub") == 0
    return jnp.where(upper, y_dev - W, 0), jnp.where(upper, ty - 1, 0)


def pack_kernel(edges, e_ref, h_ref, c_ref, t_ref, cap_ref, up_ref, dn_ref, *out_refs):
    s_dev, y_dev = c_ref.shape[0], c_ref.shape[1]
    ts, ty = t_ref.shape[0], t_ref.shape[1]
    for out, planes, i in zip((up_ref, dn_ref), plane_list(s_dev), (ts - 1, 0)):
        for n, (f, r) in enumerate(planes):
            if f < 3:
                out[n] = e_ref[f, r]
            elif f < 6:
                out[n] = h_ref[f - 3, r]
            else:
                out[n] = c_ref[r]
        out[len(planes), pl.ds(0, ty), :] = t_ref[i]
        out[len(planes), pl.ds(ty, ty), :] = cap_ref[i]
    for edge, out in zip(edges, out_refs):
        y0, t0 = edge_rows(edge, y_dev, ty)
        for c in range(3):
            for r in range(s_dev):
                out[c * s_dev + r, pl.ds(0, W), :] = e_ref[c, r, pl.ds(y0, W), :]
                out[c * s_dev + r, pl.ds(W, W), :] = h_ref[c, r, pl.ds(y0, W), :]
        for r in range(s_dev):
            out[3 * s_dev + r // 2, pl.ds((r % 2) * W, W), :] = c_ref[r, pl.ds(y0, W), :]
        base = 3 * s_dev + s_dev // 2
        for i in range(ts):
            out[base + i // 8, pl.ds(i % 8, 1), :] = t_ref[i, pl.ds(t0, 1), :]
            out[base + (ts + i) // 8, pl.ds(i % 8, 1), :] = cap_ref[i, pl.ds(t0, 1), :]


def corner_kernel(edges, s_dev, ty, lo_ref, hi_ref, *out_refs):
    up_index, dn_index = indices_of(s_dev)
    y_dev, lanes = lo_ref.shape[1], lo_ref.shape[2]
    zero = jnp.zeros((W, lanes), F32)
    for edge, out in zip(edges, out_refs):
        y0, _ = edge_rows(edge, y_dev, ty)
        for f in range(7):
            for k in range(2 * W):
                i = k if k < W else s_dev + k
                source = row_source(f, i, s_dev, None, lo_ref, hi_ref, up_index, dn_index)
                value = zero if source is None else source[0][source[1] + (pl.ds(y0, W), slice(None))]
                if f < 6:
                    out[(f % 3) * 2 * W + k, pl.ds((f // 3) * W, W), :] = value
                else:
                    out[6 * W + k // 2, pl.ds((k % 2) * W, W), :] = value


def y_tile(m_ref, k_ref, c, i, s_dev):
    r = i - W
    if 0 <= r < s_dev:
        return m_ref, (c * s_dev + r if c < 3 else 3 * s_dev + r // 2)
    k = i if r < 0 else i - s_dev
    return k_ref, (c * 2 * W + k if c < 3 else 6 * W + k // 2)


def sub_pass(messages):
    if len(messages) == 1:
        received = swapped(messages[0], "sub")
        return received, received
    return passed_along(messages[0], "sub", 1), passed_along(messages[1], "sub", -1)


def halo_exchange(electric, magnetic, conduct, temp_old, capacity):
    s_dev, y_dev, lanes = conduct.shape
    ts, ty, _ = temp_old.shape
    edges = ("either",) if lax.axis_size("sub") == 2 else ("high", "low")
    up, dn = plane_list(s_dev)
    tiles = 3 * s_dev + s_dev // 2 + 2 * ts // 8
    up, dn, *messages = pl.pallas_call(
        functools.partial(pack_kernel, edges),
        out_shape=[
            jax.ShapeDtypeStruct((len(up) + 1, y_dev, lanes), F32),
            jax.ShapeDtypeStruct((len(dn) + 1, y_dev, lanes), F32),
        ]
        + [jax.ShapeDtypeStruct((tiles, 8, lanes), F32)] * len(edges),
        compiler_params=pltpu.CompilerParams(vmem_limit_bytes=SMALL_LIMIT),
        name="pack",
    )(electric, magnetic, conduct, temp_old, capacity)
    m_lo, m_hi = sub_pass(messages)
    lo, hi = passed_along(up, "slab", 1), passed_along(dn, "slab", -1)
    corners = pl.pallas_call(
        functools.partial(corner_kernel, edges, s_dev, ty),
        out_shape=[jax.ShapeDtypeStruct((7 * W, 8, lanes), F32)] * len(edges),
        compiler_params=pltpu.CompilerParams(vmem_limit_bytes=SMALL_LIMIT),
        name="corners",
    )(lo, hi)
    k_lo, k_hi = sub_pass(corners)
    return lo, hi, m_lo, m_hi, k_lo, k_hi


def inside_flags(axis, count):
    index = lax.axis_index(axis)
    return (index > 0), (index < count - 1)


def comp_pack_kernel(
    n_sub, e_ref, h_ref, c_ref, t_ref, cap_ref, lo_ref, hi_ref, ml_ref, mh_ref, kl_ref, kh_ref,
    out_ref, a_ref, b_ref,
):
    s_dev, y_dev, lanes = c_ref.shape
    y_ext = y_dev + 2 * W
    up_index, dn_index = indices_of(s_dev)
    own = (e_ref, h_ref, c_ref)
    has_lo, has_hi = inside_flags("sub", n_sub)
    first = jnp.where(lax.axis_index("comp") == 0, lanes - W, 0)
    lane = lax.broadcasted_iota(jnp.int32, (8, lanes), 1) // W
    a_ref[...] = jnp.zeros_like(a_ref)
    b_ref[...] = jnp.zeros_like(b_ref)
    blocks = (s_dev + 2 * W) // 8
    for b in range(blocks):
        acc_a = jnp.zeros((y_dev, lanes), F32)
        acc_b = jnp.zeros((y_dev, lanes), F32)
        acc_lo = jnp.zeros((8, lanes), F32)
        acc_hi = jnp.zeros((8, lanes), F32)
        for c in range(4):
            for j in range(8):
                i = b * 8 + j
                group = c * 8 + j
                shift = lax.rem(group * W - first + 2 * lanes, lanes)
                here = lane == group
                here_own = jnp.concatenate([here] * (y_dev // 8), 0)
                for which in range(2):
                    if c == 3 and which != i % 2:
                        continue
                    f = 6 if c == 3 else c + 3 * which
                    source = row_source(f, i, s_dev, own, lo_ref, hi_ref, up_index, dn_index)
                    if source is None:
                        continue
                    ref, at = source
                    moved = pltpu.roll(ref[at], shift, 1)
                    if which == 0:
                        acc_a = jnp.where(here_own, moved, acc_a)
                    else:
                        acc_b = jnp.where(here_own, moved, acc_b)
                low, at = y_tile(ml_ref, kl_ref, c, i, s_dev)
                high, _ = y_tile(mh_ref, kh_ref, c, i, s_dev)
                acc_lo = jnp.where(here, pltpu.roll(low[at], shift, 1), acc_lo)
                acc_hi = jnp.where(here, pltpu.roll(high[at], shift, 1), acc_hi)
        acc_lo = jnp.where(has_lo, acc_lo, 0.0)
        acc_hi = jnp.where(has_hi, acc_hi, 0.0)
        a_ref[pl.ds(0, W), :] = acc_lo[:W]
        a_ref[pl.ds(W, y_dev), :] = acc_a
        a_ref[pl.ds(W + y_dev, W), :] = acc_hi[:W]
        b_ref[pl.ds(0, W), :] = acc_lo[W:]
        b_ref[pl.ds(W, y_dev), :] = acc_b
        b_ref[pl.ds(W + y_dev, W), :] = acc_hi[W:]
        out_ref[2 * b] = a_ref[...].T
        out_ref[2 * b + 1] = b_ref[...].T
    rows = t_ref.shape[0] * t_ref.shape[1] // lanes
    for n in range(rows):
        per = lanes // t_ref.shape[1]
        out_ref[2 * blocks + n] = t_ref[pl.ds(n * per, per)].reshape(lanes, lanes)
        out_ref[2 * blocks + rows + n] = cap_ref[pl.ds(n * per, per)].reshape(lanes, lanes)


def comp_pack(electric, magnetic, conduct, temp_old, capacity, *halos):
    s_dev, y_dev, lanes = conduct.shape
    count = 2 * ((s_dev + 2 * W) // 8) + 2 * (temp_old.shape[0] * temp_old.shape[1] // lanes)
    return pl.pallas_call(
        functools.partial(comp_pack_kernel, lax.axis_size("sub")),
        out_shape=jax.ShapeDtypeStruct((count, lanes, lanes), F32),
        scratch_shapes=[pltpu.VMEM((lanes, lanes), F32)] * 2,
        compiler_params=pltpu.CompilerParams(vmem_limit_bytes=SMALL_LIMIT),
        name="comp_pack",
    )(electric, magnetic, conduct, temp_old, capacity, *halos)


TOP = 8


def coefficients(conduct, inside):
    damping = 0.5 * time_step * conduct
    inverse = inside / (1.0 + damping)
    return (1.0 - damping) * inverse, (time_step * time_step) * inverse


def scaled(values, scale):
    return values if scale == 1.0 else values * scale


def split_two(values):
    high = values.astype(BF16)
    low = (values - high.astype(F32)).astype(BF16)
    return jnp.concatenate([high, low], 1)


def main_kernel(
    n_slab, n_sub,
    e_ref, h_ref, c_ref, t_ref, ids_ref, lo_ref, hi_ref, ml_ref, mh_ref, kl_ref, kh_ref,
    own_ref, other_ref,
    e_out, h_out, d_out,
    es, hs, ce, ch, heat, sde, sdh, sce, sch, bt, bp,
):
    s_dev, y_dev, lanes = c_ref.shape
    s_ext, y_ext = s_dev + 2 * W, y_dev + 2 * W
    up_index, dn_index = indices_of(s_dev)
    own = (e_ref, h_ref, c_ref)
    slab_lo, slab_hi = inside_flags("slab", n_slab)
    sub_lo, sub_hi = inside_flags("sub", n_sub)
    comp = lax.axis_index("comp")

    def place(ref, at, f, i, half, c, scale=1.0):
        source = row_source(f, i, s_dev, own, lo_ref, hi_ref, up_index, dn_index)
        if source is None:
            ref[at + (pl.ds(TOP + W, y_dev), slice(None))] = jnp.zeros((y_dev, lanes), F32)
        else:
            s, sat = source
            ref[at + (pl.ds(TOP + W, y_dev), slice(None))] = scaled(s[sat], scale)
        low, tile = y_tile(ml_ref, kl_ref, c, i, s_dev)
        high, _ = y_tile(mh_ref, kh_ref, c, i, s_dev)
        low = low[tile, pl.ds(half * W, W), :]
        high = high[tile, pl.ds(half * W, W), :]
        ref[at + (pl.ds(TOP, W), slice(None))] = scaled(jnp.where(sub_lo, low, 0.0), scale)
        ref[at + (pl.ds(TOP + W + y_dev, W), slice(None))] = scaled(jnp.where(sub_hi, high, 0.0), scale)
        ref[at + (pl.ds(0, TOP), slice(None))] = jnp.zeros((TOP, lanes), F32)
        ref[at + (pl.ds(TOP + y_ext, 8), slice(None))] = jnp.zeros((8, lanes), F32)

    place_y = lax.broadcasted_iota(jnp.int32, (y_ext, lanes), 0)
    in_y = ((place_y >= W) | sub_lo) & ((place_y < W + y_dev) | sub_hi)
    in_y = jnp.where(in_y, 1.0, 0.0)
    lane = lax.broadcasted_iota(jnp.int32, (y_ext, lanes), 1)
    is_last = lane == lanes - 1
    is_first = lane == 0

    def slab_inside(i):
        good = ((i >= W) | slab_lo) & ((i < W + s_dev) | slab_hi)
        return jnp.where(good, 1.0, 0.0)

    for i in range(s_ext):
        for c in range(3):
            place(es, (c, i), c, i, 0, c)
            place(hs, (c, i), c + 3, i, 1, c, 1.0 / time_step)
        place(ce, (i,), 6, i, i % 2, 3)

    def coefs(i, carry):
        keep, gain = coefficients(ce[i, pl.ds(TOP, y_ext), :], in_y * slab_inside(i))
        ce[i, pl.ds(TOP, y_ext), :] = keep
        ch[i] = gain
        return carry

    lax.fori_loop(0, s_ext, coefs, 0)

    first = comp == 0
    blocks = s_ext // 8
    lane8 = lax.broadcasted_iota(jnp.int32, (8, lanes), 1)
    in_y8 = ((lane8 >= W) | sub_lo) & ((lane8 < W + y_dev) | sub_hi)
    in_y8 = jnp.where(in_y8, 1.0, 0.0)
    for b in range(blocks):
        for c in range(4):
            for j in range(8):
                i = b * 8 + j
                for which in range(2):
                    if c == 3 and which != i % 2:
                        continue
                    at = pl.ds((c * 8 + j) * W, W)
                    scale = 1.0 / time_step if which and c < 3 else 1.0
                    mine = scaled(own_ref[2 * b + which, at, :], scale)
                    theirs = scaled(other_ref[2 * b + which, at, :], scale)
                    target = (sdh if which else sde).at[c, i] if c < 3 else sce.at[i]
                    target[pl.ds(0, W), :] = jnp.where(first, mine, theirs)
                    target[pl.ds(W, W), :] = jnp.where(first, theirs, mine)

    def side_coefs(i, carry):
        sce[i], sch[i] = coefficients(sce[i], in_y8 * slab_inside(i))
        return carry

    lax.fori_loop(0, s_ext, side_coefs, 0)

    e_on = jnp.where(comp == 0, 1.0, 0.0)
    h_on = jnp.where(comp == 0, 0.0, 1.0)

    def up_y(v):
        return pltpu.roll(v, lanes - 1, 1)

    def down_y(v):
        return pltpu.roll(v, 1, 1)

    def up_x(v):
        return pltpu.roll(v, 7, 0)

    def down_x(v):
        return pltpu.roll(v, 1, 0)

    bt[...] = jnp.zeros_like(bt)

    def side_h(step, i):
        e0, e1, e2 = sde[0, i], sde[1, i], sde[2, i]
        at = i * 16 + 2 * step
        bt[pl.ds(at, 1), :] = e0[W : W + 1] * e_on
        bt[pl.ds(at + 1, 1), :] = e1[W : W + 1] * e_on
        inside = in_y8 if i >= W else in_y8 * slab_inside(i)
        h0 = (sdh[0, i] - ((up_y(e2) - e2) - (up_x(e1) - e1))) * inside
        h1 = (sdh[1, i] - ((up_x(e0) - e0) - (sde[2, i + 1] - e2))) * inside
        h2 = (sdh[2, i] - ((sde[1, i + 1] - e1) - (up_y(e0) - e0))) * inside
        sdh[0, i], sdh[1, i], sdh[2, i] = h0, h1, h2
        bt[pl.ds(at + 8, 1), :] = h0[W - 1 : W] * h_on
        bt[pl.ds(at + 9, 1), :] = h1[W - 1 : W] * h_on

    def side_e(i):
        h0, h1, h2 = sdh[0, i], sdh[1, i], sdh[2, i]
        keep, gain = sce[i], sch[i]
        sde[0, i] = keep * sde[0, i] + gain * ((h2 - down_y(h2)) - (h1 - down_x(h1)))
        sde[1, i] = keep * sde[1, i] + gain * ((h0 - down_x(h0)) - (h2 - sdh[2, i - 1]))
        sde[2, i] = keep * sde[2, i] + gain * ((h1 - sdh[1, i - 1]) - (h0 - down_y(h0)))

    def side_step(step, carry):
        for i in range(s_ext - 1):
            side_h(step, i)
        for i in range(1, s_ext - 1):
            side_e(i)
        return carry

    lax.fori_loop(0, STEPS, side_step, 0)

    for b in range(blocks):
        bp[b] = bt[pl.ds(b * lanes, lanes), :].T[:y_ext]

    centre = pl.ds(TOP, y_ext)
    above = pl.ds(TOP + 1, y_ext)
    below = pl.ds(TOP - 1, y_ext)

    def border(i, q, to):
        shift = lax.rem(2 * lanes + to - (i % 8) * 16 - q, lanes)
        return pltpu.roll(bp[i // 8], shift, 1)

    def put_h(c, i, curl):
        value = hs[c, i, centre, :] - curl
        if i < W:
            value = value * slab_inside(i)
        hs[c, i, pl.ds(TOP, 8), :] = value[:8] * in_y[:8]
        hs[c, i, pl.ds(TOP + 8, y_ext - 8), :] = value[8:]

    def main_h(step, i):
        e0, e1, e2 = es[0, i, centre, :], es[1, i, centre, :], es[2, i, centre, :]
        e0x = jnp.where(is_last, border(i, 2 * step, lanes - 1), pltpu.roll(e0, lanes - 1, 1))
        e1x = jnp.where(is_last, border(i, 2 * step + 1, lanes - 1), pltpu.roll(e1, lanes - 1, 1))
        put_h(0, i, (es[2, i, above, :] - e2) - (e1x - e1))
        put_h(1, i, (e0x - e0) - (es[2, i + 1, centre, :] - e2))
        put_h(2, i, (es[1, i + 1, centre, :] - e1) - (es[0, i, above, :] - e0))

    def main_e(step, i):
        h0, h1, h2 = hs[0, i, centre, :], hs[1, i, centre, :], hs[2, i, centre, :]
        h0x = jnp.where(is_first, border(i, 8 + 2 * step, 0), pltpu.roll(h0, 1, 1))
        h1x = jnp.where(is_first, border(i, 8 + 2 * step + 1, 0), pltpu.roll(h1, 1, 1))
        keep, gain = ce[i, centre, :], ch[i]
        e0, e1, e2 = es[0, i, centre, :], es[1, i, centre, :], es[2, i, centre, :]
        n0 = keep * e0 + gain * ((h2 - hs[2, i, below, :]) - (h1 - h1x))
        n1 = keep * e1 + gain * ((h0 - h0x) - (h2 - hs[2, i - 1, centre, :]))
        n2 = keep * e2 + gain * ((h1 - hs[1, i - 1, centre, :]) - (h0 - hs[0, i, below, :]))
        es[0, i, centre, :] = n0
        es[1, i, centre, :] = n1
        es[2, i, centre, :] = n2
        if W <= i < W + s_dev:
            s0, s1, s2 = e0 + n0, e1 + n1, e2 + n2
            heat[i - W] = heat[i - W] + (s0 * s0 + s1 * s1 + s2 * s2)

    heat[...] = jnp.zeros_like(heat)

    def main_step(step, carry):
        for i in range(s_ext - 1):
            main_h(step, i)
        for i in range(1, s_ext - 1):
            main_e(step, i)
        return carry

    lax.fori_loop(0, STEPS, main_step, 0)

    ys = pl.ds(TOP + W, y_dev)
    for c in range(3):
        e_out[c] = es[c, pl.ds(W, s_dev), ys, :]
        h_out[c] = hs[c, pl.ds(W, s_dev), ys, :] * time_step

    loss = heat[:, pl.ds(W, y_dev), :] * c_ref[...] * (0.25 * time_step * heating)
    parts = split_two(loss.reshape(s_dev * y_dev, lanes))
    thermal = t_ref.shape[0] * t_ref.shape[1]
    ids = ids_ref[...]
    for n in range(3):
        kinds = lax.broadcasted_iota(jnp.int32, (thermal, s_dev * y_dev), 0) + n * thermal
        chosen = jnp.where(kinds == ids, 1.0, 0.0).astype(BF16)
        sums = jnp.dot(chosen, parts, preferred_element_type=F32)
        d_out[n] = (sums[:, :lanes] + sums[:, lanes:]).reshape(t_ref.shape)

    ts, ty = t_ref.shape[0], t_ref.shape[1]
    per = lanes // ty
    row_t = lax.broadcasted_iota(jnp.int32, (ty, lanes), 0)
    lane_t = lax.broadcasted_iota(jnp.int32, (ty, lanes), 1)
    lo_plane, hi_plane = len(up_index), len(dn_index)
    for i in range(ts):
        x = t_ref[i]
        before = t_ref[i - 1] if i > 0 else lo_ref[lo_plane, pl.ds(0, ty), :]
        after = t_ref[i + 1] if i < ts - 1 else hi_ref[hi_plane, pl.ds(0, ty), :]
        tile = 3 * s_dev + s_dev // 2 + i // 8
        edge_lo = jnp.where(sub_lo, ml_ref[tile, pl.ds(i % 8, 1), :], 0.0)
        edge_hi = jnp.where(sub_hi, mh_ref[tile, pl.ds(i % 8, 1), :], 0.0)
        left_y = jnp.where(row_t == 0, edge_lo, pltpu.roll(x, 1, 0))
        right_y = jnp.where(row_t == ty - 1, edge_hi, pltpu.roll(x, ty - 1, 0))
        beyond = other_ref[2 * blocks + i // per, pl.ds((i % per) * ty, ty), :]
        from_low = pltpu.roll(beyond, 1, 1) * h_on
        from_high = pltpu.roll(beyond, lanes - 1, 1) * e_on
        left_x = jnp.where(lane_t == 0, from_low, pltpu.roll(x, 1, 1))
        right_x = jnp.where(lane_t == lanes - 1, from_high, pltpu.roll(x, lanes - 1, 1))
        beside = before + after + left_y + right_y + left_x + right_x
        d_out[1, i] = d_out[1, i] - conduction * (6.0 * x - beside)


def main_call(electric, magnetic, conduct, temp_old, ids, *halos):
    s_dev, y_dev, lanes = conduct.shape
    s_ext, y_ext = s_dev + 2 * W, y_dev + 2 * W
    tall = TOP + y_ext + 8
    return pl.pallas_call(
        functools.partial(main_kernel, lax.axis_size("slab"), lax.axis_size("sub")),
        out_shape=[
            jax.ShapeDtypeStruct(electric.shape, F32),
            jax.ShapeDtypeStruct(magnetic.shape, F32),
            jax.ShapeDtypeStruct((3,) + temp_old.shape, F32),
        ],
        scratch_shapes=[
            pltpu.VMEM((3, s_ext, tall, lanes), F32),
            pltpu.VMEM((3, s_ext, tall, lanes), F32),
            pltpu.VMEM((s_ext, tall, lanes), F32),
            pltpu.VMEM((s_ext, y_ext, lanes), F32),
            pltpu.VMEM((s_dev, y_ext, lanes), F32),
            pltpu.VMEM((3, s_ext, 8, lanes), F32),
            pltpu.VMEM((3, s_ext, 8, lanes), F32),
            pltpu.VMEM((s_ext, 8, lanes), F32),
            pltpu.VMEM((s_ext, 8, lanes), F32),
            pltpu.VMEM((s_ext * 16, lanes), F32),
            pltpu.VMEM((s_ext // 8, y_ext, lanes), F32),
        ],
        compiler_params=pltpu.CompilerParams(vmem_limit_bytes=VMEM_LIMIT),
        name="leapfrog",
    )(electric, magnetic, conduct, temp_old, ids, *halos)


R = SWEEPS - 1
TTOP = 8


def thermal_kernel(
    n_slab, n_sub, z_ref, zo_ref, t_ref, cap_ref, lo_ref, hi_ref, ml_ref, mh_ref, other_ref,
    out_ref, d0, d1, r0, cs,
):
    ts, ty, lanes = t_ref.shape
    center, spread, rhos = chebyshev_constants(SWEEPS)
    slab_lo, slab_hi = inside_flags("slab", n_slab)
    sub_lo, sub_hi = inside_flags("sub", n_sub)
    comp = lax.axis_index("comp")
    y_ext = 24
    shift = 4
    chunk = pl.ds(TTOP, y_ext)
    above = pl.ds(TTOP + 1, y_ext)
    below = pl.ds(TTOP - 1, y_ext)
    for ref in (d0, d1, r0, cs):
        ref[...] = jnp.zeros_like(ref)
    per = lanes // ty
    caps = other_ref.shape[0] - ts // per
    for half, z in enumerate((z_ref, zo_ref)):
        r0[half, :, pl.ds(TTOP + shift - R, ty + 2 * R), :] = z[...]
    for i in range(ts):
        cs[0, i + 1, pl.ds(TTOP + shift, ty), :] = cap_ref[i]
        tile = ml_ref.shape[0] - ts // 8 + i // 8
        cs[0, i + 1, pl.ds(TTOP + shift - 1, 1), :] = ml_ref[tile, pl.ds(i % 8, 1), :]
        cs[0, i + 1, pl.ds(TTOP + shift + ty, 1), :] = mh_ref[tile, pl.ds(i % 8, 1), :]
        cs[1, i + 1, pl.ds(TTOP + shift, ty), :] = other_ref[caps + i // per, pl.ds((i % per) * ty, ty), :]
    cs[0, 0, pl.ds(TTOP + shift, ty), :] = lo_ref[lo_ref.shape[0] - 1, pl.ds(ty, ty), :]
    cs[0, ts + 1, pl.ds(TTOP + shift, ty), :] = hi_ref[hi_ref.shape[0] - 1, pl.ds(ty, ty), :]
    d0[...] = r0[...] * (1.0 / center)

    row = lax.broadcasted_iota(jnp.int32, (y_ext, lanes), 0)
    lane = lax.broadcasted_iota(jnp.int32, (y_ext, lanes), 1)
    in_y = ((row >= shift) | sub_lo) & ((row < shift + ty) | sub_hi)
    in_y = jnp.where(in_y, 1.0, 0.0)
    low_half = comp == 0

    def applied(ref, half, i, cap):
        v = ref[half, i, chunk, :]
        w = ref[1 - half, i, chunk, :]
        other_high = low_half if half == 0 else jnp.logical_not(low_half)
        from_low = jnp.where(other_high, 0.0, pltpu.roll(w, 1, 1))
        from_high = jnp.where(other_high, pltpu.roll(w, lanes - 1, 1), 0.0)
        left = jnp.where(lane == 0, from_low, pltpu.roll(v, 1, 1))
        right = jnp.where(lane == lanes - 1, from_high, pltpu.roll(v, lanes - 1, 1))
        beside = ref[half, i - 1, chunk, :] + ref[half, i + 1, chunk, :]
        beside = beside + ref[half, i, above, :] + ref[half, i, below, :] + left + right
        return v, cap * v + conduction * (6.0 * v - beside)

    for i in range(R - 1, ts + R + 1):
        inside = in_y
        if i < R:
            inside = inside * jnp.where(slab_lo, 1.0, 0.0)
        if i >= ts + R:
            inside = inside * jnp.where(slab_hi, 1.0, 0.0)
        for half in range(2):
            if half == 1 and not R <= i < ts + R:
                continue
            v, av = applied(d0, half, i, cs[half, i - 1, chunk, :])
            resid = (r0[half, i, chunk, :] - av) * inside
            r0[half, i, chunk, :] = resid
            d1[half, i, chunk, :] = (rhos[1] * rhos[0]) * v + (2.0 * rhos[1] / spread) * resid
    mine = pl.ds(TTOP + shift, ty)
    for i in range(R, ts + R):
        v, av = applied(d1, 0, i, cs[0, i - 1, chunk, :])
        resid = r0[0, i, chunk, :] - av
        last = (rhos[2] * rhos[1]) * v + (2.0 * rhos[2] / spread) * resid
        r0[0, i, chunk, :] = d0[0, i, chunk, :] + v + last
        out_ref[i - R] = t_ref[i - R] + r0[0, i, mine, :]


def thermal_call(z, z_other, temp_old, capacity, lo, hi, m_lo, m_hi, other):
    ts, ty, lanes = temp_old.shape
    wide = pltpu.VMEM((2, ts + 2 * R, TTOP + 24 + 8, lanes), F32)
    return pl.pallas_call(
        functools.partial(thermal_kernel, lax.axis_size("slab"), lax.axis_size("sub")),
        out_shape=jax.ShapeDtypeStruct(temp_old.shape, F32),
        scratch_shapes=[wide, wide, wide, pltpu.VMEM((2, ts + 2, TTOP + 24 + 8, lanes), F32)],
        compiler_params=pltpu.CompilerParams(vmem_limit_bytes=SMALL_LIMIT),
        name="conduction",
    )(z, z_other, temp_old, capacity, lo, hi, m_lo, m_hi, other)


def lookup_kernel(ids_ref, t_ref, lo_ref, hi_ref, c_ref, out_ref):
    ts, ty, lanes = t_ref.shape
    thermal = ts * ty
    s_dev, y_dev, _ = c_ref.shape
    rows = s_dev * y_dev // lanes
    columns = ids_ref[...].T
    tables = [split_two(r[...].reshape(thermal, lanes)) for r in (lo_ref, t_ref, hi_ref)]
    per = lanes // y_dev
    for a in range(rows):
        column = columns[:, a : a + 1]
        total = jnp.zeros((lanes, 2 * lanes), F32)
        for n in range(3):
            kinds = lax.broadcasted_iota(jnp.int32, (lanes, thermal), 1) + n * thermal
            chosen = jnp.where(kinds == column, 1.0, 0.0).astype(BF16)
            total = total + jnp.dot(chosen, tables[n], preferred_element_type=F32)
        looked = (total[:, :lanes] + total[:, lanes:]).reshape(per, y_dev, lanes)
        at = pl.ds(a * per, per)
        out_ref[at] = c_ref[at] / (1.0 + softening * looked * looked)


def lookup_call(ids, temp_new, lo, hi, conduct):
    return pl.pallas_call(
        lookup_kernel,
        out_shape=jax.ShapeDtypeStruct(conduct.shape, F32),
        compiler_params=pltpu.CompilerParams(vmem_limit_bytes=SMALL_LIMIT),
        name="lookup",
    )(ids, temp_new, lo, hi, conduct)


def sub_edges(values, depth):
    count = lax.axis_size("sub")
    index = lax.axis_index("sub")
    length = values.shape[1]
    if count == 2:
        start = jnp.where(index == 0, length - depth, 0)
        received = swapped(lax.dynamic_slice_in_dim(values, start, depth, axis=1), "sub")
        zero = jnp.zeros_like(received)
        return jnp.where(index == 0, zero, received), jnp.where(index == 0, received, zero)
    return (
        passed_along(values[:, length - depth :], "sub", 1),
        passed_along(values[:, :depth], "sub", -1),
    )


def on_device(electric, magnetic, conduct, temp_old, capacity, offsets, targets):
    lanes = conduct.shape[2]
    thermal = temp_old.shape[0] * temp_old.shape[1]
    ids = (offsets + 1) * thermal + targets
    ids_row = ids.reshape(1, -1)
    ids_square = ids.reshape(-1, lanes)

    halos = halo_exchange(electric, magnetic, conduct, temp_old, capacity)
    lo, hi, m_lo, m_hi = halos[:4]
    own = comp_pack(electric, magnetic, conduct, temp_old, capacity, *halos)
    other = swapped(own, "comp")
    electric, magnetic, sums = main_call(
        electric, magnetic, conduct, temp_old, ids_row, *halos, own, other
    )
    r0 = sums[1] + passed_along(sums[2], "slab", 1) + passed_along(sums[0], "slab", -1)
    y_lo, y_hi = sub_edges(r0, R)
    r_y = jnp.concatenate([y_lo, r0, y_hi], 1)
    s_lo = passed_along(r_y[-R:], "slab", 1)
    s_hi = passed_along(r_y[:R], "slab", -1)
    z = jnp.concatenate([s_lo, r_y, s_hi], 0)
    z_other = swapped(z, "comp")
    temp_new = thermal_call(z, z_other, temp_old, capacity, lo, hi, m_lo, m_hi, other)
    t_lo = passed_along(temp_new, "slab", 1)
    t_hi = passed_along(temp_new, "slab", -1)
    conduct_new = lookup_call(ids_square, temp_new, t_lo, t_hi, conduct)
    return (electric, magnetic, temp_new, conduct_new)


def solution(mesh):
    placed = (
        P(None, ("groups", "slab"), "sub", "comp"),
        P(None, ("groups", "slab"), "sub", "comp"),
        P(("groups", "slab"), "sub", "comp"),
        P(("groups", "slab"), "sub", "comp"),
        P(("groups", "slab"), "sub", "comp"),
        P(("groups", "slab"), "sub", "comp"),
        P(("groups", "slab"), "sub", "comp"),
    )
    return jax.shard_map(
        on_device,
        mesh=mesh,
        in_specs=placed,
        out_specs=(
            P(None, ("groups", "slab"), "sub", "comp"),
            P(None, ("groups", "slab"), "sub", "comp"),
            P(("groups", "slab"), "sub", "comp"),
            P(("groups", "slab"), "sub", "comp"),
        ),
        check_vma=False,
    )
```

```python
import functools

import jax
import jax.numpy as jnp
from jax import lax
from jax.experimental import pallas as pl
from jax.experimental.pallas import tpu as pltpu
from jax.sharding import PartitionSpec as P

STEPS = 4
SWEEPS = 3
W = STEPS

time_step = 0.5
conduction = 2.0
heating = 0.25
softening = 0.25

F32 = jnp.float32
BF16 = jnp.bfloat16
VMEM_LIMIT = 20 * 1024 * 1024
SMALL_LIMIT = 12 * 1024 * 1024
PACK_LIMIT = 62 * 1024 * 1024


def chebyshev_constants(sweep_count):
    lowest = 1.0
    highest = 4.0 + 12.0 * conduction
    center = 0.5 * (highest + lowest)
    spread = 0.5 * (highest - lowest)
    ratio = center / spread
    rhos = [1.0 / ratio]
    for sweep in range(sweep_count - 1):
        rhos.append(1.0 / (2.0 * ratio - rhos[-1]))
    return (center, spread, rhos)


def passed_along(array, axis, by):
    devices = lax.axis_size(axis)
    pairs = [(i, i + by) for i in range(devices) if 0 <= i + by < devices]
    return lax.ppermute(array, axis, pairs)


def swapped(array, axis):
    return lax.ppermute(array, axis, [(0, 1), (1, 0)])


def plane_list(s_dev):
    up, dn = [], []
    for f in range(7):
        up_rows = W if f in (0, 1, 2, 4, 5) else W - 1
        dn_rows = W if f in (1, 2) else W - 1
        for r in range(s_dev - up_rows, s_dev):
            up.append((f, r))
        for r in range(dn_rows):
            dn.append((f, r))
    return up, dn


def row_source(f, i, s_dev, own, lo, hi, up_index, dn_index):
    r = i - W
    if 0 <= r < s_dev:
        e_ref, h_ref, c_ref = own
        if f < 3:
            return e_ref, (f, r)
        if f < 6:
            return h_ref, (f - 3, r)
        return c_ref, (r,)
    if r < 0:
        key = (f, s_dev + r)
        return (lo, (up_index[key],)) if key in up_index else None
    key = (f, r - s_dev)
    return (hi, (dn_index[key],)) if key in dn_index else None


def indices_of(s_dev):
    up, dn = plane_list(s_dev)
    return (
        {key: n for n, key in enumerate(up)},
        {key: n for n, key in enumerate(dn)},
    )


def pack_kernel(
    edges, e_ref, h_ref, c_ref, t_ref, cap_ref, off_ref, tgt_ref, ids_ref, up_ref, dn_ref, *refs
):
    count = len(edges)
    sides, ups, downs = refs[:count], refs[count : 2 * count], refs[2 * count : 3 * count]
    es, hs, cs, ts_, caps, sems = refs[3 * count :]
    s_dev, y_dev = c_ref.shape[0], c_ref.shape[1]
    ts, ty = t_ref.shape[0], t_ref.shape[1]
    copies = []

    def copy(src, dst):
        copies.append(pltpu.make_async_copy(src, dst, sems.at[len(copies)]))
        copies[-1].start()

    starts = []
    for n, edge in enumerate(edges):
        if edge == "high":
            y8, t8, y0, t0 = y_dev - 8, ty - 8, 8 - W, 7
        elif edge == "low":
            y8, t8, y0, t0 = 0, 0, 0, 0
        else:
            upper = lax.axis_index("sub") == 0
            y8 = pl.multiple_of(jnp.where(upper, y_dev - 8, 0), 8)
            t8 = pl.multiple_of(jnp.where(upper, ty - 8, 0), 8)
            y0, t0 = jnp.where(upper, 8 - W, 0), jnp.where(upper, 7, 0)
        starts.append((y0, t0))
        copy(e_ref.at[:, :, pl.ds(y8, 8), :], es.at[n])
        copy(h_ref.at[:, :, pl.ds(y8, 8), :], hs.at[n])
        copy(c_ref.at[:, pl.ds(y8, 8), :], cs.at[n])
        copy(t_ref.at[:, pl.ds(t8, 8), :], ts_.at[n])
        copy(cap_ref.at[:, pl.ds(t8, 8), :], caps.at[n])
    edge_copies = len(copies)
    for out, planes, i in zip((up_ref, dn_ref), plane_list(s_dev), (ts - 1, 0)):
        at = 0
        for f in range(7):
            rows = [r for g, r in planes if g == f]
            span = pl.ds(rows[0], len(rows))
            src = e_ref.at[f, span] if f < 3 else h_ref.at[f - 3, span] if f < 6 else c_ref.at[span]
            copy(src, out.at[pl.ds(at, len(rows))])
            at += len(rows)
        copy(t_ref.at[i], out.at[at, pl.ds(0, ty), :])
        copy(cap_ref.at[i], out.at[at, pl.ds(ty, ty), :])
    lanes = ids_ref.shape[1]
    part = lax.broadcasted_iota(jnp.int32, (1, lanes), 1) // y_dev
    for a in range(ids_ref.shape[0]):
        row = jnp.zeros((1, lanes), jnp.int32)
        for k in range(lanes // y_dev):
            s = a * (lanes // y_dev) + k
            kind = (off_ref[s] + 1) * (ts * ty) + tgt_ref[s]
            kind = jnp.concatenate([kind] * (lanes // y_dev), 1)
            row = jnp.where(part == k, kind, row)
        ids_ref[pl.ds(a, 1), :] = row
    for c in copies[:edge_copies]:
        c.wait()
    for n in range(count):
        out = sides[n]
        y0, t0 = starts[n]
        for c in range(3):
            for r in range(s_dev):
                out[c * s_dev + r, pl.ds(0, W), :] = es[n, c, r, pl.ds(y0, W), :]
                out[c * s_dev + r, pl.ds(W, W), :] = hs[n, c, r, pl.ds(y0, W), :]
        for r in range(s_dev):
            out[3 * s_dev + r // 2, pl.ds((r % 2) * W, W), :] = cs[n, r, pl.ds(y0, W), :]
        base = 3 * s_dev + s_dev // 2
        for i in range(ts):
            out[base + i // 8, pl.ds(i % 8, 1), :] = ts_[n, i, pl.ds(t0, 1), :]
            out[base + (ts + i) // 8, pl.ds(i % 8, 1), :] = caps[n, i, pl.ds(t0, 1), :]
        for corner, r0 in ((ups[n], s_dev - W), (downs[n], 0)):
            for c in range(3):
                corner[pl.ds(c * W, W)] = out[pl.ds(c * s_dev + r0, W)]
            corner[pl.ds(3 * W, W // 2)] = out[pl.ds(3 * s_dev + r0 // 2, W // 2)]
    for c in copies[edge_copies:]:
        c.wait()


def y_tile(m_ref, k_refs, c, i, s_dev):
    r = i - W
    if 0 <= r < s_dev:
        return m_ref, (c * s_dev + r if c < 3 else 3 * s_dev + r // 2)
    k = i if r < 0 else r - s_dev
    return k_refs[0 if r < 0 else 1], (c * W + k if c < 3 else 3 * W + k // 2)


def along_both(array, by_slab, by_sub):
    slabs, subs = lax.axis_size("slab"), lax.axis_size("sub")
    pairs = []
    for k in range(slabs):
        for u in range(subs):
            to_k, to_u = k + by_slab, (1 - u if by_sub is None else u + by_sub)
            if 0 <= to_k < slabs and 0 <= to_u < subs:
                pairs.append((k * subs + u, to_k * subs + to_u))
    return lax.ppermute(array, ("slab", "sub"), pairs)


def halo_exchange(electric, magnetic, conduct, temp_old, capacity, offsets, targets):
    s_dev, y_dev, lanes = conduct.shape
    ts, ty, _ = temp_old.shape
    two = lax.axis_size("sub") == 2
    edges = ("either",) if two else ("high", "low")
    count = len(edges)
    up, dn = plane_list(s_dev)
    tiles = 3 * s_dev + s_dev // 2 + 2 * ts // 8
    corner = jax.ShapeDtypeStruct((3 * W + W // 2, 8, lanes), F32)
    ids, up, dn, *messages = pl.pallas_call(
        functools.partial(pack_kernel, edges),
        in_specs=[pl.BlockSpec(memory_space=pltpu.HBM)] * 5
        + [pl.BlockSpec(memory_space=pltpu.VMEM)] * 2,
        out_shape=[
            jax.ShapeDtypeStruct((s_dev * y_dev // lanes, lanes), jnp.int32),
            jax.ShapeDtypeStruct((len(up) + 1, y_dev, lanes), F32),
            jax.ShapeDtypeStruct((len(dn) + 1, y_dev, lanes), F32),
        ]
        + [jax.ShapeDtypeStruct((tiles, 8, lanes), F32)] * count
        + [corner] * (2 * count),
        scratch_shapes=[
            pltpu.VMEM((count, 3, s_dev, 8, lanes), F32),
            pltpu.VMEM((count, 3, s_dev, 8, lanes), F32),
            pltpu.VMEM((count, s_dev, 8, lanes), F32),
            pltpu.VMEM((count, ts, 8, lanes), F32),
            pltpu.VMEM((count, ts, 8, lanes), F32),
            pltpu.SemaphoreType.DMA((5 * count + 18,)),
        ],
        compiler_params=pltpu.CompilerParams(vmem_limit_bytes=PACK_LIMIT),
        name="pack",
    )(
        electric, magnetic, conduct, temp_old, capacity,
        offsets.reshape(s_dev, 1, y_dev), targets.reshape(s_dev, 1, y_dev),
    )
    sides, ups, downs = messages[:count], messages[count : 2 * count], messages[2 * count :]
    lo, hi = passed_along(up, "slab", 1), passed_along(dn, "slab", -1)
    if two:
        m = swapped(sides[0], "sub")
        k = (along_both(ups[0], 1, None), along_both(downs[0], -1, None))
        return ids, (lo, hi, m, m) + k + k
    m_lo, m_hi = passed_along(sides[0], "sub", 1), passed_along(sides[1], "sub", -1)
    k_lo = (along_both(ups[0], 1, 1), along_both(downs[0], -1, 1))
    k_hi = (along_both(ups[1], 1, -1), along_both(downs[1], -1, -1))
    return ids, (lo, hi, m_lo, m_hi) + k_lo + k_hi


def inside_flags(axis, count):
    index = lax.axis_index(axis)
    return (index > 0), (index < count - 1)


def column_shift(group, lanes):
    first = jnp.where(lax.axis_index("comp") == 0, lanes - W, 0)
    return lax.rem(group * W - first + 2 * lanes, lanes)


def gather_columns(sources, which_rows, height, lanes, lane):
    accs = [jnp.zeros((height, lanes), F32), jnp.zeros((height, lanes), F32)]
    for c in range(4):
        for j in range(8):
            group = c * 8 + j
            shift = column_shift(group, lanes)
            here = jnp.concatenate([lane == group] * (height // 8), 0)
            for which in range(2):
                if c == 3 and which != which_rows(j) % 2:
                    continue
                value = sources(6 if c == 3 else c + 3 * which, j)
                if value is not None:
                    accs[which] = jnp.where(here, pltpu.roll(value, shift, 1), accs[which])
    return accs


def columns_kernel(e_ref, h_ref, c_ref, t_ref, cap_ref, out_ref, turn):
    s_dev, y_dev, lanes = c_ref.shape
    lane = lax.broadcasted_iota(jnp.int32, (8, lanes), 1) // W
    turn[...] = jnp.zeros_like(turn)
    for b in range(s_dev // 8):

        def source(f, j, b=b):
            r = b * 8 + j
            return e_ref[f, r] if f < 3 else h_ref[f - 3, r] if f < 6 else c_ref[r]

        accs = gather_columns(source, lambda j: j, y_dev, lanes, lane)
        for which in range(2):
            turn[pl.ds(W, y_dev), :] = accs[which]
            out_ref[2 * b + which] = turn[...].T
    base = s_dev // 4
    rows = t_ref.shape[0] * t_ref.shape[1] // lanes
    per = lanes // t_ref.shape[1]
    for n in range(rows):
        out_ref[base + n] = t_ref[pl.ds(n * per, per)].reshape(lanes, lanes)
        out_ref[base + rows + n] = cap_ref[pl.ds(n * per, per)].reshape(lanes, lanes)


def rims_kernel(
    n_sub, s_dev, lo_ref, hi_ref, ml_ref, mh_ref, kl0_ref, kl1_ref, kh0_ref, kh1_ref, out_ref, turn
):
    y_dev, lanes = lo_ref.shape[1], lo_ref.shape[2]
    y_ext = y_dev + 2 * W
    up_index, dn_index = indices_of(s_dev)
    has_lo, has_hi = inside_flags("sub", n_sub)
    lane = lax.broadcasted_iota(jnp.int32, (8, lanes), 1) // W

    def beside(rows):
        low = jnp.zeros((8, lanes), F32)
        high = jnp.zeros((8, lanes), F32)
        for c in range(4):
            for j in range(8):
                group = c * 8 + j
                shift = column_shift(group, lanes)
                a, tile = y_tile(ml_ref, (kl0_ref, kl1_ref), c, rows[j], s_dev)
                b, _ = y_tile(mh_ref, (kh0_ref, kh1_ref), c, rows[j], s_dev)
                low = jnp.where(lane == group, pltpu.roll(a[tile], shift, 1), low)
                high = jnp.where(lane == group, pltpu.roll(b[tile], shift, 1), high)
        return jnp.where(has_lo, low, 0.0), jnp.where(has_hi, high, 0.0)

    turn[...] = jnp.zeros_like(turn)
    for b in range(s_dev // 8):
        low, high = beside([W + b * 8 + j for j in range(8)])
        turn[pl.ds(16 * b, 8), :] = low
        turn[pl.ds(16 * b + 8, 8), :] = high
    out_ref[0] = turn[...].T

    rows = [k if k < W else s_dev + k for k in range(2 * W)]

    def source(f, j):
        found = row_source(f, rows[j], s_dev, None, lo_ref, hi_ref, up_index, dn_index)
        return None if found is None else found[0][found[1]]

    accs = gather_columns(source, lambda j: j, y_dev, lanes, lane)
    low, high = beside(rows)
    turn[...] = jnp.zeros_like(turn)
    for which in range(2):
        turn[pl.ds(which * y_ext, W), :] = low[which * W : which * W + W]
        turn[pl.ds(which * y_ext + W, y_dev), :] = accs[which]
        turn[pl.ds(which * y_ext + W + y_dev, W), :] = high[which * W : which * W + W]
    out_ref[1] = turn[...].T


def own_columns(electric, magnetic, conduct, temp_old, capacity):
    s_dev, _, lanes = conduct.shape
    count = s_dev // 4 + 2 * (temp_old.shape[0] * temp_old.shape[1] // lanes)
    return pl.pallas_call(
        columns_kernel,
        out_shape=jax.ShapeDtypeStruct((count, lanes, lanes), F32),
        scratch_shapes=[pltpu.VMEM((lanes, lanes), F32)],
        compiler_params=pltpu.CompilerParams(vmem_limit_bytes=SMALL_LIMIT),
        cost_estimate=pl.CostEstimate(flops=10**7, bytes_accessed=8 * 10**6, transcendentals=0),
        name="columns",
    )(electric, magnetic, conduct, temp_old, capacity)


def rim_columns(s_dev, *halos):
    lanes = halos[0].shape[2]
    return pl.pallas_call(
        functools.partial(rims_kernel, lax.axis_size("sub"), s_dev),
        out_shape=jax.ShapeDtypeStruct((2, lanes, lanes), F32),
        scratch_shapes=[pltpu.VMEM((lanes, lanes), F32)],
        compiler_params=pltpu.CompilerParams(vmem_limit_bytes=SMALL_LIMIT),
        name="rims",
    )(*halos)


TOP = 8


def coefficients(conduct, inside):
    damping = 0.5 * time_step * conduct
    inverse = inside / (1.0 + damping)
    return (1.0 - damping) * inverse, (time_step * time_step) * inverse


def scaled(values, scale):
    return values if scale == 1.0 else values * scale


def split_two(values):
    high = values.astype(BF16)
    low = (values - high.astype(F32)).astype(BF16)
    return jnp.concatenate([high, low], 1)


def main_kernel(
    n_slab, n_sub,
    e_ref, h_ref, c_ref, t_ref, ids_ref, lo_ref, hi_ref, ml_ref, mh_ref,
    kl0_ref, kl1_ref, kh0_ref, kh1_ref, own_ref, other_ref, own_rim, other_rim,
    e_out, h_out, d_out,
    e_done, h_done, out_sem, es, hs, ce, ch, heat, sde, sdh, sce, sch, bt, bp,
):
    s_dev, y_dev, lanes = c_ref.shape
    s_ext, y_ext = s_dev + 2 * W, y_dev + 2 * W
    up_index, dn_index = indices_of(s_dev)
    own = (e_ref, h_ref, c_ref)
    slab_lo, slab_hi = inside_flags("slab", n_slab)
    sub_lo, sub_hi = inside_flags("sub", n_sub)
    comp = lax.axis_index("comp")

    def place(ref, at, f, i, half, c, scale=1.0):
        source = row_source(f, i, s_dev, own, lo_ref, hi_ref, up_index, dn_index)
        if source is None:
            ref[at + (pl.ds(TOP + W, y_dev), slice(None))] = jnp.zeros((y_dev, lanes), F32)
        else:
            s, sat = source
            ref[at + (pl.ds(TOP + W, y_dev), slice(None))] = scaled(s[sat], scale)
        low, tile = y_tile(ml_ref, (kl0_ref, kl1_ref), c, i, s_dev)
        high, _ = y_tile(mh_ref, (kh0_ref, kh1_ref), c, i, s_dev)
        low = low[tile, pl.ds(half * W, W), :]
        high = high[tile, pl.ds(half * W, W), :]
        ref[at + (pl.ds(TOP, W), slice(None))] = scaled(jnp.where(sub_lo, low, 0.0), scale)
        ref[at + (pl.ds(TOP + W + y_dev, W), slice(None))] = scaled(jnp.where(sub_hi, high, 0.0), scale)
        ref[at + (pl.ds(0, TOP), slice(None))] = jnp.zeros((TOP, lanes), F32)
        ref[at + (pl.ds(TOP + y_ext, 8), slice(None))] = jnp.zeros((8, lanes), F32)

    place_y = lax.broadcasted_iota(jnp.int32, (y_ext, lanes), 0)
    in_y = ((place_y >= W) | sub_lo) & ((place_y < W + y_dev) | sub_hi)
    in_y = jnp.where(in_y, 1.0, 0.0)
    lane = lax.broadcasted_iota(jnp.int32, (y_ext, lanes), 1)
    is_last = lane == lanes - 1
    is_first = lane == 0

    def slab_inside(i):
        good = ((i >= W) | slab_lo) & ((i < W + s_dev) | slab_hi)
        return jnp.where(good, 1.0, 0.0)

    for i in range(s_ext):
        for c in range(3):
            place(es, (c, i), c, i, 0, c)
            place(hs, (c, i), c + 3, i, 1, c, 1.0 / time_step)
        place(ce, (i,), 6, i, i % 2, 3)

    def coefs(i, carry):
        keep, gain = coefficients(ce[i, pl.ds(TOP, y_ext), :], in_y * slab_inside(i))
        ce[i, pl.ds(TOP, y_ext), :] = keep
        ch[i] = gain
        return carry

    lax.fori_loop(0, s_ext, coefs, 0)

    first = comp == 0
    blocks = s_ext // 8
    lane8 = lax.broadcasted_iota(jnp.int32, (8, lanes), 1)
    in_y8 = ((lane8 >= W) | sub_lo) & ((lane8 < W + y_dev) | sub_hi)
    in_y8 = jnp.where(in_y8, 1.0, 0.0)
    lane_turn = lax.broadcasted_iota(jnp.int32, (lanes, lanes), 1)
    for b in range(s_dev // 8 + 1):
        for which in range(2):
            halves = []
            for cols, rim in ((own_ref, own_rim), (other_ref, other_rim)):
                if b < s_dev // 8:
                    at = 16 * b + W * which
                    low = pltpu.roll(rim[0], (lanes - at) % lanes, 1)
                    high = pltpu.roll(rim[0], (W + y_dev - at - 8) % lanes, 1)
                    value = jnp.where(lane_turn < W, low, cols[2 * b + which])
                    value = jnp.where(lane_turn >= W + y_dev, high, value)
                else:
                    value = pltpu.roll(rim[1], (lanes - which * y_ext) % lanes, 1)
                halves.append(value)
            low = jnp.where(first, halves[0], halves[1])
            high = jnp.where(first, halves[1], halves[0])
            for c in range(4):
                for j in range(8):
                    if c == 3 and which != j % 2:
                        continue
                    i = W + 8 * b + j
                    if b == s_dev // 8:
                        i = j if j < W else s_dev + j
                    at = (c * 8 + j) * W
                    scale = 1.0 / time_step if which and c < 3 else 1.0
                    target = (sdh if which else sde).at[c, i] if c < 3 else sce.at[i]
                    target[pl.ds(0, W), :] = scaled(low[at : at + W], scale)
                    target[pl.ds(W, W), :] = scaled(high[at : at + W], scale)

    def side_coefs(i, carry):
        sce[i], sch[i] = coefficients(sce[i], in_y8 * slab_inside(i))
        return carry

    lax.fori_loop(0, s_ext, side_coefs, 0)

    e_on = jnp.where(comp == 0, 1.0, 0.0)
    h_on = jnp.where(comp == 0, 0.0, 1.0)

    def up_y(v):
        return pltpu.roll(v, lanes - 1, 1)

    def down_y(v):
        return pltpu.roll(v, 1, 1)

    def up_x(v):
        return pltpu.roll(v, 7, 0)

    def down_x(v):
        return pltpu.roll(v, 1, 0)

    bt[...] = jnp.zeros_like(bt)

    def side_h(step, i):
        e0, e1, e2 = sde[0, i], sde[1, i], sde[2, i]
        at = i * 16 + 2 * step
        bt[pl.ds(at, 1), :] = e0[W : W + 1] * e_on
        bt[pl.ds(at + 1, 1), :] = e1[W : W + 1] * e_on
        inside = in_y8 if i >= W else in_y8 * slab_inside(i)
        h0 = (sdh[0, i] - ((up_y(e2) - e2) - (up_x(e1) - e1))) * inside
        h1 = (sdh[1, i] - ((up_x(e0) - e0) - (sde[2, i + 1] - e2))) * inside
        h2 = (sdh[2, i] - ((sde[1, i + 1] - e1) - (up_y(e0) - e0))) * inside
        sdh[0, i], sdh[1, i], sdh[2, i] = h0, h1, h2
        bt[pl.ds(at + 8, 1), :] = h0[W - 1 : W] * h_on
        bt[pl.ds(at + 9, 1), :] = h1[W - 1 : W] * h_on

    def side_e(i):
        h0, h1, h2 = sdh[0, i], sdh[1, i], sdh[2, i]
        keep, gain = sce[i], sch[i]
        sde[0, i] = keep * sde[0, i] + gain * ((h2 - down_y(h2)) - (h1 - down_x(h1)))
        sde[1, i] = keep * sde[1, i] + gain * ((h0 - down_x(h0)) - (h2 - sdh[2, i - 1]))
        sde[2, i] = keep * sde[2, i] + gain * ((h1 - sdh[1, i - 1]) - (h0 - down_y(h0)))

    def side_step(step, carry):
        for i in range(s_ext - 1):
            side_h(step, i)
        for i in range(1, s_ext - 1):
            side_e(i)
        return carry

    lax.fori_loop(0, STEPS, side_step, 0)

    for b in range(blocks):
        bp[b] = bt[pl.ds(b * lanes, lanes), :].T[:y_ext]

    centre = pl.ds(TOP, y_ext)
    above = pl.ds(TOP + 1, y_ext)
    below = pl.ds(TOP - 1, y_ext)

    def border(i, q, to):
        shift = lax.rem(2 * lanes + to - (i % 8) * 16 - q, lanes)
        return pltpu.roll(bp[i // 8], shift, 1)

    def put_h(c, i, curl):
        value = hs[c, i, centre, :] - curl
        if i < W:
            value = value * slab_inside(i)
        hs[c, i, pl.ds(TOP, 8), :] = value[:8] * in_y[:8]
        hs[c, i, pl.ds(TOP + 8, y_ext - 8), :] = value[8:]

    def main_h(step, i):
        e0, e1, e2 = es[0, i, centre, :], es[1, i, centre, :], es[2, i, centre, :]
        e0x = jnp.where(is_last, border(i, 2 * step, lanes - 1), pltpu.roll(e0, lanes - 1, 1))
        e1x = jnp.where(is_last, border(i, 2 * step + 1, lanes - 1), pltpu.roll(e1, lanes - 1, 1))
        put_h(0, i, (es[2, i, above, :] - e2) - (e1x - e1))
        put_h(1, i, (e0x - e0) - (es[2, i + 1, centre, :] - e2))
        put_h(2, i, (es[1, i + 1, centre, :] - e1) - (es[0, i, above, :] - e0))

    def main_e(step, i):
        h0, h1, h2 = hs[0, i, centre, :], hs[1, i, centre, :], hs[2, i, centre, :]
        h0x = jnp.where(is_first, border(i, 8 + 2 * step, 0), pltpu.roll(h0, 1, 1))
        h1x = jnp.where(is_first, border(i, 8 + 2 * step + 1, 0), pltpu.roll(h1, 1, 1))
        keep, gain = ce[i, centre, :], ch[i]
        e0, e1, e2 = es[0, i, centre, :], es[1, i, centre, :], es[2, i, centre, :]
        n0 = keep * e0 + gain * ((h2 - hs[2, i, below, :]) - (h1 - h1x))
        n1 = keep * e1 + gain * ((h0 - h0x) - (h2 - hs[2, i - 1, centre, :]))
        n2 = keep * e2 + gain * ((h1 - hs[1, i - 1, centre, :]) - (h0 - hs[0, i, below, :]))
        es[0, i, centre, :] = n0
        es[1, i, centre, :] = n1
        es[2, i, centre, :] = n2
        if W <= i < W + s_dev:
            s0, s1, s2 = e0 + n0, e1 + n1, e2 + n2
            heat[i - W] = heat[i - W] + (s0 * s0 + s1 * s1 + s2 * s2)

    heat[...] = jnp.zeros_like(heat)

    def main_step(step, carry):
        for i in range(s_ext - 1):
            main_h(step, i)
        for i in range(1, s_ext - 1):
            main_e(step, i)
        return carry

    lax.fori_loop(0, STEPS, main_step, 0)

    ys = pl.ds(TOP + W, y_dev)
    copies = []
    for c in range(3):
        e_done[c] = es[c, pl.ds(W, s_dev), ys, :]
        copies.append(pltpu.make_async_copy(e_done.at[c], e_out.at[c], out_sem.at[2 * c]))
        copies[-1].start()
        h_done[c] = hs[c, pl.ds(W, s_dev), ys, :] * time_step
        copies.append(pltpu.make_async_copy(h_done.at[c], h_out.at[c], out_sem.at[2 * c + 1]))
        copies[-1].start()

    loss = heat[:, pl.ds(W, y_dev), :] * c_ref[...] * (0.25 * time_step * heating)
    parts = split_two(loss.reshape(s_dev * y_dev, lanes))
    thermal = t_ref.shape[0] * t_ref.shape[1]
    ids = ids_ref[...]
    for n in range(3):
        kinds = lax.broadcasted_iota(jnp.int32, (thermal, lanes), 0) + n * thermal
        chosen = [jnp.where(kinds == ids[a : a + 1], 1.0, 0.0).astype(BF16) for a in range(ids.shape[0])]
        chosen = jnp.concatenate(chosen, 1)
        sums = jnp.dot(chosen, parts, preferred_element_type=F32)
        d_out[n] = (sums[:, :lanes] + sums[:, lanes:]).reshape(t_ref.shape)

    ts, ty = t_ref.shape[0], t_ref.shape[1]
    per = lanes // ty
    row_t = lax.broadcasted_iota(jnp.int32, (ty, lanes), 0)
    lane_t = lax.broadcasted_iota(jnp.int32, (ty, lanes), 1)
    lo_plane, hi_plane = len(up_index), len(dn_index)
    for i in range(ts):
        x = t_ref[i]
        before = t_ref[i - 1] if i > 0 else lo_ref[lo_plane, pl.ds(0, ty), :]
        after = t_ref[i + 1] if i < ts - 1 else hi_ref[hi_plane, pl.ds(0, ty), :]
        tile = 3 * s_dev + s_dev // 2 + i // 8
        edge_lo = jnp.where(sub_lo, ml_ref[tile, pl.ds(i % 8, 1), :], 0.0)
        edge_hi = jnp.where(sub_hi, mh_ref[tile, pl.ds(i % 8, 1), :], 0.0)
        left_y = jnp.where(row_t == 0, edge_lo, pltpu.roll(x, 1, 0))
        right_y = jnp.where(row_t == ty - 1, edge_hi, pltpu.roll(x, ty - 1, 0))
        beyond = other_ref[s_dev // 4 + i // per, pl.ds((i % per) * ty, ty), :]
        from_low = pltpu.roll(beyond, 1, 1) * h_on
        from_high = pltpu.roll(beyond, lanes - 1, 1) * e_on
        left_x = jnp.where(lane_t == 0, from_low, pltpu.roll(x, 1, 1))
        right_x = jnp.where(lane_t == lanes - 1, from_high, pltpu.roll(x, lanes - 1, 1))
        beside = before + after + left_y + right_y + left_x + right_x
        d_out[1, i] = d_out[1, i] - conduction * (6.0 * x - beside)
    for copy in copies:
        copy.wait()


def main_call(electric, magnetic, conduct, temp_old, ids, *halos):
    s_dev, y_dev, lanes = conduct.shape
    s_ext, y_ext = s_dev + 2 * W, y_dev + 2 * W
    tall = TOP + y_ext + 8
    return pl.pallas_call(
        functools.partial(main_kernel, lax.axis_size("slab"), lax.axis_size("sub")),
        out_shape=[
            jax.ShapeDtypeStruct(electric.shape, F32),
            jax.ShapeDtypeStruct(magnetic.shape, F32),
            jax.ShapeDtypeStruct((3,) + temp_old.shape, F32),
        ],
        out_specs=[
            pl.BlockSpec(memory_space=pl.ANY),
            pl.BlockSpec(memory_space=pl.ANY),
            pl.BlockSpec(memory_space=pltpu.VMEM),
        ],
        scratch_shapes=[
            pltpu.VMEM(electric.shape, F32),
            pltpu.VMEM(magnetic.shape, F32),
            pltpu.SemaphoreType.DMA((6,)),
            pltpu.VMEM((3, s_ext, tall, lanes), F32),
            pltpu.VMEM((3, s_ext, tall, lanes), F32),
            pltpu.VMEM((s_ext, tall, lanes), F32),
            pltpu.VMEM((s_ext, y_ext, lanes), F32),
            pltpu.VMEM((s_dev, y_ext, lanes), F32),
            pltpu.VMEM((3, s_ext, 8, lanes), F32),
            pltpu.VMEM((3, s_ext, 8, lanes), F32),
            pltpu.VMEM((s_ext, 8, lanes), F32),
            pltpu.VMEM((s_ext, 8, lanes), F32),
            pltpu.VMEM((s_ext * 16, lanes), F32),
            pltpu.VMEM((s_ext // 8, y_ext, lanes), F32),
        ],
        compiler_params=pltpu.CompilerParams(vmem_limit_bytes=VMEM_LIMIT),
        name="leapfrog",
    )(electric, magnetic, conduct, temp_old, ids, *halos)


R = SWEEPS - 1
TTOP = 8


def thermal_kernel(
    n_slab, n_sub, z_ref, zo_ref, t_ref, cap_ref, lo_ref, hi_ref, ml_ref, mh_ref, other_ref,
    out_ref, d0, d1, r0, cs,
):
    ts, ty, lanes = t_ref.shape
    center, spread, rhos = chebyshev_constants(SWEEPS)
    slab_lo, slab_hi = inside_flags("slab", n_slab)
    sub_lo, sub_hi = inside_flags("sub", n_sub)
    comp = lax.axis_index("comp")
    y_ext = 24
    shift = 4
    chunk = pl.ds(TTOP, y_ext)
    above = pl.ds(TTOP + 1, y_ext)
    below = pl.ds(TTOP - 1, y_ext)
    for ref in (d0, d1, r0, cs):
        ref[...] = jnp.zeros_like(ref)
    per = lanes // ty
    caps = other_ref.shape[0] - ts // per
    for half, z in enumerate((z_ref, zo_ref)):
        r0[half, :, pl.ds(TTOP + shift - R, ty + 2 * R), :] = z[...]
    for i in range(ts):
        cs[0, i + 1, pl.ds(TTOP + shift, ty), :] = cap_ref[i]
        tile = ml_ref.shape[0] - ts // 8 + i // 8
        cs[0, i + 1, pl.ds(TTOP + shift - 1, 1), :] = ml_ref[tile, pl.ds(i % 8, 1), :]
        cs[0, i + 1, pl.ds(TTOP + shift + ty, 1), :] = mh_ref[tile, pl.ds(i % 8, 1), :]
        cs[1, i + 1, pl.ds(TTOP + shift, ty), :] = other_ref[caps + i // per, pl.ds((i % per) * ty, ty), :]
    cs[0, 0, pl.ds(TTOP + shift, ty), :] = lo_ref[lo_ref.shape[0] - 1, pl.ds(ty, ty), :]
    cs[0, ts + 1, pl.ds(TTOP + shift, ty), :] = hi_ref[hi_ref.shape[0] - 1, pl.ds(ty, ty), :]
    d0[...] = r0[...] * (1.0 / center)

    row = lax.broadcasted_iota(jnp.int32, (y_ext, lanes), 0)
    lane = lax.broadcasted_iota(jnp.int32, (y_ext, lanes), 1)
    in_y = ((row >= shift) | sub_lo) & ((row < shift + ty) | sub_hi)
    in_y = jnp.where(in_y, 1.0, 0.0)
    low_half = comp == 0

    def applied(ref, half, i, cap):
        v = ref[half, i, chunk, :]
        w = ref[1 - half, i, chunk, :]
        other_high = low_half if half == 0 else jnp.logical_not(low_half)
        from_low = jnp.where(other_high, 0.0, pltpu.roll(w, 1, 1))
        from_high = jnp.where(other_high, pltpu.roll(w, lanes - 1, 1), 0.0)
        left = jnp.where(lane == 0, from_low, pltpu.roll(v, 1, 1))
        right = jnp.where(lane == lanes - 1, from_high, pltpu.roll(v, lanes - 1, 1))
        beside = ref[half, i - 1, chunk, :] + ref[half, i + 1, chunk, :]
        beside = beside + ref[half, i, above, :] + ref[half, i, below, :] + left + right
        return v, cap * v + conduction * (6.0 * v - beside)

    for i in range(R - 1, ts + R + 1):
        inside = in_y
        if i < R:
            inside = inside * jnp.where(slab_lo, 1.0, 0.0)
        if i >= ts + R:
            inside = inside * jnp.where(slab_hi, 1.0, 0.0)
        for half in range(2):
            if half == 1 and not R <= i < ts + R:
                continue
            v, av = applied(d0, half, i, cs[half, i - 1, chunk, :])
            resid = (r0[half, i, chunk, :] - av) * inside
            r0[half, i, chunk, :] = resid
            d1[half, i, chunk, :] = (rhos[1] * rhos[0]) * v + (2.0 * rhos[1] / spread) * resid
    mine = pl.ds(TTOP + shift, ty)
    for i in range(R, ts + R):
        v, av = applied(d1, 0, i, cs[0, i - 1, chunk, :])
        resid = r0[0, i, chunk, :] - av
        last = (rhos[2] * rhos[1]) * v + (2.0 * rhos[2] / spread) * resid
        r0[0, i, chunk, :] = d0[0, i, chunk, :] + v + last
        out_ref[i - R] = t_ref[i - R] + r0[0, i, mine, :]


def thermal_call(z, z_other, temp_old, capacity, lo, hi, m_lo, m_hi, other):
    ts, ty, lanes = temp_old.shape
    wide = pltpu.VMEM((2, ts + 2 * R, TTOP + 24 + 8, lanes), F32)
    return pl.pallas_call(
        functools.partial(thermal_kernel, lax.axis_size("slab"), lax.axis_size("sub")),
        out_shape=jax.ShapeDtypeStruct(temp_old.shape, F32),
        scratch_shapes=[wide, wide, wide, pltpu.VMEM((2, ts + 2, TTOP + 24 + 8, lanes), F32)],
        compiler_params=pltpu.CompilerParams(vmem_limit_bytes=SMALL_LIMIT),
        name="conduction",
    )(z, z_other, temp_old, capacity, lo, hi, m_lo, m_hi, other)


def lookup_kernel(ids_ref, t_ref, lo_ref, hi_ref, c_ref, out_ref):
    ts, ty, lanes = t_ref.shape
    thermal = ts * ty
    s_dev, y_dev, _ = c_ref.shape
    rows = s_dev * y_dev // lanes
    columns = ids_ref[...].T
    tables = [split_two(r[...].reshape(thermal, lanes)) for r in (lo_ref, t_ref, hi_ref)]
    per = lanes // y_dev
    for a in range(rows):
        column = columns[:, a : a + 1]
        total = jnp.zeros((lanes, 2 * lanes), F32)
        for n in range(3):
            kinds = lax.broadcasted_iota(jnp.int32, (lanes, thermal), 1) + n * thermal
            chosen = jnp.where(kinds == column, 1.0, 0.0).astype(BF16)
            total = total + jnp.dot(chosen, tables[n], preferred_element_type=F32)
        looked = (total[:, :lanes] + total[:, lanes:]).reshape(per, y_dev, lanes)
        at = pl.ds(a * per, per)
        out_ref[at] = c_ref[at] / (1.0 + softening * looked * looked)


def lookup_call(ids, temp_new, lo, hi, conduct):
    return pl.pallas_call(
        lookup_kernel,
        out_shape=jax.ShapeDtypeStruct(conduct.shape, F32),
        compiler_params=pltpu.CompilerParams(vmem_limit_bytes=SMALL_LIMIT),
        name="lookup",
    )(ids, temp_new, lo, hi, conduct)


def sub_edges(values, depth):
    count = lax.axis_size("sub")
    index = lax.axis_index("sub")
    length = values.shape[1]
    if count == 2:
        start = jnp.where(index == 0, length - depth, 0)
        received = swapped(lax.dynamic_slice_in_dim(values, start, depth, axis=1), "sub")
        zero = jnp.zeros_like(received)
        return jnp.where(index == 0, zero, received), jnp.where(index == 0, received, zero)
    return (
        passed_along(values[:, length - depth :], "sub", 1),
        passed_along(values[:, :depth], "sub", -1),
    )


def on_device(electric, magnetic, conduct, temp_old, capacity, offsets, targets):
    ids, halos = halo_exchange(
        electric, magnetic, conduct, temp_old, capacity, offsets, targets
    )
    lo, hi, m_lo, m_hi = halos[:4]
    fields = (electric, magnetic, conduct, temp_old, capacity)
    *fields, ids = lax.optimization_barrier(fields + (ids,))
    own = own_columns(*fields)
    own, *halos = lax.optimization_barrier((own,) + halos)
    other = swapped(own, "comp")
    own_rim = rim_columns(conduct.shape[0], *halos)
    other_rim = swapped(own_rim, "comp")
    electric, magnetic, sums = main_call(
        electric, magnetic, conduct, temp_old, ids, *halos, own, other, own_rim, other_rim
    )
    below, here, above = sums[0], sums[1], sums[2]
    from_low = passed_along(jnp.concatenate([here[-R:], above], 0), "slab", 1)
    from_high = passed_along(jnp.concatenate([below, here[:R]], 0), "slab", -1)
    far_low = passed_along(above[-R:], "slab", 2)
    far_high = passed_along(below[:R], "slab", -2)
    index = lax.axis_index("slab")
    low_rows = jnp.where(index > 0, below[-R:] + from_low[:R] + far_low, 0.0)
    high_rows = above[:R] + from_high[-R:] + far_high
    high_rows = jnp.where(index < lax.axis_size("slab") - 1, high_rows, 0.0)
    r0 = jnp.concatenate([low_rows, here + from_low[R:] + from_high[:-R], high_rows], 0)
    y_lo, y_hi = sub_edges(r0, R)
    z = jnp.concatenate([y_lo, r0, y_hi], 1)
    z_other = swapped(z, "comp")
    temp_new = thermal_call(z, z_other, temp_old, capacity, lo, hi, m_lo, m_hi, other)
    t_lo = passed_along(temp_new, "slab", 1)
    t_hi = passed_along(temp_new, "slab", -1)
    conduct_new = lookup_call(ids, temp_new, t_lo, t_hi, conduct)
    return (electric, magnetic, temp_new, conduct_new)


def solution(mesh):
    placed = (
        P(None, ("groups", "slab"), "sub", "comp"),
        P(None, ("groups", "slab"), "sub", "comp"),
        P(("groups", "slab"), "sub", "comp"),
        P(("groups", "slab"), "sub", "comp"),
        P(("groups", "slab"), "sub", "comp"),
        P(("groups", "slab"), "sub", "comp"),
        P(("groups", "slab"), "sub", "comp"),
    )
    return jax.shard_map(
        on_device,
        mesh=mesh,
        in_specs=placed,
        out_specs=(
            P(None, ("groups", "slab"), "sub", "comp"),
            P(None, ("groups", "slab"), "sub", "comp"),
            P(("groups", "slab"), "sub", "comp"),
            P(("groups", "slab"), "sub", "comp"),
        ),
        check_vma=False,
    )
```

```python
import functools

import jax
import jax.numpy as jnp
from jax import lax
from jax.experimental import pallas as pl
from jax.experimental.pallas import tpu as pltpu
from jax.sharding import PartitionSpec as P

STEPS = 4
SWEEPS = 3
W = STEPS
R = SWEEPS - 1

time_step = 0.5
conduction = 2.0
heating = 0.25
softening = 0.25

F32 = jnp.float32
BF16 = jnp.bfloat16
VMEM_LIMIT = 20 * 1024 * 1024
SMALL_LIMIT = 12 * 1024 * 1024
PACK_LIMIT = 60 * 1024 * 1024


def chebyshev_constants(sweep_count):
    lowest = 1.0
    highest = 4.0 + 12.0 * conduction
    center = 0.5 * (highest + lowest)
    spread = 0.5 * (highest - lowest)
    ratio = center / spread
    rhos = [1.0 / ratio]
    for sweep in range(sweep_count - 1):
        rhos.append(1.0 / (2.0 * ratio - rhos[-1]))
    return (center, spread, rhos)


def passed_along(array, axis, by):
    devices = lax.axis_size(axis)
    pairs = [(i, i + by) for i in range(devices) if 0 <= i + by < devices]
    return lax.ppermute(array, axis, pairs)


def swapped(array, axis):
    return lax.ppermute(array, axis, [(0, 1), (1, 0)])


def plane_list(s_dev):
    up, dn = [], []
    for f in range(7):
        up_rows = W if f in (0, 1, 2, 4, 5) else W - 1
        dn_rows = W if f in (1, 2) else W - 1
        for r in range(s_dev - up_rows, s_dev):
            up.append((f, r))
        for r in range(dn_rows):
            dn.append((f, r))
    return up, dn


def row_source(f, i, s_dev, own, lo, hi, up_index, dn_index):
    r = i - W
    if 0 <= r < s_dev:
        e_ref, h_ref, c_ref = own
        if f < 3:
            return e_ref, (f, r)
        if f < 6:
            return h_ref, (f - 3, r)
        return c_ref, (r,)
    if r < 0:
        key = (f, s_dev + r)
        return (lo, (up_index[key],)) if key in up_index else None
    key = (f, r - s_dev)
    return (hi, (dn_index[key],)) if key in dn_index else None


def indices_of(s_dev):
    up, dn = plane_list(s_dev)
    return (
        {key: n for n, key in enumerate(up)},
        {key: n for n, key in enumerate(dn)},
    )


def pack_kernel(
    edges, e_ref, h_ref, c_ref, t_ref, cap_ref, off_ref, tgt_ref, ids_ref, up_ref, dn_ref, *refs
):
    count = len(edges)
    sides, ups, downs = refs[:count], refs[count : 2 * count], refs[2 * count : 3 * count]
    es, hs, cs, ts_, caps, sems = refs[3 * count :]
    s_dev, y_dev = c_ref.shape[0], c_ref.shape[1]
    ts, ty = t_ref.shape[0], t_ref.shape[1]
    copies = []

    def copy(src, dst):
        copies.append(pltpu.make_async_copy(src, dst, sems.at[len(copies)]))
        copies[-1].start()

    starts = []
    for n, edge in enumerate(edges):
        if edge == "high":
            y8, t8, y0, t0 = y_dev - 8, ty - 8, 8 - W, 7
        elif edge == "low":
            y8, t8, y0, t0 = 0, 0, 0, 0
        else:
            upper = lax.axis_index("sub") == 0
            y8 = pl.multiple_of(jnp.where(upper, y_dev - 8, 0), 8)
            t8 = pl.multiple_of(jnp.where(upper, ty - 8, 0), 8)
            y0, t0 = jnp.where(upper, 8 - W, 0), jnp.where(upper, 7, 0)
        starts.append((y0, t0))
        copy(e_ref.at[:, :, pl.ds(y8, 8), :], es.at[n])
        copy(h_ref.at[:, :, pl.ds(y8, 8), :], hs.at[n])
        copy(c_ref.at[:, pl.ds(y8, 8), :], cs.at[n])
        copy(t_ref.at[:, pl.ds(t8, 8), :], ts_.at[n])
        copy(cap_ref.at[:, pl.ds(t8, 8), :], caps.at[n])
    edge_copies = len(copies)
    for out, planes, i in zip((up_ref, dn_ref), plane_list(s_dev), (ts - 1, 0)):
        at = 0
        for f in range(7):
            rows = [r for g, r in planes if g == f]
            span = pl.ds(rows[0], len(rows))
            src = e_ref.at[f, span] if f < 3 else h_ref.at[f - 3, span] if f < 6 else c_ref.at[span]
            copy(src, out.at[pl.ds(at, len(rows))])
            at += len(rows)
        copy(t_ref.at[i], out.at[at, pl.ds(0, ty), :])
        copy(cap_ref.at[i], out.at[at, pl.ds(ty, ty), :])
    lanes = ids_ref.shape[1]
    part = lax.broadcasted_iota(jnp.int32, (1, lanes), 1) // y_dev
    for a in range(ids_ref.shape[0]):
        row = jnp.zeros((1, lanes), jnp.int32)
        for k in range(lanes // y_dev):
            s = a * (lanes // y_dev) + k
            kind = (off_ref[s] + 1) * (ts * ty) + tgt_ref[s]
            kind = jnp.concatenate([kind] * (lanes // y_dev), 1)
            row = jnp.where(part == k, kind, row)
        ids_ref[pl.ds(a, 1), :] = row
    for c in copies[:edge_copies]:
        c.wait()
    for n in range(count):
        out = sides[n]
        y0, t0 = starts[n]
        for c in range(3):
            for r in range(s_dev):
                out[c * s_dev + r, pl.ds(0, W), :] = es[n, c, r, pl.ds(y0, W), :]
                out[c * s_dev + r, pl.ds(W, W), :] = hs[n, c, r, pl.ds(y0, W), :]
        for r in range(s_dev):
            out[3 * s_dev + r // 2, pl.ds((r % 2) * W, W), :] = cs[n, r, pl.ds(y0, W), :]
        base = 3 * s_dev + s_dev // 2
        for i in range(ts):
            out[base + i // 8, pl.ds(i % 8, 1), :] = ts_[n, i, pl.ds(t0, 1), :]
            out[base + (ts + i) // 8, pl.ds(i % 8, 1), :] = caps[n, i, pl.ds(t0, 1), :]
        for corner, r0 in ((ups[n], s_dev - W), (downs[n], 0)):
            for c in range(3):
                corner[pl.ds(c * W, W)] = out[pl.ds(c * s_dev + r0, W)]
            corner[pl.ds(3 * W, W // 2)] = out[pl.ds(3 * s_dev + r0 // 2, W // 2)]
    for c in copies[edge_copies:]:
        c.wait()


def y_tile(m_ref, k_refs, c, i, s_dev):
    r = i - W
    if 0 <= r < s_dev:
        return m_ref, (c * s_dev + r if c < 3 else 3 * s_dev + r // 2)
    k = i if r < 0 else r - s_dev
    return k_refs[0 if r < 0 else 1], (c * W + k if c < 3 else 3 * W + k // 2)


def along_both(array, by_slab, by_sub):
    slabs, subs = lax.axis_size("slab"), lax.axis_size("sub")
    pairs = []
    for k in range(slabs):
        for u in range(subs):
            to_k, to_u = k + by_slab, (1 - u if by_sub is None else u + by_sub)
            if 0 <= to_k < slabs and 0 <= to_u < subs:
                pairs.append((k * subs + u, to_k * subs + to_u))
    return lax.ppermute(array, ("slab", "sub"), pairs)


def halo_exchange(electric, magnetic, conduct, temp_old, capacity, offsets, targets):
    s_dev, y_dev, lanes = conduct.shape
    ts, ty, _ = temp_old.shape
    two = lax.axis_size("sub") == 2
    edges = ("either",) if two else ("high", "low")
    count = len(edges)
    up, dn = plane_list(s_dev)
    tiles = 3 * s_dev + s_dev // 2 + 2 * ts // 8
    corner = jax.ShapeDtypeStruct((3 * W + W // 2, 8, lanes), F32)
    ids, up, dn, *messages = pl.pallas_call(
        functools.partial(pack_kernel, edges),
        in_specs=[pl.BlockSpec(memory_space=pltpu.HBM)] * 5
        + [pl.BlockSpec(memory_space=pltpu.VMEM)] * 2,
        out_shape=[
            jax.ShapeDtypeStruct((s_dev * y_dev // lanes, lanes), jnp.int32),
            jax.ShapeDtypeStruct((len(up) + 1, y_dev, lanes), F32),
            jax.ShapeDtypeStruct((len(dn) + 1, y_dev, lanes), F32),
        ]
        + [jax.ShapeDtypeStruct((tiles, 8, lanes), F32)] * count
        + [corner] * (2 * count),
        scratch_shapes=[
            pltpu.VMEM((count, 3, s_dev, 8, lanes), F32),
            pltpu.VMEM((count, 3, s_dev, 8, lanes), F32),
            pltpu.VMEM((count, s_dev, 8, lanes), F32),
            pltpu.VMEM((count, ts, 8, lanes), F32),
            pltpu.VMEM((count, ts, 8, lanes), F32),
            pltpu.SemaphoreType.DMA((5 * count + 18,)),
        ],
        compiler_params=pltpu.CompilerParams(vmem_limit_bytes=PACK_LIMIT),
        name="pack",
    )(
        electric, magnetic, conduct, temp_old, capacity,
        offsets.reshape(s_dev, 1, y_dev), targets.reshape(s_dev, 1, y_dev),
    )
    sides, ups, downs = messages[:count], messages[count : 2 * count], messages[2 * count :]
    lo, hi = passed_along(up, "slab", 1), passed_along(dn, "slab", -1)
    if two:
        m = swapped(sides[0], "sub")
        k = (along_both(ups[0], 1, None), along_both(downs[0], -1, None))
        return ids, (lo, hi, m, m) + k + k
    m_lo, m_hi = passed_along(sides[0], "sub", 1), passed_along(sides[1], "sub", -1)
    k_lo = (along_both(ups[0], 1, 1), along_both(downs[0], -1, 1))
    k_hi = (along_both(ups[1], 1, -1), along_both(downs[1], -1, -1))
    return ids, (lo, hi, m_lo, m_hi) + k_lo + k_hi


def inside_flags(axis, count):
    index = lax.axis_index(axis)
    return (index > 0), (index < count - 1)


def column_shift(group, lanes):
    first = jnp.where(lax.axis_index("comp") == 0, lanes - W, 0)
    return lax.rem(group * W - first + 2 * lanes, lanes)


def gather_columns(sources, which_rows, height, lanes, lane):
    accs = [jnp.zeros((height, lanes), F32), jnp.zeros((height, lanes), F32)]
    for c in range(4):
        for j in range(8):
            group = c * 8 + j
            shift = column_shift(group, lanes)
            here = jnp.concatenate([lane == group] * (height // 8), 0)
            for which in range(2):
                if c == 3 and which != which_rows(j) % 2:
                    continue
                value = sources(6 if c == 3 else c + 3 * which, j)
                if value is not None:
                    accs[which] = jnp.where(here, pltpu.roll(value, shift, 1), accs[which])
    return accs


def columns_kernel(e_ref, h_ref, c_ref, t_ref, cap_ref, out_ref, turn):
    s_dev, y_dev, lanes = c_ref.shape
    lane = lax.broadcasted_iota(jnp.int32, (8, lanes), 1) // W
    turn[...] = jnp.zeros_like(turn)
    for b in range(s_dev // 8):

        def source(f, j, b=b):
            r = b * 8 + j
            return e_ref[f, r] if f < 3 else h_ref[f - 3, r] if f < 6 else c_ref[r]

        accs = gather_columns(source, lambda j: j, y_dev, lanes, lane)
        for which in range(2):
            turn[pl.ds(W, y_dev), :] = accs[which]
            out_ref[2 * b + which] = turn[...].T
    base = s_dev // 4
    rows = t_ref.shape[0] * t_ref.shape[1] // lanes
    per = lanes // t_ref.shape[1]
    for n in range(rows):
        out_ref[base + n] = t_ref[pl.ds(n * per, per)].reshape(lanes, lanes)
        out_ref[base + rows + n] = cap_ref[pl.ds(n * per, per)].reshape(lanes, lanes)


def rims_kernel(
    n_sub, s_dev, lo_ref, hi_ref, ml_ref, mh_ref, kl0_ref, kl1_ref, kh0_ref, kh1_ref, out_ref, turn
):
    y_dev, lanes = lo_ref.shape[1], lo_ref.shape[2]
    y_ext = y_dev + 2 * W
    up_index, dn_index = indices_of(s_dev)
    has_lo, has_hi = inside_flags("sub", n_sub)
    lane = lax.broadcasted_iota(jnp.int32, (8, lanes), 1) // W

    def beside(rows):
        low = jnp.zeros((8, lanes), F32)
        high = jnp.zeros((8, lanes), F32)
        for c in range(4):
            for j in range(8):
                group = c * 8 + j
                shift = column_shift(group, lanes)
                a, tile = y_tile(ml_ref, (kl0_ref, kl1_ref), c, rows[j], s_dev)
                b, _ = y_tile(mh_ref, (kh0_ref, kh1_ref), c, rows[j], s_dev)
                low = jnp.where(lane == group, pltpu.roll(a[tile], shift, 1), low)
                high = jnp.where(lane == group, pltpu.roll(b[tile], shift, 1), high)
        return jnp.where(has_lo, low, 0.0), jnp.where(has_hi, high, 0.0)

    turn[...] = jnp.zeros_like(turn)
    for b in range(s_dev // 8):
        low, high = beside([W + b * 8 + j for j in range(8)])
        turn[pl.ds(16 * b, 8), :] = low
        turn[pl.ds(16 * b + 8, 8), :] = high
    out_ref[0] = turn[...].T

    rows = [k if k < W else s_dev + k for k in range(2 * W)]

    def source(f, j):
        found = row_source(f, rows[j], s_dev, None, lo_ref, hi_ref, up_index, dn_index)
        return None if found is None else found[0][found[1]]

    accs = gather_columns(source, lambda j: j, y_dev, lanes, lane)
    low, high = beside(rows)
    turn[...] = jnp.zeros_like(turn)
    for which in range(2):
        turn[pl.ds(which * y_ext, W), :] = low[which * W : which * W + W]
        turn[pl.ds(which * y_ext + W, y_dev), :] = accs[which]
        turn[pl.ds(which * y_ext + W + y_dev, W), :] = high[which * W : which * W + W]
    out_ref[1] = turn[...].T


def own_columns(electric, magnetic, conduct, temp_old, capacity):
    s_dev, _, lanes = conduct.shape
    count = s_dev // 4 + 2 * (temp_old.shape[0] * temp_old.shape[1] // lanes)
    return pl.pallas_call(
        columns_kernel,
        out_shape=jax.ShapeDtypeStruct((count, lanes, lanes), F32),
        scratch_shapes=[pltpu.VMEM((lanes, lanes), F32)],
        compiler_params=pltpu.CompilerParams(vmem_limit_bytes=SMALL_LIMIT),
        cost_estimate=pl.CostEstimate(flops=10**7, bytes_accessed=8 * 10**6, transcendentals=0),
        name="columns",
    )(electric, magnetic, conduct, temp_old, capacity)


def rim_columns(s_dev, *halos):
    lanes = halos[0].shape[2]
    return pl.pallas_call(
        functools.partial(rims_kernel, lax.axis_size("sub"), s_dev),
        out_shape=jax.ShapeDtypeStruct((2, lanes, lanes), F32),
        scratch_shapes=[pltpu.VMEM((lanes, lanes), F32)],
        compiler_params=pltpu.CompilerParams(vmem_limit_bytes=SMALL_LIMIT),
        name="rims",
    )(*halos)


TOP = 8


def coefficients(conduct, inside):
    damping = 0.5 * time_step * conduct
    inverse = inside / (1.0 + damping)
    return (1.0 - damping) * inverse, (time_step * time_step) * inverse


def scaled(values, scale):
    return values if scale == 1.0 else values * scale


def split_two(values):
    high = values.astype(BF16)
    low = (values - high.astype(F32)).astype(BF16)
    return jnp.concatenate([high, low], 1)


def main_kernel(
    n_slab, n_sub,
    e_ref, h_ref, c_ref, t_ref, ids_ref, lo_ref, hi_ref, ml_ref, mh_ref,
    kl0_ref, kl1_ref, kh0_ref, kh1_ref, own_ref, other_ref, own_rim, other_rim,
    e_out, h_out, here_out, up_out, dn_out, far_up_out, far_dn_out,
    e_done, h_done, out_sem, es, hs, ce, ch, heat, sde, sdh, sce, sch, bt, bp,
):
    s_dev, y_dev, lanes = c_ref.shape
    s_ext, y_ext = s_dev + 2 * W, y_dev + 2 * W
    up_index, dn_index = indices_of(s_dev)
    own = (e_ref, h_ref, c_ref)
    slab_lo, slab_hi = inside_flags("slab", n_slab)
    sub_lo, sub_hi = inside_flags("sub", n_sub)
    comp = lax.axis_index("comp")

    def place(ref, at, f, i, half, c, scale=1.0):
        source = row_source(f, i, s_dev, own, lo_ref, hi_ref, up_index, dn_index)
        if source is None:
            ref[at + (pl.ds(TOP + W, y_dev), slice(None))] = jnp.zeros((y_dev, lanes), F32)
        else:
            s, sat = source
            ref[at + (pl.ds(TOP + W, y_dev), slice(None))] = scaled(s[sat], scale)
        low, tile = y_tile(ml_ref, (kl0_ref, kl1_ref), c, i, s_dev)
        high, _ = y_tile(mh_ref, (kh0_ref, kh1_ref), c, i, s_dev)
        low = low[tile, pl.ds(half * W, W), :]
        high = high[tile, pl.ds(half * W, W), :]
        ref[at + (pl.ds(TOP, W), slice(None))] = scaled(jnp.where(sub_lo, low, 0.0), scale)
        ref[at + (pl.ds(TOP + W + y_dev, W), slice(None))] = scaled(jnp.where(sub_hi, high, 0.0), scale)
        ref[at + (pl.ds(0, TOP), slice(None))] = jnp.zeros((TOP, lanes), F32)
        ref[at + (pl.ds(TOP + y_ext, 8), slice(None))] = jnp.zeros((8, lanes), F32)

    place_y = lax.broadcasted_iota(jnp.int32, (y_ext, lanes), 0)
    in_y = ((place_y >= W) | sub_lo) & ((place_y < W + y_dev) | sub_hi)
    in_y = jnp.where(in_y, 1.0, 0.0)
    lane = lax.broadcasted_iota(jnp.int32, (y_ext, lanes), 1)
    is_last = lane == lanes - 1
    is_first = lane == 0

    def slab_inside(i):
        good = ((i >= W) | slab_lo) & ((i < W + s_dev) | slab_hi)
        return jnp.where(good, 1.0, 0.0)

    for i in range(s_ext):
        for c in range(3):
            place(es, (c, i), c, i, 0, c)
            place(hs, (c, i), c + 3, i, 1, c, 1.0 / time_step)
        place(ce, (i,), 6, i, i % 2, 3)

    def coefs(i, carry):
        keep, gain = coefficients(ce[i, pl.ds(TOP, y_ext), :], in_y * slab_inside(i))
        ce[i, pl.ds(TOP, y_ext), :] = keep
        ch[i] = gain
        return carry

    lax.fori_loop(0, s_ext, coefs, 0)

    first = comp == 0
    blocks = s_ext // 8
    lane8 = lax.broadcasted_iota(jnp.int32, (8, lanes), 1)
    in_y8 = ((lane8 >= W) | sub_lo) & ((lane8 < W + y_dev) | sub_hi)
    in_y8 = jnp.where(in_y8, 1.0, 0.0)
    lane_turn = lax.broadcasted_iota(jnp.int32, (lanes, lanes), 1)
    for b in range(s_dev // 8 + 1):
        for which in range(2):
            halves = []
            for cols, rim in ((own_ref, own_rim), (other_ref, other_rim)):
                if b < s_dev // 8:
                    at = 16 * b + W * which
                    low = pltpu.roll(rim[0], (lanes - at) % lanes, 1)
                    high = pltpu.roll(rim[0], (W + y_dev - at - 8) % lanes, 1)
                    value = jnp.where(lane_turn < W, low, cols[2 * b + which])
                    value = jnp.where(lane_turn >= W + y_dev, high, value)
                else:
                    value = pltpu.roll(rim[1], (lanes - which * y_ext) % lanes, 1)
                halves.append(value)
            low = jnp.where(first, halves[0], halves[1])
            high = jnp.where(first, halves[1], halves[0])
            for c in range(4):
                for j in range(8):
                    if c == 3 and which != j % 2:
                        continue
                    i = W + 8 * b + j
                    if b == s_dev // 8:
                        i = j if j < W else s_dev + j
                    at = (c * 8 + j) * W
                    scale = 1.0 / time_step if which and c < 3 else 1.0
                    target = (sdh if which else sde).at[c, i] if c < 3 else sce.at[i]
                    target[pl.ds(0, W), :] = scaled(low[at : at + W], scale)
                    target[pl.ds(W, W), :] = scaled(high[at : at + W], scale)

    def side_coefs(i, carry):
        sce[i], sch[i] = coefficients(sce[i], in_y8 * slab_inside(i))
        return carry

    lax.fori_loop(0, s_ext, side_coefs, 0)

    e_on = jnp.where(comp == 0, 1.0, 0.0)
    h_on = jnp.where(comp == 0, 0.0, 1.0)

    def up_y(v):
        return pltpu.roll(v, lanes - 1, 1)

    def down_y(v):
        return pltpu.roll(v, 1, 1)

    def up_x(v):
        return pltpu.roll(v, 7, 0)

    def down_x(v):
        return pltpu.roll(v, 1, 0)

    bt[...] = jnp.zeros_like(bt)

    def side_h(step, i):
        e0, e1, e2 = sde[0, i], sde[1, i], sde[2, i]
        at = i * 16 + 2 * step
        bt[pl.ds(at, 1), :] = e0[W : W + 1] * e_on
        bt[pl.ds(at + 1, 1), :] = e1[W : W + 1] * e_on
        inside = in_y8 if i >= W else in_y8 * slab_inside(i)
        h0 = (sdh[0, i] - ((up_y(e2) - e2) - (up_x(e1) - e1))) * inside
        h1 = (sdh[1, i] - ((up_x(e0) - e0) - (sde[2, i + 1] - e2))) * inside
        h2 = (sdh[2, i] - ((sde[1, i + 1] - e1) - (up_y(e0) - e0))) * inside
        sdh[0, i], sdh[1, i], sdh[2, i] = h0, h1, h2
        bt[pl.ds(at + 8, 1), :] = h1[W - 1 : W] * h_on
        bt[pl.ds(at + 9, 1), :] = h0[W - 1 : W] * h_on

    def side_e(i):
        h0, h1, h2 = sdh[0, i], sdh[1, i], sdh[2, i]
        keep, gain = sce[i], sch[i]
        sde[0, i] = keep * sde[0, i] + gain * ((h2 - down_y(h2)) - (h1 - down_x(h1)))
        sde[1, i] = keep * sde[1, i] + gain * ((h0 - down_x(h0)) - (h2 - sdh[2, i - 1]))
        sde[2, i] = keep * sde[2, i] + gain * ((h1 - sdh[1, i - 1]) - (h0 - down_y(h0)))

    def side_step(step, carry):
        for i in range(s_ext - 1):
            side_h(step, i)
        for i in range(1, s_ext - 1):
            side_e(i)
        return carry

    lax.fori_loop(0, STEPS, side_step, 0)

    for b in range(blocks):
        bp[b] = bt[pl.ds(b * lanes, lanes), :].T[:y_ext]

    centre = pl.ds(TOP, y_ext)
    above = pl.ds(TOP + 1, y_ext)
    below = pl.ds(TOP - 1, y_ext)

    def border(i, q):
        shift = lax.rem(2 * lanes - 1 - (i % 8) * 16 - q, lanes)
        return pltpu.roll(bp[i // 8], shift, 1)

    def put_h(c, i, curl):
        value = hs[c, i, centre, :] - curl
        if i < W:
            value = value * slab_inside(i)
        hs[c, i, pl.ds(TOP, 8), :] = value[:8] * in_y[:8]
        hs[c, i, pl.ds(TOP + 8, y_ext - 8), :] = value[8:]

    def main_h(step, i):
        e0, e1, e2 = es[0, i, centre, :], es[1, i, centre, :], es[2, i, centre, :]
        beyond = border(i, 2 * step)
        e0x = jnp.where(is_last, beyond, pltpu.roll(e0, lanes - 1, 1))
        beyond = border(i, 2 * step + 1)
        e1x = jnp.where(is_last, beyond, pltpu.roll(e1, lanes - 1, 1))
        put_h(0, i, (es[2, i, above, :] - e2) - (e1x - e1))
        put_h(1, i, (e0x - e0) - (es[2, i + 1, centre, :] - e2))
        put_h(2, i, (es[1, i + 1, centre, :] - e1) - (es[0, i, above, :] - e0))

    def main_e(step, i):
        h0, h1, h2 = hs[0, i, centre, :], hs[1, i, centre, :], hs[2, i, centre, :]
        beyond = border(i, 8 + 2 * step)
        h0x = jnp.where(is_first, beyond, pltpu.roll(h0, 1, 1))
        beyond = border(i, 8 + 2 * step - 1)
        h1x = jnp.where(is_first, beyond, pltpu.roll(h1, 1, 1))
        keep, gain = ce[i, centre, :], ch[i]
        e0, e1, e2 = es[0, i, centre, :], es[1, i, centre, :], es[2, i, centre, :]
        n0 = keep * e0 + gain * ((h2 - hs[2, i, below, :]) - (h1 - h1x))
        n1 = keep * e1 + gain * ((h0 - h0x) - (h2 - hs[2, i - 1, centre, :]))
        n2 = keep * e2 + gain * ((h1 - hs[1, i - 1, centre, :]) - (h0 - hs[0, i, below, :]))
        es[0, i, centre, :] = n0
        es[1, i, centre, :] = n1
        es[2, i, centre, :] = n2
        if W <= i < W + s_dev:
            s0, s1, s2 = e0 + n0, e1 + n1, e2 + n2
            heat[i - W] = heat[i - W] + (s0 * s0 + s1 * s1 + s2 * s2)

    heat[...] = jnp.zeros_like(heat)

    for step in range(STEPS):
        for i in range(step, s_ext - 1 - step):
            main_h(step, i)
        for i in range(step + 1, s_ext - 1 - step):
            main_e(step, i)

    ys = pl.ds(TOP + W, y_dev)
    copies = []
    for c in range(3):
        e_done[c] = es[c, pl.ds(W, s_dev), ys, :]
        copies.append(pltpu.make_async_copy(e_done.at[c], e_out.at[c], out_sem.at[2 * c]))
        copies[-1].start()
        h_done[c] = hs[c, pl.ds(W, s_dev), ys, :] * time_step
        copies.append(pltpu.make_async_copy(h_done.at[c], h_out.at[c], out_sem.at[2 * c + 1]))
        copies[-1].start()

    loss = heat[:, pl.ds(W, y_dev), :] * c_ref[...] * (0.25 * time_step * heating)
    parts = split_two(loss.reshape(s_dev * y_dev, lanes))
    thermal = t_ref.shape[0] * t_ref.shape[1]
    ids = ids_ref[...]
    for n in range(3):
        kinds = lax.broadcasted_iota(jnp.int32, (thermal, lanes), 0) + n * thermal
        chosen = [jnp.where(kinds == ids[a : a + 1], 1.0, 0.0).astype(BF16) for a in range(ids.shape[0])]
        chosen = jnp.concatenate(chosen, 1)
        sums = jnp.dot(chosen, parts, preferred_element_type=F32)
        sums = (sums[:, :lanes] + sums[:, lanes:]).reshape(t_ref.shape)
        if n == 0:
            dn_out[pl.ds(0, t_ref.shape[0])] = sums
            far_dn_out[...] = sums[:R]
        elif n == 1:
            here_out[...] = sums
        else:
            up_out[pl.ds(R, t_ref.shape[0])] = sums
            far_up_out[...] = sums[-R:]

    ts, ty = t_ref.shape[0], t_ref.shape[1]
    per = lanes // ty
    row_t = lax.broadcasted_iota(jnp.int32, (ty, lanes), 0)
    lane_t = lax.broadcasted_iota(jnp.int32, (ty, lanes), 1)
    lo_plane, hi_plane = len(up_index), len(dn_index)
    for i in range(ts):
        x = t_ref[i]
        before = t_ref[i - 1] if i > 0 else lo_ref[lo_plane, pl.ds(0, ty), :]
        after = t_ref[i + 1] if i < ts - 1 else hi_ref[hi_plane, pl.ds(0, ty), :]
        tile = 3 * s_dev + s_dev // 2 + i // 8
        edge_lo = jnp.where(sub_lo, ml_ref[tile, pl.ds(i % 8, 1), :], 0.0)
        edge_hi = jnp.where(sub_hi, mh_ref[tile, pl.ds(i % 8, 1), :], 0.0)
        left_y = jnp.where(row_t == 0, edge_lo, pltpu.roll(x, 1, 0))
        right_y = jnp.where(row_t == ty - 1, edge_hi, pltpu.roll(x, ty - 1, 0))
        beyond = other_ref[s_dev // 4 + i // per, pl.ds((i % per) * ty, ty), :]
        from_low = pltpu.roll(beyond, 1, 1) * h_on
        from_high = pltpu.roll(beyond, lanes - 1, 1) * e_on
        left_x = jnp.where(lane_t == 0, from_low, pltpu.roll(x, 1, 1))
        right_x = jnp.where(lane_t == lanes - 1, from_high, pltpu.roll(x, lanes - 1, 1))
        beside = before + after + left_y + right_y + left_x + right_x
        value = here_out[i] - conduction * (6.0 * x - beside)
        here_out[i] = value
        if i < R:
            dn_out[ts + i] = value
        if i >= ts - R:
            up_out[i - ts + R] = value
    for copy in copies:
        copy.wait()


def main_call(electric, magnetic, conduct, temp_old, ids, *halos):
    s_dev, y_dev, lanes = conduct.shape
    s_ext, y_ext = s_dev + 2 * W, y_dev + 2 * W
    tall = TOP + y_ext + 8
    ts, ty, _ = temp_old.shape
    return pl.pallas_call(
        functools.partial(main_kernel, lax.axis_size("slab"), lax.axis_size("sub")),
        out_shape=[
            jax.ShapeDtypeStruct(electric.shape, F32),
            jax.ShapeDtypeStruct(magnetic.shape, F32),
            jax.ShapeDtypeStruct(temp_old.shape, F32),
            jax.ShapeDtypeStruct((ts + R, ty, lanes), F32),
            jax.ShapeDtypeStruct((ts + R, ty, lanes), F32),
            jax.ShapeDtypeStruct((R, ty, lanes), F32),
            jax.ShapeDtypeStruct((R, ty, lanes), F32),
        ],
        out_specs=[pl.BlockSpec(memory_space=pl.ANY)] * 2
        + [pl.BlockSpec(memory_space=pltpu.VMEM)] * 5,
        scratch_shapes=[
            pltpu.VMEM(electric.shape, F32),
            pltpu.VMEM(magnetic.shape, F32),
            pltpu.SemaphoreType.DMA((6,)),
            pltpu.VMEM((3, s_ext, tall, lanes), F32),
            pltpu.VMEM((3, s_ext, tall, lanes), F32),
            pltpu.VMEM((s_ext, tall, lanes), F32),
            pltpu.VMEM((s_ext, y_ext, lanes), F32),
            pltpu.VMEM((s_dev, y_ext, lanes), F32),
            pltpu.VMEM((3, s_ext, 8, lanes), F32),
            pltpu.VMEM((3, s_ext, 8, lanes), F32),
            pltpu.VMEM((s_ext, 8, lanes), F32),
            pltpu.VMEM((s_ext, 8, lanes), F32),
            pltpu.VMEM((s_ext * 16, lanes), F32),
            pltpu.VMEM((s_ext // 8, y_ext, lanes), F32),
        ],
        compiler_params=pltpu.CompilerParams(vmem_limit_bytes=VMEM_LIMIT),
        name="leapfrog",
    )(electric, magnetic, conduct, temp_old, ids, *halos)


TTOP = 8


def thermal_kernel(
    n_slab, n_sub, z_ref, zo_ref, t_ref, cap_ref, lo_ref, hi_ref, ml_ref, mh_ref, other_ref,
    out_ref, send_ref, d0, d1, r0, cs,
):
    ts, ty, lanes = t_ref.shape
    center, spread, rhos = chebyshev_constants(SWEEPS)
    slab_lo, slab_hi = inside_flags("slab", n_slab)
    sub_lo, sub_hi = inside_flags("sub", n_sub)
    comp = lax.axis_index("comp")
    y_ext = 24
    shift = 4
    chunk = pl.ds(TTOP, y_ext)
    above = pl.ds(TTOP + 1, y_ext)
    below = pl.ds(TTOP - 1, y_ext)
    for ref in (d0, d1, r0, cs):
        ref[...] = jnp.zeros_like(ref)
    per = lanes // ty
    caps = other_ref.shape[0] - ts // per
    for half, z in enumerate((z_ref, zo_ref)):
        r0[half, :, pl.ds(TTOP + shift - R, ty + 2 * R), :] = z[...]
    for i in range(ts):
        cs[0, i + 1, pl.ds(TTOP + shift, ty), :] = cap_ref[i]
        tile = ml_ref.shape[0] - ts // 8 + i // 8
        cs[0, i + 1, pl.ds(TTOP + shift - 1, 1), :] = ml_ref[tile, pl.ds(i % 8, 1), :]
        cs[0, i + 1, pl.ds(TTOP + shift + ty, 1), :] = mh_ref[tile, pl.ds(i % 8, 1), :]
        cs[1, i + 1, pl.ds(TTOP + shift, ty), :] = other_ref[caps + i // per, pl.ds((i % per) * ty, ty), :]
    cs[0, 0, pl.ds(TTOP + shift, ty), :] = lo_ref[lo_ref.shape[0] - 1, pl.ds(ty, ty), :]
    cs[0, ts + 1, pl.ds(TTOP + shift, ty), :] = hi_ref[hi_ref.shape[0] - 1, pl.ds(ty, ty), :]
    d0[...] = r0[...] * (1.0 / center)

    row = lax.broadcasted_iota(jnp.int32, (y_ext, lanes), 0)
    lane = lax.broadcasted_iota(jnp.int32, (y_ext, lanes), 1)
    in_y = ((row >= shift) | sub_lo) & ((row < shift + ty) | sub_hi)
    in_y = jnp.where(in_y, 1.0, 0.0)
    low_half = comp == 0

    def applied(ref, half, i, cap):
        v = ref[half, i, chunk, :]
        w = ref[1 - half, i, chunk, :]
        other_high = low_half if half == 0 else jnp.logical_not(low_half)
        from_low = jnp.where(other_high, 0.0, pltpu.roll(w, 1, 1))
        from_high = jnp.where(other_high, pltpu.roll(w, lanes - 1, 1), 0.0)
        left = jnp.where(lane == 0, from_low, pltpu.roll(v, 1, 1))
        right = jnp.where(lane == lanes - 1, from_high, pltpu.roll(v, lanes - 1, 1))
        beside = ref[half, i - 1, chunk, :] + ref[half, i + 1, chunk, :]
        beside = beside + ref[half, i, above, :] + ref[half, i, below, :] + left + right
        return v, cap * v + conduction * (6.0 * v - beside)

    for i in range(R - 1, ts + R + 1):
        inside = in_y
        if i < R:
            inside = inside * jnp.where(slab_lo, 1.0, 0.0)
        if i >= ts + R:
            inside = inside * jnp.where(slab_hi, 1.0, 0.0)
        for half in range(2):
            if half == 1 and not R <= i < ts + R:
                continue
            v, av = applied(d0, half, i, cs[half, i - 1, chunk, :])
            resid = (r0[half, i, chunk, :] - av) * inside
            r0[half, i, chunk, :] = resid
            d1[half, i, chunk, :] = (rhos[1] * rhos[0]) * v + (2.0 * rhos[1] / spread) * resid
    mine = pl.ds(TTOP + shift, ty)
    for i in range(R, ts + R):
        v, av = applied(d1, 0, i, cs[0, i - 1, chunk, :])
        resid = r0[0, i, chunk, :] - av
        last = (rhos[2] * rhos[1]) * v + (2.0 * rhos[2] / spread) * resid
        r0[0, i, chunk, :] = d0[0, i, chunk, :] + v + last
        value = t_ref[i - R] + r0[0, i, mine, :]
        out_ref[i - R] = value
        send_ref[i - R] = value


def thermal_call(z, z_other, temp_old, capacity, lo, hi, m_lo, m_hi, other):
    ts, ty, lanes = temp_old.shape
    wide = pltpu.VMEM((2, ts + 2 * R, TTOP + 24 + 8, lanes), F32)
    return pl.pallas_call(
        functools.partial(thermal_kernel, lax.axis_size("slab"), lax.axis_size("sub")),
        out_shape=[jax.ShapeDtypeStruct(temp_old.shape, F32)] * 2,
        scratch_shapes=[wide, wide, wide, pltpu.VMEM((2, ts + 2, TTOP + 24 + 8, lanes), F32)],
        compiler_params=pltpu.CompilerParams(vmem_limit_bytes=SMALL_LIMIT),
        name="conduction",
    )(z, z_other, temp_old, capacity, lo, hi, m_lo, m_hi, other)


def lookup_kernel(ids_ref, t_ref, lo_ref, hi_ref, c_ref, out_ref):
    ts, ty, lanes = t_ref.shape
    thermal = ts * ty
    s_dev, y_dev, _ = c_ref.shape
    rows = s_dev * y_dev // lanes
    columns = ids_ref[...].T
    tables = [split_two(r[...].reshape(thermal, lanes)) for r in (lo_ref, t_ref, hi_ref)]
    per = lanes // y_dev
    for a in range(rows):
        column = columns[:, a : a + 1]
        total = jnp.zeros((lanes, 2 * lanes), F32)
        for n in range(3):
            kinds = lax.broadcasted_iota(jnp.int32, (lanes, thermal), 1) + n * thermal
            chosen = jnp.where(kinds == column, 1.0, 0.0).astype(BF16)
            total = total + jnp.dot(chosen, tables[n], preferred_element_type=F32)
        looked = (total[:, :lanes] + total[:, lanes:]).reshape(per, y_dev, lanes)
        at = pl.ds(a * per, per)
        out_ref[at] = c_ref[at] / (1.0 + softening * looked * looked)


def lookup_call(ids, temp_new, lo, hi, conduct):
    return pl.pallas_call(
        lookup_kernel,
        out_shape=jax.ShapeDtypeStruct(conduct.shape, F32),
        compiler_params=pltpu.CompilerParams(vmem_limit_bytes=SMALL_LIMIT),
        name="lookup",
    )(ids, temp_new, lo, hi, conduct)


def combine_kernel(
    n_slab, edges, here_ref, up_ref, dn_ref, low_ref, high_ref, far_low_ref, far_high_ref,
    out_ref, *edge_refs
):
    ts, ty, _ = here_ref.shape
    slab_lo, slab_hi = inside_flags("slab", n_slab)
    low = dn_ref[pl.ds(ts - R, R)] + low_ref[pl.ds(0, R)] + far_low_ref[...]
    high = up_ref[pl.ds(R, R)] + high_ref[pl.ds(ts, R)] + far_high_ref[...]
    out_ref[pl.ds(0, R)] = jnp.where(slab_lo, low, 0.0)
    out_ref[pl.ds(R, ts)] = here_ref[...] + low_ref[pl.ds(R, ts)] + high_ref[pl.ds(0, ts)]
    out_ref[pl.ds(R + ts, R)] = jnp.where(slab_hi, high, 0.0)
    for edge, ref in zip(edges, edge_refs):
        if edge == "either":
            start = jnp.where(lax.axis_index("sub") == 0, ty - R, 0)
        else:
            start = ty - R if edge == "high" else 0
        ref[...] = out_ref[:, pl.ds(start, R), :]


def residual(here, up, dn, far_up, far_dn):
    ts, ty, lanes = here.shape
    from_low, from_high = passed_along(up, "slab", 1), passed_along(dn, "slab", -1)
    far_low, far_high = passed_along(far_up, "slab", 2), passed_along(far_dn, "slab", -2)
    two = lax.axis_size("sub") == 2
    edges = ("either",) if two else ("high", "low")
    r0, *messages = pl.pallas_call(
        functools.partial(combine_kernel, lax.axis_size("slab"), edges),
        out_shape=[jax.ShapeDtypeStruct((ts + 2 * R, ty, lanes), F32)]
        + [jax.ShapeDtypeStruct((ts + 2 * R, R, lanes), F32)] * len(edges),
        compiler_params=pltpu.CompilerParams(vmem_limit_bytes=SMALL_LIMIT),
        name="combine",
    )(here, up, dn, from_low, from_high, far_low, far_high)
    if two:
        received = swapped(messages[0], "sub")
        index = lax.axis_index("sub")
        y_lo, y_hi = jnp.where(index == 0, 0.0, received), jnp.where(index == 0, received, 0.0)
    else:
        y_lo = passed_along(messages[0], "sub", 1)
        y_hi = passed_along(messages[1], "sub", -1)
    return jnp.concatenate([y_lo, r0, y_hi], 1)


def on_device(electric, magnetic, conduct, temp_old, capacity, offsets, targets):
    ids, halos = halo_exchange(
        electric, magnetic, conduct, temp_old, capacity, offsets, targets
    )
    lo, hi, m_lo, m_hi = halos[:4]
    fields = (electric, magnetic, conduct, temp_old, capacity)
    *fields, ids = lax.optimization_barrier(fields + (ids,))
    own = own_columns(*fields)
    own, *halos = lax.optimization_barrier((own,) + halos)
    other = swapped(own, "comp")
    own_rim = rim_columns(conduct.shape[0], *halos)
    other_rim = swapped(own_rim, "comp")
    electric, magnetic, *shares = main_call(
        electric, magnetic, conduct, temp_old, ids, *halos, own, other, own_rim, other_rim
    )
    z = residual(*shares)
    z_other = swapped(z, "comp")
    temp_new, temp_sent = thermal_call(z, z_other, temp_old, capacity, lo, hi, m_lo, m_hi, other)
    t_lo = passed_along(temp_sent, "slab", 1)
    t_hi = passed_along(temp_sent, "slab", -1)
    conduct_new = lookup_call(ids, temp_sent, t_lo, t_hi, conduct)
    return (electric, magnetic, temp_new, conduct_new)


def solution(mesh):
    placed = (
        P(None, ("groups", "slab"), "sub", "comp"),
        P(None, ("groups", "slab"), "sub", "comp"),
        P(("groups", "slab"), "sub", "comp"),
        P(("groups", "slab"), "sub", "comp"),
        P(("groups", "slab"), "sub", "comp"),
        P(("groups", "slab"), "sub", "comp"),
        P(("groups", "slab"), "sub", "comp"),
    )
    return jax.shard_map(
        on_device,
        mesh=mesh,
        in_specs=placed,
        out_specs=(
            P(None, ("groups", "slab"), "sub", "comp"),
            P(None, ("groups", "slab"), "sub", "comp"),
            P(("groups", "slab"), "sub", "comp"),
            P(("groups", "slab"), "sub", "comp"),
        ),
        check_vma=False,
    )
```

```python
import functools

import jax
import jax.numpy as jnp
from jax import lax
from jax.experimental import pallas as pl
from jax.experimental.pallas import tpu as pltpu
from jax.sharding import PartitionSpec as P

STEPS = 4
SWEEPS = 3
W = STEPS
R = SWEEPS - 1

time_step = 0.5
conduction = 2.0
heating = 0.25
softening = 0.25

F32 = jnp.float32
BF16 = jnp.bfloat16
VMEM_LIMIT = 20 * 1024 * 1024
SMALL_LIMIT = 12 * 1024 * 1024
PACK_LIMIT = 60 * 1024 * 1024


def chebyshev_constants(sweep_count):
    lowest = 1.0
    highest = 4.0 + 12.0 * conduction
    center = 0.5 * (highest + lowest)
    spread = 0.5 * (highest - lowest)
    ratio = center / spread
    rhos = [1.0 / ratio]
    for sweep in range(sweep_count - 1):
        rhos.append(1.0 / (2.0 * ratio - rhos[-1]))
    return (center, spread, rhos)


def passed_along(array, axis, by):
    devices = lax.axis_size(axis)
    pairs = [(i, i + by) for i in range(devices) if 0 <= i + by < devices]
    return lax.ppermute(array, axis, pairs)


def swapped(array, axis):
    return lax.ppermute(array, axis, [(0, 1), (1, 0)])


def plane_list(s_dev):
    up, dn = [], []
    for f in range(7):
        up_rows = W if f in (0, 1, 2, 4, 5) else W - 1
        dn_rows = W if f in (1, 2) else W - 1
        for r in range(s_dev - up_rows, s_dev):
            up.append((f, r))
        for r in range(dn_rows):
            dn.append((f, r))
    return up, dn


def row_source(f, i, s_dev, own, lo, hi, up_index, dn_index):
    r = i - W
    if 0 <= r < s_dev:
        e_ref, h_ref, c_ref = own
        if f < 3:
            return e_ref, (f, r)
        if f < 6:
            return h_ref, (f - 3, r)
        return c_ref, (r,)
    if r < 0:
        key = (f, s_dev + r)
        return (lo, (up_index[key],)) if key in up_index else None
    key = (f, r - s_dev)
    return (hi, (dn_index[key],)) if key in dn_index else None


def indices_of(s_dev):
    up, dn = plane_list(s_dev)
    return (
        {key: n for n, key in enumerate(up)},
        {key: n for n, key in enumerate(dn)},
    )


def pack_kernel(
    edges, e_ref, h_ref, c_ref, t_ref, cap_ref, off_ref, tgt_ref, ids_ref, up_ref, dn_ref, *refs
):
    count = len(edges)
    sides, ups, downs = refs[:count], refs[count : 2 * count], refs[2 * count : 3 * count]
    es, hs, cs, ts_, caps, sems = refs[3 * count :]
    s_dev, y_dev = c_ref.shape[0], c_ref.shape[1]
    ts, ty = t_ref.shape[0], t_ref.shape[1]
    copies = []

    def copy(src, dst):
        copies.append(pltpu.make_async_copy(src, dst, sems.at[len(copies)]))
        copies[-1].start()

    starts = []
    for n, edge in enumerate(edges):
        if edge == "high":
            y8, t8, y0, t0 = y_dev - 8, ty - 8, 8 - W, 7
        elif edge == "low":
            y8, t8, y0, t0 = 0, 0, 0, 0
        else:
            upper = lax.axis_index("sub") == 0
            y8 = pl.multiple_of(jnp.where(upper, y_dev - 8, 0), 8)
            t8 = pl.multiple_of(jnp.where(upper, ty - 8, 0), 8)
            y0, t0 = jnp.where(upper, 8 - W, 0), jnp.where(upper, 7, 0)
        starts.append((y0, t0))
        copy(e_ref.at[:, :, pl.ds(y8, 8), :], es.at[n])
        copy(h_ref.at[:, :, pl.ds(y8, 8), :], hs.at[n])
        copy(c_ref.at[:, pl.ds(y8, 8), :], cs.at[n])
        copy(t_ref.at[:, pl.ds(t8, 8), :], ts_.at[n])
        copy(cap_ref.at[:, pl.ds(t8, 8), :], caps.at[n])
    edge_copies = len(copies)
    for out, planes, i in zip((up_ref, dn_ref), plane_list(s_dev), (ts - 1, 0)):
        at = 0
        for f in range(7):
            rows = [r for g, r in planes if g == f]
            span = pl.ds(rows[0], len(rows))
            src = e_ref.at[f, span] if f < 3 else h_ref.at[f - 3, span] if f < 6 else c_ref.at[span]
            copy(src, out.at[pl.ds(at, len(rows))])
            at += len(rows)
        copy(t_ref.at[i], out.at[at, pl.ds(0, ty), :])
        copy(cap_ref.at[i], out.at[at, pl.ds(ty, ty), :])
    lanes = ids_ref.shape[1]
    part = lax.broadcasted_iota(jnp.int32, (1, lanes), 1) // y_dev
    for a in range(ids_ref.shape[0]):
        row = jnp.zeros((1, lanes), jnp.int32)
        for k in range(lanes // y_dev):
            s = a * (lanes // y_dev) + k
            kind = (off_ref[s] + 1) * (ts * ty) + tgt_ref[s]
            kind = jnp.concatenate([kind] * (lanes // y_dev), 1)
            row = jnp.where(part == k, kind, row)
        ids_ref[pl.ds(a, 1), :] = row
    for c in copies[:edge_copies]:
        c.wait()
    for n in range(count):
        out = sides[n]
        y0, t0 = starts[n]
        for c in range(3):
            for r in range(s_dev):
                out[c * s_dev + r, pl.ds(0, W), :] = es[n, c, r, pl.ds(y0, W), :]
                out[c * s_dev + r, pl.ds(W, W), :] = hs[n, c, r, pl.ds(y0, W), :]
        for r in range(s_dev):
            out[3 * s_dev + r // 2, pl.ds((r % 2) * W, W), :] = cs[n, r, pl.ds(y0, W), :]
        base = 3 * s_dev + s_dev // 2
        for i in range(ts):
            out[base + i // 8, pl.ds(i % 8, 1), :] = ts_[n, i, pl.ds(t0, 1), :]
            out[base + (ts + i) // 8, pl.ds(i % 8, 1), :] = caps[n, i, pl.ds(t0, 1), :]
        for corner, r0 in ((ups[n], s_dev - W), (downs[n], 0)):
            for c in range(3):
                corner[pl.ds(c * W, W)] = out[pl.ds(c * s_dev + r0, W)]
            corner[pl.ds(3 * W, W // 2)] = out[pl.ds(3 * s_dev + r0 // 2, W // 2)]
    for c in copies[edge_copies:]:
        c.wait()


def y_tile(m_ref, k_refs, c, i, s_dev):
    r = i - W
    if 0 <= r < s_dev:
        return m_ref, (c * s_dev + r if c < 3 else 3 * s_dev + r // 2)
    k = i if r < 0 else r - s_dev
    return k_refs[0 if r < 0 else 1], (c * W + k if c < 3 else 3 * W + k // 2)


def along_both(array, by_slab, by_sub):
    slabs, subs = lax.axis_size("slab"), lax.axis_size("sub")
    pairs = []
    for k in range(slabs):
        for u in range(subs):
            to_k, to_u = k + by_slab, (1 - u if by_sub is None else u + by_sub)
            if 0 <= to_k < slabs and 0 <= to_u < subs:
                pairs.append((k * subs + u, to_k * subs + to_u))
    return lax.ppermute(array, ("slab", "sub"), pairs)


def halo_exchange(electric, magnetic, conduct, temp_old, capacity, offsets, targets):
    s_dev, y_dev, lanes = conduct.shape
    ts, ty, _ = temp_old.shape
    two = lax.axis_size("sub") == 2
    edges = ("either",) if two else ("high", "low")
    count = len(edges)
    up, dn = plane_list(s_dev)
    tiles = 3 * s_dev + s_dev // 2 + 2 * ts // 8
    corner = jax.ShapeDtypeStruct((3 * W + W // 2, 8, lanes), F32)
    ids, up, dn, *messages = pl.pallas_call(
        functools.partial(pack_kernel, edges),
        in_specs=[pl.BlockSpec(memory_space=pltpu.HBM)] * 5
        + [pl.BlockSpec(memory_space=pltpu.VMEM)] * 2,
        out_shape=[
            jax.ShapeDtypeStruct((s_dev * y_dev // lanes, lanes), jnp.int32),
            jax.ShapeDtypeStruct((len(up) + 1, y_dev, lanes), F32),
            jax.ShapeDtypeStruct((len(dn) + 1, y_dev, lanes), F32),
        ]
        + [jax.ShapeDtypeStruct((tiles, 8, lanes), F32)] * count
        + [corner] * (2 * count),
        scratch_shapes=[
            pltpu.VMEM((count, 3, s_dev, 8, lanes), F32),
            pltpu.VMEM((count, 3, s_dev, 8, lanes), F32),
            pltpu.VMEM((count, s_dev, 8, lanes), F32),
            pltpu.VMEM((count, ts, 8, lanes), F32),
            pltpu.VMEM((count, ts, 8, lanes), F32),
            pltpu.SemaphoreType.DMA((5 * count + 18,)),
        ],
        compiler_params=pltpu.CompilerParams(vmem_limit_bytes=PACK_LIMIT),
        name="pack",
    )(
        electric, magnetic, conduct, temp_old, capacity,
        offsets.reshape(s_dev, 1, y_dev), targets.reshape(s_dev, 1, y_dev),
    )
    sides, ups, downs = messages[:count], messages[count : 2 * count], messages[2 * count :]
    lo, hi = passed_along(up, "slab", 1), passed_along(dn, "slab", -1)
    if two:
        m = swapped(sides[0], "sub")
        k = (along_both(ups[0], 1, None), along_both(downs[0], -1, None))
        return ids, (lo, hi, m, m) + k + k
    m_lo, m_hi = passed_along(sides[0], "sub", 1), passed_along(sides[1], "sub", -1)
    k_lo = (along_both(ups[0], 1, 1), along_both(downs[0], -1, 1))
    k_hi = (along_both(ups[1], 1, -1), along_both(downs[1], -1, -1))
    return ids, (lo, hi, m_lo, m_hi) + k_lo + k_hi


def inside_flags(axis, count):
    index = lax.axis_index(axis)
    return (index > 0), (index < count - 1)


def column_shift(group, lanes):
    first = jnp.where(lax.axis_index("comp") == 0, lanes - W, 0)
    return lax.rem(group * W - first + 2 * lanes, lanes)


def gather_columns(sources, which_rows, height, lanes, lane):
    accs = [jnp.zeros((height, lanes), F32), jnp.zeros((height, lanes), F32)]
    for c in range(4):
        for j in range(8):
            group = c * 8 + j
            shift = column_shift(group, lanes)
            here = jnp.concatenate([lane == group] * (height // 8), 0)
            for which in range(2):
                if c == 3 and which != which_rows(j) % 2:
                    continue
                value = sources(6 if c == 3 else c + 3 * which, j)
                if value is not None:
                    accs[which] = jnp.where(here, pltpu.roll(value, shift, 1), accs[which])
    return accs


def columns_kernel(e_ref, h_ref, c_ref, t_ref, cap_ref, out_ref, turn):
    s_dev, y_dev, lanes = c_ref.shape
    lane = lax.broadcasted_iota(jnp.int32, (8, lanes), 1) // W
    turn[...] = jnp.zeros_like(turn)
    for b in range(s_dev // 8):

        def source(f, j, b=b):
            r = b * 8 + j
            return e_ref[f, r] if f < 3 else h_ref[f - 3, r] if f < 6 else c_ref[r]

        accs = gather_columns(source, lambda j: j, y_dev, lanes, lane)
        for which in range(2):
            turn[pl.ds(W, y_dev), :] = accs[which]
            out_ref[2 * b + which] = turn[...].T
    base = s_dev // 4
    rows = t_ref.shape[0] * t_ref.shape[1] // lanes
    per = lanes // t_ref.shape[1]
    for n in range(rows):
        out_ref[base + n] = t_ref[pl.ds(n * per, per)].reshape(lanes, lanes)
        out_ref[base + rows + n] = cap_ref[pl.ds(n * per, per)].reshape(lanes, lanes)


def rims_kernel(
    n_sub, s_dev, lo_ref, hi_ref, ml_ref, mh_ref, kl0_ref, kl1_ref, kh0_ref, kh1_ref, out_ref, turn
):
    y_dev, lanes = lo_ref.shape[1], lo_ref.shape[2]
    y_ext = y_dev + 2 * W
    up_index, dn_index = indices_of(s_dev)
    has_lo, has_hi = inside_flags("sub", n_sub)
    lane = lax.broadcasted_iota(jnp.int32, (8, lanes), 1) // W

    def beside(rows):
        low = jnp.zeros((8, lanes), F32)
        high = jnp.zeros((8, lanes), F32)
        for c in range(4):
            for j in range(8):
                group = c * 8 + j
                shift = column_shift(group, lanes)
                a, tile = y_tile(ml_ref, (kl0_ref, kl1_ref), c, rows[j], s_dev)
                b, _ = y_tile(mh_ref, (kh0_ref, kh1_ref), c, rows[j], s_dev)
                low = jnp.where(lane == group, pltpu.roll(a[tile], shift, 1), low)
                high = jnp.where(lane == group, pltpu.roll(b[tile], shift, 1), high)
        return jnp.where(has_lo, low, 0.0), jnp.where(has_hi, high, 0.0)

    turn[...] = jnp.zeros_like(turn)
    for b in range(s_dev // 8):
        low, high = beside([W + b * 8 + j for j in range(8)])
        turn[pl.ds(16 * b, 8), :] = low
        turn[pl.ds(16 * b + 8, 8), :] = high
    out_ref[0] = turn[...].T

    rows = [k if k < W else s_dev + k for k in range(2 * W)]

    def source(f, j):
        found = row_source(f, rows[j], s_dev, None, lo_ref, hi_ref, up_index, dn_index)
        return None if found is None else found[0][found[1]]

    accs = gather_columns(source, lambda j: j, y_dev, lanes, lane)
    low, high = beside(rows)
    turn[...] = jnp.zeros_like(turn)
    for which in range(2):
        turn[pl.ds(which * y_ext, W), :] = low[which * W : which * W + W]
        turn[pl.ds(which * y_ext + W, y_dev), :] = accs[which]
        turn[pl.ds(which * y_ext + W + y_dev, W), :] = high[which * W : which * W + W]
    out_ref[1] = turn[...].T


def own_columns(electric, magnetic, conduct, temp_old, capacity):
    s_dev, _, lanes = conduct.shape
    count = s_dev // 4 + 2 * (temp_old.shape[0] * temp_old.shape[1] // lanes)
    return pl.pallas_call(
        columns_kernel,
        out_shape=jax.ShapeDtypeStruct((count, lanes, lanes), F32),
        scratch_shapes=[pltpu.VMEM((lanes, lanes), F32)],
        compiler_params=pltpu.CompilerParams(vmem_limit_bytes=SMALL_LIMIT),
        cost_estimate=pl.CostEstimate(flops=10**7, bytes_accessed=8 * 10**6, transcendentals=0),
        name="columns",
    )(electric, magnetic, conduct, temp_old, capacity)


def rim_columns(s_dev, *halos):
    lanes = halos[0].shape[2]
    return pl.pallas_call(
        functools.partial(rims_kernel, lax.axis_size("sub"), s_dev),
        out_shape=jax.ShapeDtypeStruct((2, lanes, lanes), F32),
        scratch_shapes=[pltpu.VMEM((lanes, lanes), F32)],
        compiler_params=pltpu.CompilerParams(vmem_limit_bytes=SMALL_LIMIT),
        name="rims",
    )(*halos)


TOP = 8


def coefficients(conduct, inside):
    damping = 0.5 * time_step * conduct
    inverse = inside / (1.0 + damping)
    return (1.0 - damping) * inverse, (time_step * time_step) * inverse


def scaled(values, scale):
    return values if scale == 1.0 else values * scale


def split_two(values):
    high = values.astype(BF16)
    low = (values - high.astype(F32)).astype(BF16)
    return jnp.concatenate([high, low], 1)


def main_kernel(
    n_slab, n_sub,
    e_ref, h_ref, c_ref, t_ref, ids_ref, lo_ref, hi_ref, ml_ref, mh_ref,
    kl0_ref, kl1_ref, kh0_ref, kh1_ref, own_ref, other_ref, own_rim, other_rim,
    e_out, h_out, here_out, up_out, dn_out, far_up_out, far_dn_out,
    e_done, h_done, out_sem, es, hs, ce, ch, heat, sde, sdh, sce, sch, bt, bp,
):
    s_dev, y_dev, lanes = c_ref.shape
    s_ext, y_ext = s_dev + 2 * W, y_dev + 2 * W
    up_index, dn_index = indices_of(s_dev)
    own = (e_ref, h_ref, c_ref)
    slab_lo, slab_hi = inside_flags("slab", n_slab)
    sub_lo, sub_hi = inside_flags("sub", n_sub)
    comp = lax.axis_index("comp")

    def place(ref, at, f, i, half, c, scale=1.0):
        source = row_source(f, i, s_dev, own, lo_ref, hi_ref, up_index, dn_index)
        if source is None:
            ref[at + (pl.ds(TOP + W, y_dev), slice(None))] = jnp.zeros((y_dev, lanes), F32)
        else:
            s, sat = source
            ref[at + (pl.ds(TOP + W, y_dev), slice(None))] = scaled(s[sat], scale)
        low, tile = y_tile(ml_ref, (kl0_ref, kl1_ref), c, i, s_dev)
        high, _ = y_tile(mh_ref, (kh0_ref, kh1_ref), c, i, s_dev)
        low = low[tile, pl.ds(half * W, W), :]
        high = high[tile, pl.ds(half * W, W), :]
        ref[at + (pl.ds(TOP, W), slice(None))] = scaled(jnp.where(sub_lo, low, 0.0), scale)
        ref[at + (pl.ds(TOP + W + y_dev, W), slice(None))] = scaled(jnp.where(sub_hi, high, 0.0), scale)
        ref[at + (pl.ds(0, TOP), slice(None))] = jnp.zeros((TOP, lanes), F32)
        ref[at + (pl.ds(TOP + y_ext, 8), slice(None))] = jnp.zeros((8, lanes), F32)

    place_y = lax.broadcasted_iota(jnp.int32, (y_ext, lanes), 0)
    in_y = ((place_y >= W) | sub_lo) & ((place_y < W + y_dev) | sub_hi)
    in_y = jnp.where(in_y, 1.0, 0.0)
    lane = lax.broadcasted_iota(jnp.int32, (y_ext, lanes), 1)
    is_last = lane == lanes - 1
    is_first = lane == 0

    def slab_inside(i):
        good = ((i >= W) | slab_lo) & ((i < W + s_dev) | slab_hi)
        return jnp.where(good, 1.0, 0.0)

    for i in range(s_ext):
        for c in range(3):
            place(es, (c, i), c, i, 0, c)
            place(hs, (c, i), c + 3, i, 1, c, 1.0 / time_step)
        place(ce, (i,), 6, i, i % 2, 3)

    def coefs(i, carry):
        keep, gain = coefficients(ce[i, pl.ds(TOP, y_ext), :], in_y * slab_inside(i))
        ce[i, pl.ds(TOP, y_ext), :] = keep
        ch[i] = gain
        return carry

    lax.fori_loop(0, s_ext, coefs, 0)

    first = comp == 0
    blocks = s_ext // 8
    lane8 = lax.broadcasted_iota(jnp.int32, (8, lanes), 1)
    in_y8 = ((lane8 >= W) | sub_lo) & ((lane8 < W + y_dev) | sub_hi)
    in_y8 = jnp.where(in_y8, 1.0, 0.0)
    lane_turn = lax.broadcasted_iota(jnp.int32, (lanes, lanes), 1)
    for b in range(s_dev // 8 + 1):
        for which in range(2):
            halves = []
            for cols, rim in ((own_ref, own_rim), (other_ref, other_rim)):
                if b < s_dev // 8:
                    at = 16 * b + W * which
                    low = pltpu.roll(rim[0], (lanes - at) % lanes, 1)
                    high = pltpu.roll(rim[0], (W + y_dev - at - 8) % lanes, 1)
                    value = jnp.where(lane_turn < W, low, cols[2 * b + which])
                    value = jnp.where(lane_turn >= W + y_dev, high, value)
                else:
                    value = pltpu.roll(rim[1], (lanes - which * y_ext) % lanes, 1)
                halves.append(value)
            low = jnp.where(first, halves[0], halves[1])
            high = jnp.where(first, halves[1], halves[0])
            for c in range(4):
                for j in range(8):
                    if c == 3 and which != j % 2:
                        continue
                    i = W + 8 * b + j
                    if b == s_dev // 8:
                        i = j if j < W else s_dev + j
                    at = (c * 8 + j) * W
                    scale = 1.0 / time_step if which and c < 3 else 1.0
                    target = (sdh if which else sde).at[c, i] if c < 3 else sce.at[i]
                    target[pl.ds(0, W), :] = scaled(low[at : at + W], scale)
                    target[pl.ds(W, W), :] = scaled(high[at : at + W], scale)

    def side_coefs(i, carry):
        sce[i], sch[i] = coefficients(sce[i], in_y8 * slab_inside(i))
        return carry

    lax.fori_loop(0, s_ext, side_coefs, 0)

    e_on = jnp.where(comp == 0, 1.0, 0.0)
    h_on = jnp.where(comp == 0, 0.0, 1.0)

    def up_y(v):
        return pltpu.roll(v, lanes - 1, 1)

    def down_y(v):
        return pltpu.roll(v, 1, 1)

    def up_x(v):
        return pltpu.roll(v, 7, 0)

    def down_x(v):
        return pltpu.roll(v, 1, 0)

    bt[...] = jnp.zeros_like(bt)

    def side_h(step, i):
        e0, e1, e2 = sde[0, i], sde[1, i], sde[2, i]
        at = i * 16 + 2 * step
        bt[pl.ds(at, 1), :] = e0[W : W + 1] * e_on
        bt[pl.ds(at + 1, 1), :] = e1[W : W + 1] * e_on
        inside = in_y8 if i >= W else in_y8 * slab_inside(i)
        h0 = (sdh[0, i] - ((up_y(e2) - e2) - (up_x(e1) - e1))) * inside
        h1 = (sdh[1, i] - ((up_x(e0) - e0) - (sde[2, i + 1] - e2))) * inside
        h2 = (sdh[2, i] - ((sde[1, i + 1] - e1) - (up_y(e0) - e0))) * inside
        sdh[0, i], sdh[1, i], sdh[2, i] = h0, h1, h2
        bt[pl.ds(at + 8, 1), :] = h1[W - 1 : W] * h_on
        bt[pl.ds(at + 9, 1), :] = h0[W - 1 : W] * h_on

    def side_e(i):
        h0, h1, h2 = sdh[0, i], sdh[1, i], sdh[2, i]
        keep, gain = sce[i], sch[i]
        sde[0, i] = keep * sde[0, i] + gain * ((h2 - down_y(h2)) - (h1 - down_x(h1)))
        sde[1, i] = keep * sde[1, i] + gain * ((h0 - down_x(h0)) - (h2 - sdh[2, i - 1]))
        sde[2, i] = keep * sde[2, i] + gain * ((h1 - sdh[1, i - 1]) - (h0 - down_y(h0)))

    def side_step(step, carry):
        for i in range(s_ext - 1):
            side_h(step, i)
        for i in range(1, s_ext - 1):
            side_e(i)
        return carry

    lax.fori_loop(0, STEPS, side_step, 0)

    for b in range(blocks):
        bp[b] = bt[pl.ds(b * lanes, lanes), :].T[:y_ext]

    centre = pl.ds(TOP, y_ext)
    above = pl.ds(TOP + 1, y_ext)
    below = pl.ds(TOP - 1, y_ext)

    def border(i, q):
        shift = lax.rem(2 * lanes - 1 - (i % 8) * 16 - q, lanes)
        return pltpu.roll(bp[i // 8], shift, 1)

    def put_h(c, i, curl):
        value = hs[c, i, centre, :] - curl
        if i < W:
            value = value * slab_inside(i)
        hs[c, i, pl.ds(TOP, 8), :] = value[:8] * in_y[:8]
        hs[c, i, pl.ds(TOP + 8, y_ext - 8), :] = value[8:]

    def main_h(step, i, low_half):
        e0, e1, e2 = es[0, i, centre, :], es[1, i, centre, :], es[2, i, centre, :]
        if low_half:
            beyond, beyond1 = border(i, 2 * step), border(i, 2 * step + 1)
        else:
            beyond, beyond1 = 0.0, 0.0
        e0x = jnp.where(is_last, beyond, pltpu.roll(e0, lanes - 1, 1))
        e1x = jnp.where(is_last, beyond1, pltpu.roll(e1, lanes - 1, 1))
        put_h(0, i, (es[2, i, above, :] - e2) - (e1x - e1))
        put_h(1, i, (e0x - e0) - (es[2, i + 1, centre, :] - e2))
        put_h(2, i, (es[1, i + 1, centre, :] - e1) - (es[0, i, above, :] - e0))

    def main_e(step, i, low_half):
        h0, h1, h2 = hs[0, i, centre, :], hs[1, i, centre, :], hs[2, i, centre, :]
        if low_half:
            beyond, beyond1 = 0.0, 0.0
        else:
            beyond, beyond1 = border(i, 8 + 2 * step), border(i, 8 + 2 * step - 1)
        h0x = jnp.where(is_first, beyond, pltpu.roll(h0, 1, 1))
        h1x = jnp.where(is_first, beyond1, pltpu.roll(h1, 1, 1))
        keep, gain = ce[i, centre, :], ch[i]
        e0, e1, e2 = es[0, i, centre, :], es[1, i, centre, :], es[2, i, centre, :]
        n0 = keep * e0 + gain * ((h2 - hs[2, i, below, :]) - (h1 - h1x))
        n1 = keep * e1 + gain * ((h0 - h0x) - (h2 - hs[2, i - 1, centre, :]))
        n2 = keep * e2 + gain * ((h1 - hs[1, i - 1, centre, :]) - (h0 - hs[0, i, below, :]))
        es[0, i, centre, :] = n0
        es[1, i, centre, :] = n1
        es[2, i, centre, :] = n2
        if W <= i < W + s_dev:
            s0, s1, s2 = e0 + n0, e1 + n1, e2 + n2
            heat[i - W] = heat[i - W] + (s0 * s0 + s1 * s1 + s2 * s2)

    heat[...] = jnp.zeros_like(heat)

    for low_half in (True, False):

        @pl.when((comp == 0) == low_half)
        def _(low_half=low_half):
            for step in range(STEPS):
                for i in range(step, s_ext - 1 - step):
                    main_h(step, i, low_half)
                for i in range(step + 1, s_ext - 1 - step):
                    main_e(step, i, low_half)

    ys = pl.ds(TOP + W, y_dev)
    copies = []
    for c in range(3):
        e_done[c] = es[c, pl.ds(W, s_dev), ys, :]
        copies.append(pltpu.make_async_copy(e_done.at[c], e_out.at[c], out_sem.at[2 * c]))
        copies[-1].start()
        h_done[c] = hs[c, pl.ds(W, s_dev), ys, :] * time_step
        copies.append(pltpu.make_async_copy(h_done.at[c], h_out.at[c], out_sem.at[2 * c + 1]))
        copies[-1].start()

    loss = heat[:, pl.ds(W, y_dev), :] * c_ref[...] * (0.25 * time_step * heating)
    parts = split_two(loss.reshape(s_dev * y_dev, lanes))
    thermal = t_ref.shape[0] * t_ref.shape[1]
    ids = ids_ref[...]
    for n in range(3):
        kinds = lax.broadcasted_iota(jnp.int32, (thermal, lanes), 0) + n * thermal
        chosen = [jnp.where(kinds == ids[a : a + 1], 1.0, 0.0).astype(BF16) for a in range(ids.shape[0])]
        chosen = jnp.concatenate(chosen, 1)
        sums = jnp.dot(chosen, parts, preferred_element_type=F32)
        sums = (sums[:, :lanes] + sums[:, lanes:]).reshape(t_ref.shape)
        if n == 0:
            dn_out[pl.ds(0, t_ref.shape[0])] = sums
            far_dn_out[...] = sums[:R]
        elif n == 1:
            here_out[...] = sums
        else:
            up_out[pl.ds(R, t_ref.shape[0])] = sums
            far_up_out[...] = sums[-R:]

    ts, ty = t_ref.shape[0], t_ref.shape[1]
    per = lanes // ty
    row_t = lax.broadcasted_iota(jnp.int32, (ty, lanes), 0)
    lane_t = lax.broadcasted_iota(jnp.int32, (ty, lanes), 1)
    lo_plane, hi_plane = len(up_index), len(dn_index)
    for i in range(ts):
        x = t_ref[i]
        before = t_ref[i - 1] if i > 0 else lo_ref[lo_plane, pl.ds(0, ty), :]
        after = t_ref[i + 1] if i < ts - 1 else hi_ref[hi_plane, pl.ds(0, ty), :]
        tile = 3 * s_dev + s_dev // 2 + i // 8
        edge_lo = jnp.where(sub_lo, ml_ref[tile, pl.ds(i % 8, 1), :], 0.0)
        edge_hi = jnp.where(sub_hi, mh_ref[tile, pl.ds(i % 8, 1), :], 0.0)
        left_y = jnp.where(row_t == 0, edge_lo, pltpu.roll(x, 1, 0))
        right_y = jnp.where(row_t == ty - 1, edge_hi, pltpu.roll(x, ty - 1, 0))
        beyond = other_ref[s_dev // 4 + i // per, pl.ds((i % per) * ty, ty), :]
        from_low = pltpu.roll(beyond, 1, 1) * h_on
        from_high = pltpu.roll(beyond, lanes - 1, 1) * e_on
        left_x = jnp.where(lane_t == 0, from_low, pltpu.roll(x, 1, 1))
        right_x = jnp.where(lane_t == lanes - 1, from_high, pltpu.roll(x, lanes - 1, 1))
        beside = before + after + left_y + right_y + left_x + right_x
        value = here_out[i] - conduction * (6.0 * x - beside)
        here_out[i] = value
        if i < R:
            dn_out[ts + i] = value
        if i >= ts - R:
            up_out[i - ts + R] = value
    for copy in copies:
        copy.wait()


def main_call(electric, magnetic, conduct, temp_old, ids, *halos):
    s_dev, y_dev, lanes = conduct.shape
    s_ext, y_ext = s_dev + 2 * W, y_dev + 2 * W
    tall = TOP + y_ext + 8
    ts, ty, _ = temp_old.shape
    return pl.pallas_call(
        functools.partial(main_kernel, lax.axis_size("slab"), lax.axis_size("sub")),
        out_shape=[
            jax.ShapeDtypeStruct(electric.shape, F32),
            jax.ShapeDtypeStruct(magnetic.shape, F32),
            jax.ShapeDtypeStruct(temp_old.shape, F32),
            jax.ShapeDtypeStruct((ts + R, ty, lanes), F32),
            jax.ShapeDtypeStruct((ts + R, ty, lanes), F32),
            jax.ShapeDtypeStruct((R, ty, lanes), F32),
            jax.ShapeDtypeStruct((R, ty, lanes), F32),
        ],
        out_specs=[pl.BlockSpec(memory_space=pl.ANY)] * 2
        + [pl.BlockSpec(memory_space=pltpu.VMEM)] * 5,
        scratch_shapes=[
            pltpu.VMEM(electric.shape, F32),
            pltpu.VMEM(magnetic.shape, F32),
            pltpu.SemaphoreType.DMA((6,)),
            pltpu.VMEM((3, s_ext, tall, lanes), F32),
            pltpu.VMEM((3, s_ext, tall, lanes), F32),
            pltpu.VMEM((s_ext, tall, lanes), F32),
            pltpu.VMEM((s_ext, y_ext, lanes), F32),
            pltpu.VMEM((s_dev, y_ext, lanes), F32),
            pltpu.VMEM((3, s_ext, 8, lanes), F32),
            pltpu.VMEM((3, s_ext, 8, lanes), F32),
            pltpu.VMEM((s_ext, 8, lanes), F32),
            pltpu.VMEM((s_ext, 8, lanes), F32),
            pltpu.VMEM((s_ext * 16, lanes), F32),
            pltpu.VMEM((s_ext // 8, y_ext, lanes), F32),
        ],
        compiler_params=pltpu.CompilerParams(vmem_limit_bytes=VMEM_LIMIT),
        name="leapfrog",
    )(electric, magnetic, conduct, temp_old, ids, *halos)


TTOP = 8


def thermal_kernel(
    n_slab, n_sub, z_ref, zo_ref, t_ref, cap_ref, lo_ref, hi_ref, ml_ref, mh_ref, other_ref,
    out_ref, send_ref, d0, d1, r0, cs,
):
    ts, ty, lanes = t_ref.shape
    center, spread, rhos = chebyshev_constants(SWEEPS)
    slab_lo, slab_hi = inside_flags("slab", n_slab)
    sub_lo, sub_hi = inside_flags("sub", n_sub)
    comp = lax.axis_index("comp")
    y_ext = 24
    shift = 4
    chunk = pl.ds(TTOP, y_ext)
    above = pl.ds(TTOP + 1, y_ext)
    below = pl.ds(TTOP - 1, y_ext)
    for ref in (d0, d1, r0, cs):
        ref[...] = jnp.zeros_like(ref)
    per = lanes // ty
    caps = other_ref.shape[0] - ts // per
    for half, z in enumerate((z_ref, zo_ref)):
        r0[half, :, pl.ds(TTOP + shift - R, ty + 2 * R), :] = z[...]
    for i in range(ts):
        cs[0, i + 1, pl.ds(TTOP + shift, ty), :] = cap_ref[i]
        tile = ml_ref.shape[0] - ts // 8 + i // 8
        cs[0, i + 1, pl.ds(TTOP + shift - 1, 1), :] = ml_ref[tile, pl.ds(i % 8, 1), :]
        cs[0, i + 1, pl.ds(TTOP + shift + ty, 1), :] = mh_ref[tile, pl.ds(i % 8, 1), :]
        cs[1, i + 1, pl.ds(TTOP + shift, ty), :] = other_ref[caps + i // per, pl.ds((i % per) * ty, ty), :]
    cs[0, 0, pl.ds(TTOP + shift, ty), :] = lo_ref[lo_ref.shape[0] - 1, pl.ds(ty, ty), :]
    cs[0, ts + 1, pl.ds(TTOP + shift, ty), :] = hi_ref[hi_ref.shape[0] - 1, pl.ds(ty, ty), :]
    d0[...] = r0[...] * (1.0 / center)

    row = lax.broadcasted_iota(jnp.int32, (y_ext, lanes), 0)
    lane = lax.broadcasted_iota(jnp.int32, (y_ext, lanes), 1)
    in_y = ((row >= shift) | sub_lo) & ((row < shift + ty) | sub_hi)
    in_y = jnp.where(in_y, 1.0, 0.0)
    low_half = comp == 0

    def applied(ref, half, i, cap):
        v = ref[half, i, chunk, :]
        w = ref[1 - half, i, chunk, :]
        other_high = low_half if half == 0 else jnp.logical_not(low_half)
        from_low = jnp.where(other_high, 0.0, pltpu.roll(w, 1, 1))
        from_high = jnp.where(other_high, pltpu.roll(w, lanes - 1, 1), 0.0)
        left = jnp.where(lane == 0, from_low, pltpu.roll(v, 1, 1))
        right = jnp.where(lane == lanes - 1, from_high, pltpu.roll(v, lanes - 1, 1))
        beside = ref[half, i - 1, chunk, :] + ref[half, i + 1, chunk, :]
        beside = beside + ref[half, i, above, :] + ref[half, i, below, :] + left + right
        return v, cap * v + conduction * (6.0 * v - beside)

    for i in range(R - 1, ts + R + 1):
        inside = in_y
        if i < R:
            inside = inside * jnp.where(slab_lo, 1.0, 0.0)
        if i >= ts + R:
            inside = inside * jnp.where(slab_hi, 1.0, 0.0)
        for half in range(2):
            if half == 1 and not R <= i < ts + R:
                continue
            v, av = applied(d0, half, i, cs[half, i - 1, chunk, :])
            resid = (r0[half, i, chunk, :] - av) * inside
            r0[half, i, chunk, :] = resid
            d1[half, i, chunk, :] = (rhos[1] * rhos[0]) * v + (2.0 * rhos[1] / spread) * resid
    mine = pl.ds(TTOP + shift, ty)
    for i in range(R, ts + R):
        v, av = applied(d1, 0, i, cs[0, i - 1, chunk, :])
        resid = r0[0, i, chunk, :] - av
        last = (rhos[2] * rhos[1]) * v + (2.0 * rhos[2] / spread) * resid
        r0[0, i, chunk, :] = d0[0, i, chunk, :] + v + last
        value = t_ref[i - R] + r0[0, i, mine, :]
        out_ref[i - R] = value
        send_ref[i - R] = value


def thermal_call(z, z_other, temp_old, capacity, lo, hi, m_lo, m_hi, other):
    ts, ty, lanes = temp_old.shape
    wide = pltpu.VMEM((2, ts + 2 * R, TTOP + 24 + 8, lanes), F32)
    return pl.pallas_call(
        functools.partial(thermal_kernel, lax.axis_size("slab"), lax.axis_size("sub")),
        out_shape=[jax.ShapeDtypeStruct(temp_old.shape, F32)] * 2,
        scratch_shapes=[wide, wide, wide, pltpu.VMEM((2, ts + 2, TTOP + 24 + 8, lanes), F32)],
        compiler_params=pltpu.CompilerParams(vmem_limit_bytes=SMALL_LIMIT),
        name="conduction",
    )(z, z_other, temp_old, capacity, lo, hi, m_lo, m_hi, other)


def lookup_kernel(ids_ref, t_ref, lo_ref, hi_ref, c_ref, out_ref):
    ts, ty, lanes = t_ref.shape
    thermal = ts * ty
    s_dev, y_dev, _ = c_ref.shape
    rows = s_dev * y_dev // lanes
    columns = ids_ref[...].T
    tables = [split_two(r[...].reshape(thermal, lanes)) for r in (lo_ref, t_ref, hi_ref)]
    per = lanes // y_dev
    for a in range(rows):
        column = columns[:, a : a + 1]
        total = jnp.zeros((lanes, 2 * lanes), F32)
        for n in range(3):
            kinds = lax.broadcasted_iota(jnp.int32, (lanes, thermal), 1) + n * thermal
            chosen = jnp.where(kinds == column, 1.0, 0.0).astype(BF16)
            total = total + jnp.dot(chosen, tables[n], preferred_element_type=F32)
        looked = (total[:, :lanes] + total[:, lanes:]).reshape(per, y_dev, lanes)
        at = pl.ds(a * per, per)
        out_ref[at] = c_ref[at] / (1.0 + softening * looked * looked)


def lookup_call(ids, temp_new, lo, hi, conduct):
    return pl.pallas_call(
        lookup_kernel,
        out_shape=jax.ShapeDtypeStruct(conduct.shape, F32),
        compiler_params=pltpu.CompilerParams(vmem_limit_bytes=SMALL_LIMIT),
        name="lookup",
    )(ids, temp_new, lo, hi, conduct)


def combine_kernel(
    n_slab, edges, here_ref, up_ref, dn_ref, low_ref, high_ref, far_low_ref, far_high_ref,
    out_ref, *edge_refs
):
    ts, ty, _ = here_ref.shape
    slab_lo, slab_hi = inside_flags("slab", n_slab)
    low = dn_ref[pl.ds(ts - R, R)] + low_ref[pl.ds(0, R)] + far_low_ref[...]
    high = up_ref[pl.ds(R, R)] + high_ref[pl.ds(ts, R)] + far_high_ref[...]
    out_ref[pl.ds(0, R)] = jnp.where(slab_lo, low, 0.0)
    out_ref[pl.ds(R, ts)] = here_ref[...] + low_ref[pl.ds(R, ts)] + high_ref[pl.ds(0, ts)]
    out_ref[pl.ds(R + ts, R)] = jnp.where(slab_hi, high, 0.0)
    for edge, ref in zip(edges, edge_refs):
        if edge == "either":
            start = jnp.where(lax.axis_index("sub") == 0, ty - R, 0)
        else:
            start = ty - R if edge == "high" else 0
        ref[...] = out_ref[:, pl.ds(start, R), :]


def residual(here, up, dn, far_up, far_dn):
    ts, ty, lanes = here.shape
    from_low, from_high = passed_along(up, "slab", 1), passed_along(dn, "slab", -1)
    far_low, far_high = passed_along(far_up, "slab", 2), passed_along(far_dn, "slab", -2)
    two = lax.axis_size("sub") == 2
    edges = ("either",) if two else ("high", "low")
    r0, *messages = pl.pallas_call(
        functools.partial(combine_kernel, lax.axis_size("slab"), edges),
        out_shape=[jax.ShapeDtypeStruct((ts + 2 * R, ty, lanes), F32)]
        + [jax.ShapeDtypeStruct((ts + 2 * R, R, lanes), F32)] * len(edges),
        compiler_params=pltpu.CompilerParams(vmem_limit_bytes=SMALL_LIMIT),
        name="combine",
    )(here, up, dn, from_low, from_high, far_low, far_high)
    if two:
        received = swapped(messages[0], "sub")
        index = lax.axis_index("sub")
        y_lo, y_hi = jnp.where(index == 0, 0.0, received), jnp.where(index == 0, received, 0.0)
    else:
        y_lo = passed_along(messages[0], "sub", 1)
        y_hi = passed_along(messages[1], "sub", -1)
    return jnp.concatenate([y_lo, r0, y_hi], 1)


def on_device(electric, magnetic, conduct, temp_old, capacity, offsets, targets):
    ids, halos = halo_exchange(
        electric, magnetic, conduct, temp_old, capacity, offsets, targets
    )
    lo, hi, m_lo, m_hi = halos[:4]
    fields = (electric, magnetic, conduct, temp_old, capacity)
    *fields, ids = lax.optimization_barrier(fields + (ids,))
    own = own_columns(*fields)
    own, *halos = lax.optimization_barrier((own,) + halos)
    other = swapped(own, "comp")
    own_rim = rim_columns(conduct.shape[0], *halos)
    other_rim = swapped(own_rim, "comp")
    electric, magnetic, *shares = main_call(
        electric, magnetic, conduct, temp_old, ids, *halos, own, other, own_rim, other_rim
    )
    z = residual(*shares)
    z_other = swapped(z, "comp")
    temp_new, temp_sent = thermal_call(z, z_other, temp_old, capacity, lo, hi, m_lo, m_hi, other)
    t_lo = passed_along(temp_sent, "slab", 1)
    t_hi = passed_along(temp_sent, "slab", -1)
    conduct_new = lookup_call(ids, temp_sent, t_lo, t_hi, conduct)
    return (electric, magnetic, temp_new, conduct_new)


def solution(mesh):
    placed = (
        P(None, ("groups", "slab"), "sub", "comp"),
        P(None, ("groups", "slab"), "sub", "comp"),
        P(("groups", "slab"), "sub", "comp"),
        P(("groups", "slab"), "sub", "comp"),
        P(("groups", "slab"), "sub", "comp"),
        P(("groups", "slab"), "sub", "comp"),
        P(("groups", "slab"), "sub", "comp"),
    )
    return jax.shard_map(
        on_device,
        mesh=mesh,
        in_specs=placed,
        out_specs=(
            P(None, ("groups", "slab"), "sub", "comp"),
            P(None, ("groups", "slab"), "sub", "comp"),
            P(("groups", "slab"), "sub", "comp"),
            P(("groups", "slab"), "sub", "comp"),
        ),
        check_vma=False,
    )
```
